512 devices in a mesh: dp: 64 (over x, y, core), fsdp: 8 (over z).
Axes of the slice: x: 4, y: 8, z: 8, core: 2. Of those that a mesh axis runs over, the one named last changes fastest.
Arguments:
- frames: bfloat16 [131072, 1536], P(('dp', 'fsdp')), may hold values from -100 to 100
- destination: int32 [32768], P(('dp', 'fsdp')), may hold values from 0 to 4095, as said below
- utt_lengths: int32 [512, 4], P(('dp', 'fsdp')), may hold values from 1 to 128, 256 in all within a row
- cotangent: bfloat16 [131072, 1536], P(('dp', 'fsdp')), may hold values from -24 to 24
- weight: bfloat16 [1536, 1536], P('fsdp'), may hold values from -0.15625 to 0.15625
- kernel: float32 [31, 1536], replicated, may hold values from -1 to 1
- norm_gain: float32 [1536], replicated, may hold values from 0.1 to 1.9
- norm_shift: float32 [1536], replicated, may hold values from -3 to 3
Outputs:
- grad_input: bfloat16 [131072, 1536], P(('dp', 'fsdp'))
- grad_weight: float32 [1536, 1536], P('fsdp')
- grad_kernel: float32 [31, 1536], replicated
- grad_gain: float32 [1536], replicated
- grad_shift: float32 [1536], replicated
The draws below stay inside these ranges and needn't reach their ends.
Inputs may be any that keep to these rules, and one draw needn't show every extreme that they name: `destination`: within one fsdp index the entries of all devices are each of 0 to 4095 once. The 64 blocks of one device go to exactly 64 owners, 1 block to each.
All inputs are finite; a program needn't handle non-finite values.
Results may differ from the reference program's by a relative error of at most 0.0065.
Values may be sent and summed in bfloat16 or wider, within the bound.
A program may use at most 128 MiB of HBM per device.

```python
import math
import jax
import jax.numpy as jnp
import numpy as np
from jax import lax

D = 1536
C = 1536
TAPS = 31
BLOCK = 4
NB = 64
UTTS = 4
MOST = 128
SPREAD = 64
CAP = 1
DEVS = 512
FRAMES = 131072
N_DP = 64
N_FSDP = 8


def draw_frames(key, part):
    key = jax.random.fold_in(key, 1)
    key_noise, key_cols, key_rows = jax.random.split(key, 3)
    col_scale = jnp.exp(jax.random.uniform(key_cols, (1, C), jnp.float32) * math.log(10.0))
    noise = jnp.clip(jax.random.normal(key_noise, (FRAMES, C), jnp.float32), -6.0, 6.0)
    row_scale = jnp.exp(jax.random.uniform(key_rows, (FRAMES, 1), jnp.float32) * math.log(10.0))
    return (noise * col_scale * row_scale / 6.0).astype(jnp.bfloat16)


def draw_cotangent(key, part):
    key = jax.random.fold_in(key, 2)
    key_noise = jax.random.fold_in(key, 0)
    device_row = (jnp.arange(FRAMES, dtype=jnp.int32) // (NB * BLOCK)).astype(jnp.float32)
    rising = 1.0 + 2.0 * device_row[:, None] / max(DEVS - 1, 1)
    noise = jnp.clip(jax.random.normal(key_noise, (FRAMES, D), jnp.float32), -6.0, 6.0)
    values = noise * rising
    return values.astype(jnp.bfloat16)


def draw_destination(key, part):
    key = jax.random.fold_in(key, 3)

    def one_group(group_key):
        key_in, key_out, key_shift, key_order, key_slot = jax.random.split(group_key, 5)
        perm_in = jax.random.permutation(key_in, N_DP)
        perm_out = jax.random.permutation(key_out, N_DP)
        shifts = jax.random.permutation(key_shift, N_DP)[:SPREAD]
        block_order = jax.vmap(lambda order_key: jax.random.permutation(order_key, NB))(jax.random.split(key_order, N_DP))
        lane_index = block_order // CAP
        owner_index = perm_out[(perm_in[:, None] + shifts[lane_index]) % N_DP]
        slot_perm = jax.vmap(lambda slot_key: jax.random.permutation(slot_key, NB))(jax.random.split(key_slot, N_DP))
        slot_index = slot_perm[owner_index, block_order]
        return owner_index * NB + slot_index
    groups = jax.vmap(one_group)(jax.random.split(key, N_FSDP))
    return groups.transpose(1, 0, 2).reshape(-1).astype(jnp.int32)


def steps_of(own_key, extent, cuts, least, high):
    def one(axis_at, shards_of):
        draws = jax.random.uniform(jax.random.fold_in(jax.random.fold_in(own_key, 6), axis_at), (shards_of,), jnp.float32, least / len(cuts), high / len(cuts))
        return jnp.repeat(jnp.exp(draws), extent[axis_at] // shards_of).reshape((-1,) + (1,) * (len(extent) - axis_at - 1))

    factor_of = one(*cuts[0])
    for cut in cuts[1:]:
        factor_of = factor_of * one(*cut)
    return factor_of


def split_up(amount, total, limit, slope):
    loads = [(1 << 20) // math.isqrt(grade ** slope) + 1 for grade in range(2, amount + 1)]
    spare, holding = total - limit - (amount - 1), [1] * (amount - 1)
    while spare > 0:
        movable = [i for i in range(amount - 1) if holding[i] < limit]
        whole, left = sum([loads[i] for i in movable]), spare
        for i in movable:
            extra = min(limit - holding[i], max(1, left * loads[i] // whole), spare)
            holding[i] = holding[i] + extra
            spare = spare - extra
    return np.array([limit] + holding)


def ragged_sizes(stream_key, count, total, bound, skew):
    if count == 2:
        one = jax.random.randint(stream_key, (), max(1, total - bound), min(bound, total - 1) + 1)
        return jnp.stack([one, total - one])
    tallies = jnp.asarray(split_up(count, total, bound, skew), jnp.int32)
    pairs = (count - 1) // 2
    giver, taker = tallies[1:1 + 2 * pairs:2], tallies[2:2 + 2 * pairs:2]
    margin = jnp.minimum(giver - 1, bound - taker)
    passed = jax.random.randint(jax.random.fold_in(stream_key, 1), (pairs,), 0, 1 << 20) % (margin + 1)
    tallies = tallies.at[1:1 + 2 * pairs:2].set(giver - passed).at[2:2 + 2 * pairs:2].set(taker + passed)
    return tallies[jax.random.permutation(jax.random.fold_in(stream_key, 2), count)]


def centred(own_key, dims, deviation, bound, pieces=(), kind=jnp.bfloat16):
    factor_of = steps_of(own_key, dims, pieces, -0.22, 0.18) if pieces else 1.0
    array = jax.random.normal(own_key, dims, jnp.float32) * deviation * factor_of
    return jnp.minimum(jnp.maximum(array, -bound), bound).astype(kind)


def setup_inputs(seed: int = 0) -> dict:
    splits = jax.random.split(jax.random.key(seed), 9)
    return {
        "frames": draw_frames(jax.random.fold_in(splits[8], 71), 0),
        "destination": draw_destination(jax.random.fold_in(splits[8], 71), 0),
        "utt_lengths": jax.vmap(lambda own: ragged_sizes(own, UTTS, NB * BLOCK, MOST, 2))(jax.random.split(splits[2], DEVS)).reshape((DEVS, UTTS)).astype(jnp.int32),
        "cotangent": draw_cotangent(jax.random.fold_in(splits[8], 71), 0),
        "weight": centred(splits[4], (D, C), C ** -0.5, 0.15625, ((0, 8),)),
        "kernel": centred(splits[5], (TAPS, C), TAPS ** -0.5, 1.0, (), jnp.float32),
        "norm_gain": jnp.clip(1.0 + 0.18 * jax.random.normal(splits[6], (C,), jnp.float32), 0.1, 1.9),
        "norm_shift": centred(splits[7], (C,), 0.5, 3.0, (), jnp.float32),
    }


EPSILON = 1e-05

def segment_ids(lengths, row_count):
    utt_ends = jnp.cumsum(lengths)
    positions = jnp.arange(row_count, dtype=jnp.int32)
    return lax.optimization_barrier(jnp.sum((positions[:, None] >= utt_ends[None, :]).astype(jnp.int32), axis=1))

def module_grads(frames_dev, cot_dev, weight, kernel, norm_gain, norm_shift, lengths_dev):
    row_count = frames_dev.shape[0]
    tap_count = kernel.shape[0]
    half_taps = tap_count // 2
    segment = segment_ids(lengths_dev, row_count)
    segment_pad = jnp.pad(segment, half_taps, constant_values=-1)
    signal = frames_dev.astype(jnp.float32)
    signal_pad = jnp.pad(signal, ((half_taps, half_taps), (0, 0)))
    filtered = jnp.zeros_like(signal)
    for offset in range(tap_count):
        inside = (segment_pad[offset:offset + row_count] == segment).astype(jnp.float32)[:, None]
        filtered = filtered + kernel[offset] * signal_pad[offset:offset + row_count] * inside
    centered = filtered - lax.optimization_barrier(jnp.mean(filtered, axis=1, keepdims=True))
    variance = lax.optimization_barrier(jnp.mean(centered * centered, axis=1, keepdims=True))
    inverse = 1.0 / jnp.sqrt(variance + EPSILON)
    whitened = centered * inverse
    normed = whitened * norm_gain + norm_shift
    logistic = jax.nn.sigmoid(normed)
    activated = (normed * logistic).astype(jnp.bfloat16)
    grad_hidden = jnp.dot(cot_dev, weight, preferred_element_type=jnp.float32)
    grad_normed = grad_hidden * logistic * (1.0 + normed * (1.0 - logistic))
    scaled = grad_normed * norm_gain
    grad_filtered = inverse * (scaled - lax.optimization_barrier(jnp.mean(scaled, axis=1, keepdims=True)) - whitened * lax.optimization_barrier(jnp.mean(scaled * whitened, axis=1, keepdims=True)))
    grad_padded = jnp.pad(grad_filtered, ((half_taps, half_taps), (0, 0)))
    kernel_rows = []
    grad_owned = jnp.zeros_like(signal)
    for offset in range(tap_count):
        inside = (segment_pad[offset:offset + row_count] == segment).astype(jnp.float32)[:, None]
        kernel_rows.append(lax.optimization_barrier(jnp.sum(grad_filtered * signal_pad[offset:offset + row_count] * inside, axis=0)))
        mirror = 2 * half_taps - offset
        mirrored = (segment_pad[mirror:mirror + row_count] == segment).astype(jnp.float32)[:, None]
        grad_owned = grad_owned + kernel[offset] * grad_padded[mirror:mirror + row_count] * mirrored
    partial_value = lax.dot_general(cot_dev, activated, (((0,), (0,)), ((), ())), preferred_element_type=jnp.float32).astype(jnp.bfloat16)
    return (grad_owned.astype(jnp.bfloat16), partial_value, jnp.stack(kernel_rows), lax.optimization_barrier(jnp.sum(grad_normed * whitened, axis=0)), lax.optimization_barrier(jnp.sum(grad_normed, axis=0)))

def reference(frames, destination, utt_lengths, cotangent, weight, kernel, norm_gain, norm_shift):
    device_count = N_DP * N_FSDP
    dev_rows = NB * BLOCK
    blocks = frames.reshape(N_DP, N_FSDP, NB, BLOCK, C).transpose(1, 0, 2, 3, 4).reshape(N_FSDP, N_DP * NB, BLOCK, C)
    targets = destination.reshape(N_DP, N_FSDP, NB).transpose(1, 0, 2).reshape(N_FSDP, N_DP * NB).astype(jnp.int32)

    def place_group(group_blocks, group_targets):
        return jnp.zeros_like(group_blocks).at[group_targets].set(group_blocks)
    owned_rows = jax.vmap(place_group)(blocks, targets)
    owned_rows = owned_rows.reshape(N_FSDP, N_DP, dev_rows, C).transpose(1, 0, 2, 3).reshape(device_count, dev_rows, C)
    cot_rows = cotangent.reshape(device_count, dev_rows, D)

    def scan_step(running, inputs):
        frames_dev, cot_dev, lengths_dev = inputs
        grad_owned, partial_value, kernel_part, gain_part, shift_part = module_grads(frames_dev, cot_dev, weight, kernel, norm_gain, norm_shift, lengths_dev)
        running = (running[0] + partial_value.astype(jnp.float32), running[1] + kernel_part, running[2] + gain_part, running[3] + shift_part)
        return (running, grad_owned)
    initial = (jnp.zeros((D, C), jnp.float32), jnp.zeros((TAPS, C), jnp.float32), jnp.zeros((C,), jnp.float32), jnp.zeros((C,), jnp.float32))
    running, grads_owned = lax.scan(scan_step, initial, (owned_rows, cot_rows, utt_lengths))
    grads_owned = grads_owned.reshape(N_DP, N_FSDP, NB, BLOCK, C).transpose(1, 0, 2, 3, 4).reshape(N_FSDP, N_DP * NB, BLOCK, C)

    def take_group(group_grads, group_targets):
        return group_grads[group_targets]
    returned = jax.vmap(take_group)(grads_owned, targets)
    grad_input = returned.reshape(N_FSDP, N_DP, NB, BLOCK, C).transpose(1, 0, 2, 3, 4).reshape(FRAMES, C)
    norm_scale = 1.0 / math.sqrt(FRAMES)
    return (grad_input, running[0] * norm_scale, running[1] * norm_scale, running[2] * norm_scale, running[3] * norm_scale)
```

```python
import functools
import math

import jax
import jax.numpy as jnp
from jax import lax
from jax.experimental import pallas as pl
from jax.experimental.pallas import tpu as pltpu
from jax.sharding import PartitionSpec as P

EPSILON = 1e-05
MESH = pl.DeviceIdType.MESH
F32 = jnp.float32
BF16 = jnp.bfloat16
BLOCK = 4
TAPS = 31
HALO = 16
KROWS = 40
VMEM_BYTES = 56 * 1024 * 1024


class Sizes:
    def __init__(self, dp_size, fsdp_size, rows, channels, shard):
        self.nd = dp_size
        self.nz = fsdp_size
        self.rows = rows
        self.ch = channels
        self.shard = shard
        self.nb = rows // BLOCK
        self.tiles = channels // 128
        self.groups = self.tiles // 4
        self.slab = 4 * self.tiles
        self.chips = dp_size // 2
        self.half = channels // 2
        self.ltiles = self.half // 128
        self.quarter = self.half // 2
        self.cuts = 4 if self.chips >= 4 * self.ltiles else 2
        self.prow = shard // self.cuts
        self.pieces = self.cuts * self.ltiles
        self.used = rows + 4 * HALO
        self.padded = self.used + 2 * HALO
        self.span = 80 if self.used % 80 == 0 else 48
        self.krow = 8 * (-(-(5 * self.ltiles) // self.chips))
        self.kall = self.krow * self.chips


def one_hot(mask):
    return jnp.where(mask, 1.0, 0.0).astype(BF16)


def dot(a, b):
    return jnp.dot(a, b, preferred_element_type=F32)


def greet(n, dp, z, steps):
    barrier = pltpu.get_barrier_semaphore()

    def along_dp(step, carry):
        pl.semaphore_signal(
            barrier, inc=1, device_id=(lax.rem(dp + step, n.nd), z), device_id_type=MESH
        )
        return carry

    lax.fori_loop(1, n.nd, along_dp, 0)
    for step in steps:
        pl.semaphore_signal(
            barrier, inc=1, device_id=(dp, lax.rem(z + step, n.nz)), device_id_type=MESH
        )
    pl.semaphore_wait(barrier, n.nd - 1 + len(steps))


def remote(src, dst, send, recv, dp, z):
    return pltpu.make_async_remote_copy(
        src_ref=src, dst_ref=dst, send_sem=send, recv_sem=recv, device_id=(dp, z), device_id_type=MESH
    )


def exchange_start(n, dp, z, src, dst, send, recv):
    def step_to(step, carry):
        peer = lax.rem(dp + step, n.nd)
        remote(src.at[peer], dst.at[dp], send.at[peer], recv.at[dp], peer, z).start()
        return carry

    lax.fori_loop(1, n.nd, step_to, 0)


def exchange_arrive(n, dp, z, src, dst, send, recv):
    def step_to(step, carry):
        peer = lax.rem(dp + step, n.nd)
        remote(src.at[peer], dst.at[peer], send.at[peer], recv.at[peer], peer, z).wait_recv()
        return carry

    lax.fori_loop(1, n.nd, step_to, 0)


def exchange_sent(n, dp, z, src, dst, send, recv):
    def step_to(step, carry):
        peer = lax.rem(dp + step, n.nd)
        remote(src.at[peer], dst.at[dp], send.at[peer], recv.at[dp], peer, z).wait_send()
        return carry

    lax.fori_loop(1, n.nd, step_to, 0)


def dispatch_kernel(
    n, code_ref, slots_ref, frames_ref, weight_ref,
    arrived_ref, label_ref, whole_ref,
    outgoing, b_send, b_recv, l_send, l_recv, u_send, u_recv, d_send, d_recv, s_send, s_recv,
):
    dp = lax.axis_index("dp")
    z = lax.axis_index("fsdp")
    core = lax.rem(dp, 2)
    mate = dp + 1 - 2 * core
    far = n.nz // 2
    up = lax.rem(z + 1, n.nz)
    down = lax.rem(z + n.nz - 1, n.nz)
    hrow = n.shard // 2
    steps = sorted({1, n.nz - 1})

    whole_ref[z] = weight_ref[...]
    code = code_ref[...]
    mats = []
    for jj in range(4):
        mats.append(
            jnp.concatenate(
                [frames_ref[:, 128 * (4 * g + jj) : 128 * (4 * g + jj + 1)] for g in range(n.groups)], axis=1
            )
        )
    chunk_rows = min(256, 16 * n.nb)

    def sort_chunk(chunk, carry):
        place = lax.broadcasted_iota(jnp.int32, (chunk_rows, n.rows), 0) + chunk * chunk_rows
        total = dot(one_hot(place == code), mats[0])
        for jj in range(1, 4):
            total = total + dot(one_hot(place == code + 4 * jj), mats[jj])
        for g in range(n.groups):
            part = total[:, 128 * g : 128 * (g + 1)].astype(BF16).reshape(chunk_rows // 16, 16, 128)
            outgoing[pl.ds(chunk * (chunk_rows // 16), chunk_rows // 16), 16 * g : 16 * (g + 1), :] = part
        return carry

    lax.fori_loop(0, 16 * n.nb // chunk_rows, sort_chunk, 0)
    arrived_ref[dp] = outgoing[dp]
    label_ref[dp] = slots_ref[dp]

    greet(n, dp, z, steps)

    def ring(step, block, first, count, to, send, recv):
        rows = pl.ds(pl.multiple_of(core * hrow + first, 16), count)
        return remote(
            whole_ref.at[block, rows], whole_ref.at[block, rows], send.at[step], recv.at[step], dp, to
        )

    def up_hop(step, block):
        last = step == far - 1
        return ring(step, block, 0, hrow // 2 if last else hrow, up, u_send, u_recv)

    def down_hop(step, block):
        last = step == far - 1
        return ring(step, block, hrow // 2 if last else 0, hrow // 2 if last else hrow, down, d_send, d_recv)

    def to_mate(slot, block):
        rows = pl.ds(pl.multiple_of(core * hrow, 16), hrow)
        return remote(
            whole_ref.at[block, rows], whole_ref.at[block, rows], s_send.at[slot], s_recv.at[slot], mate, z
        )

    up_hop(0, z).start()
    down_hop(0, z).start()
    exchange_start(n, dp, z, slots_ref, label_ref, l_send, l_recv)
    exchange_start(n, dp, z, outgoing, arrived_ref, b_send, b_recv)
    for step in range(far):
        below = lax.rem(z + n.nz - step - 1, n.nz)
        above = lax.rem(z + step + 1, n.nz)
        up_hop(step, below).wait_recv()
        if step < far - 1:
            up_hop(step + 1, below).start()
            to_mate(2 * step, below).start()
        down_hop(step, above).wait_recv()
        if step < far - 1:
            down_hop(step + 1, above).start()
            to_mate(2 * step + 1, above).start()
        else:
            to_mate(2 * step, above).start()
    exchange_arrive(n, dp, z, slots_ref, label_ref, l_send, l_recv)
    exchange_arrive(n, dp, z, outgoing, arrived_ref, b_send, b_recv)

    def from_mate(slot, block):
        rows = pl.ds(pl.multiple_of((1 - core) * hrow, 16), hrow)
        return remote(
            whole_ref.at[block, rows], whole_ref.at[block, rows], s_send.at[slot], s_recv.at[slot], mate, z
        )

    for step in range(far):
        below = lax.rem(z + n.nz - step - 1, n.nz)
        above = lax.rem(z + step + 1, n.nz)
        if step < far - 1:
            from_mate(2 * step, below).wait_recv()
            from_mate(2 * step + 1, above).wait_recv()
        else:
            from_mate(2 * step, above).wait_recv()
    for step in range(far):
        below = lax.rem(z + n.nz - step - 1, n.nz)
        above = lax.rem(z + step + 1, n.nz)
        up_hop(step, lax.rem(z + n.nz - step, n.nz)).wait_send()
        down_hop(step, lax.rem(z + step, n.nz)).wait_send()
        if step < far - 1:
            to_mate(2 * step, below).wait_send()
            to_mate(2 * step + 1, above).wait_send()
        else:
            to_mate(2 * step, above).wait_send()
    exchange_sent(n, dp, z, slots_ref, label_ref, l_send, l_recv)
    exchange_sent(n, dp, z, outgoing, arrived_ref, b_send, b_recv)


def dispatch(n, code_row, slots, frames, weight):
    far = n.nz // 2
    dma = pltpu.SemaphoreType.DMA
    return pl.pallas_call(
        functools.partial(dispatch_kernel, n),
        out_shape=(
            jax.ShapeDtypeStruct((n.nb, n.slab, 128), BF16),
            jax.ShapeDtypeStruct((n.nb, 1, 128), F32),
            jax.ShapeDtypeStruct((n.nz, n.shard, n.ch), BF16),
        ),
        in_specs=[pl.BlockSpec(memory_space=pltpu.VMEM)] * 4,
        out_specs=tuple([pl.BlockSpec(memory_space=pltpu.VMEM)] * 3),
        scratch_shapes=[
            pltpu.VMEM((n.nb, n.slab, 128), BF16),
            dma((n.nd,)), dma((n.nd,)), dma((n.nd,)), dma((n.nd,)),
            dma((far,)), dma((far,)), dma((far,)), dma((far,)),
            dma((2 * far,)), dma((2 * far,)),
        ],
        compiler_params=pltpu.CompilerParams(
            collective_id=0, has_side_effects=True, vmem_limit_bytes=VMEM_BYTES
        ),
    )(code_row, slots, frames, weight)


def padded_place(frame, ends):
    place = frame + HALO
    for end in ends:
        place = place + jnp.where(frame >= end, HALO, 0)
    return place


def compute_kernel(
    n, utt_ref, arrived_ref, label_ref, whole_ref, cot_ref, kernel_ref, gain_ref, shift_ref,
    back_ref, act_ref, kgrad_ref,
    xs, filt, hidden, gf, actp, go, labels, k8,
):
    ends = [utt_ref[0, 0]]
    for i in range(1, 3):
        ends.append(ends[-1] + utt_ref[0, i])
    lanes = 16 * n.nb

    lane = lax.broadcasted_iota(jnp.int32, (1, 128), 1)
    chunks = []
    for q in range(n.nb // 8):
        row = jnp.zeros((1, 128), F32)
        for s in range(8):
            row = row + jnp.where(lane // 16 == s, label_ref[8 * q + s], 0.0)
        chunks.append(row)
    slot_row = jnp.concatenate(chunks, axis=1).astype(jnp.int32)
    lane_all = lax.broadcasted_iota(jnp.int32, (1, lanes), 1)
    place_row = padded_place(slot_row * BLOCK + lane_all % 4, ends)

    def spread(src, carry):
        labels[pl.ds(pl.multiple_of(16 * src, 16), 16), :] = jnp.broadcast_to(label_ref[src], (16, 128))
        return carry

    lax.fori_loop(0, n.nb, spread, 0)

    blocks = jnp.concatenate(
        [arrived_ref[:, 16 * g : 16 * (g + 1), :].reshape(lanes, 128) for g in range(n.groups)], axis=1
    )
    row_iota = lax.broadcasted_iota(jnp.int32, (n.padded, lanes), 0)

    def put(jj, carry):
        mine = jnp.where((lane_all // 4) % 4 == jj, place_row, -1)
        owned = dot(one_hot(row_iota == mine), blocks)
        for g in range(n.groups):
            xs[4 * g + jj] = owned[:, 128 * g : 128 * (g + 1)]
        return carry

    lax.fori_loop(0, 4, put, 0)

    frame_row = padded_place(lax.broadcasted_iota(jnp.int32, (1, n.rows), 1), ends)
    pad_mat = one_hot(lax.broadcasted_iota(jnp.int32, (n.padded, n.rows), 0) == frame_row)
    cot_pad = dot(pad_mat, cot_ref[...]).astype(BF16)
    width = 512
    per = width // 128

    def project(i, carry):
        cols = pl.ds(pl.multiple_of(i * width, width), width)
        part = dot(cot_pad, whole_ref[:, :, cols].reshape(n.ch, width))
        for q in range(per):
            hidden[per * i + q] = part[:, 128 * q : 128 * (q + 1)]
        return carry

    lax.fori_loop(0, n.ch // width, project, 0)

    spans = range(n.used // n.span)

    def filter_tile(j, carry):
        taps = kernel_ref[j]
        for b in spans:
            base = 1 + n.span * b
            total = jnp.zeros((n.span, 128), F32)
            for s in range(8):
                window = xs[j, base + s : base + s + n.span + 24, :]
                for m in range(4):
                    k = s + 8 * m
                    if k < TAPS:
                        total = total + taps[k : k + 1] * window[8 * m : 8 * m + n.span]
            filt[j, HALO + n.span * b : HALO + n.span * (b + 1), :] = total
        return carry

    lax.fori_loop(0, n.tiles, filter_tile, 0)

    kgrad_ref[...] = jnp.zeros_like(kgrad_ref)
    actp[...] = jnp.zeros_like(actp)
    gf[:, :HALO, :] = jnp.zeros((n.tiles, HALO, 128), F32)
    gf[:, n.padded - HALO :, :] = jnp.zeros((n.tiles, HALO, 128), F32)

    def norm_span(b, carry):
        rows = pl.ds(pl.multiple_of(HALO + n.span * b, 16), n.span)
        total = filt[0, rows, :]
        for j in range(1, n.tiles):
            total = total + filt[j, rows, :]
        mean = jnp.sum(total, axis=1, keepdims=True) * (1.0 / n.ch)
        square = jnp.zeros((n.span, 128), F32)
        for j in range(n.tiles):
            centred = filt[j, rows, :] - mean
            square = square + centred * centred
        variance = jnp.sum(square, axis=1, keepdims=True) * (1.0 / n.ch)
        inverse = 1.0 / jnp.sqrt(variance + EPSILON)
        first = jnp.zeros((n.span, 128), F32)
        second = jnp.zeros((n.span, 128), F32)
        for j in range(n.tiles):
            gain = gain_ref[j]
            whitened = (filt[j, rows, :] - mean) * inverse
            normed = whitened * gain + shift_ref[j]
            logistic = 1.0 / (1.0 + jnp.exp(-normed))
            actp[rows, 128 * j : 128 * (j + 1)] = (normed * logistic).astype(BF16)
            grad_normed = hidden[j, rows, :] * logistic * (1.0 + normed * (1.0 - logistic))
            scaled = grad_normed * gain
            filt[j, rows, :] = whitened
            hidden[j, rows, :] = scaled
            first = first + scaled
            second = second + scaled * whitened
            half, at = j // n.ltiles, (j % n.ltiles) * KROWS
            kgrad_ref[half, at + TAPS : at + TAPS + 1, :] += jnp.sum(grad_normed * whitened, axis=0, keepdims=True)
            kgrad_ref[half, at + TAPS + 1 : at + TAPS + 2, :] += jnp.sum(grad_normed, axis=0, keepdims=True)
        mean1 = jnp.sum(first, axis=1, keepdims=True) * (1.0 / n.ch)
        mean2 = jnp.sum(second, axis=1, keepdims=True) * (1.0 / n.ch)
        for j in range(n.tiles):
            gf[j, rows, :] = inverse * (hidden[j, rows, :] - mean1 - filt[j, rows, :] * mean2)
        return carry

    lax.fori_loop(0, n.used // n.span, norm_span, 0)

    frame_col = padded_place(lax.broadcasted_iota(jnp.int32, (n.rows, 1), 0), ends)
    take = one_hot(lax.broadcasted_iota(jnp.int32, (n.rows, n.padded), 1) == frame_col)
    act_ref[...] = dot(take, actp[...]).astype(BF16)

    go[...] = jnp.zeros_like(go)

    def back_tile(j, carry):
        taps = kernel_ref[j]
        for b in spans:
            base = 1 + n.span * b
            here = slice(HALO + n.span * b, HALO + n.span * (b + 1))
            signal = xs[j, here, :]
            total = jnp.zeros((n.span, 128), F32)
            for s in range(8):
                window = gf[j, base + s : base + s + n.span + 24, :]
                for m in range(4):
                    k = TAPS - 1 - s - 8 * m
                    if k >= 0:
                        shifted = window[8 * m : 8 * m + n.span]
                        total = total + taps[k : k + 1] * shifted
                        product = jnp.sum((shifted * signal).reshape(n.span // 8, 8, 128), axis=0)
                        if b == 0:
                            k8[k] = product
                        else:
                            k8[k] += product
            go[j, here, :] = total.astype(BF16)
        at = pl.multiple_of(lax.rem(j, n.ltiles) * KROWS, 8)
        kgrad_ref[j // n.ltiles, pl.ds(at, TAPS), :] = jnp.sum(k8[...], axis=1)
        return carry

    lax.fori_loop(0, n.tiles, back_tile, 0)

    chunk_rows = min(256, lanes)

    def gather_chunk(chunk, carry):
        at = pl.ds(pl.multiple_of(chunk * chunk_rows, chunk_rows), chunk_rows)
        slot = labels[at, :][:, :1].astype(jnp.int32)
        sub = lax.broadcasted_iota(jnp.int32, (chunk_rows, 1), 0)
        place = padded_place(slot * BLOCK + sub % 4, ends)
        cols = lax.broadcasted_iota(jnp.int32, (chunk_rows, n.padded), 1)
        total = None
        for jj in range(4):
            mine = jnp.where((sub // 4) % 4 == jj, place, -1)
            rhs = jnp.concatenate([go[4 * g + jj] for g in range(n.groups)], axis=1)
            part = dot(one_hot(cols == mine), rhs)
            total = part if total is None else total + part
        for g in range(n.groups):
            part = total[:, 128 * g : 128 * (g + 1)].astype(BF16).reshape(chunk_rows // 16, 16, 128)
            back_ref[pl.ds(chunk * (chunk_rows // 16), chunk_rows // 16), 16 * g : 16 * (g + 1), :] = part
        return carry

    lax.fori_loop(0, lanes // chunk_rows, gather_chunk, 0)


def compute(n, lengths, arrived, labels, whole, cot, taps, gain, shift):
    vmem = pl.BlockSpec(memory_space=pltpu.VMEM)
    return pl.pallas_call(
        functools.partial(compute_kernel, n),
        out_shape=(
            jax.ShapeDtypeStruct((n.nb, n.slab, 128), BF16),
            jax.ShapeDtypeStruct((n.rows, n.ch), BF16),
            jax.ShapeDtypeStruct((2, n.kall, 128), F32),
        ),
        in_specs=[pl.BlockSpec(memory_space=pltpu.SMEM)] + [vmem] * 7,
        out_specs=(vmem,) * 3,
        scratch_shapes=[
            pltpu.VMEM((n.tiles, n.padded, 128), F32),
            pltpu.VMEM((n.tiles, n.padded, 128), F32),
            pltpu.VMEM((n.tiles, n.padded, 128), F32),
            pltpu.VMEM((n.tiles, n.padded, 128), F32),
            pltpu.VMEM((n.padded, n.ch), BF16),
            pltpu.VMEM((n.tiles, n.padded, 128), BF16),
            pltpu.VMEM((16 * n.nb, 128), F32),
            pltpu.VMEM((TAPS, 8, 128), F32),
        ],
        compiler_params=pltpu.CompilerParams(vmem_limit_bytes=VMEM_BYTES),
    )(lengths, arrived, labels, whole, cot, taps, gain, shift)


def finish_kernel(
    n, scale, code_ref, back_ref, act_ref, cot_ref, kgrad_ref,
    frames_out, weight_out, ksum_out,
    home, mate_act, mate_cot, mate_k, part, up_out, up_in, down_out, down_in,
    own_f, own_b, piece_in, all_b, mate_b, k_in, k_z, k_all, k_mate,
    h_send, h_recv, m_send, m_recv, u_send, u_recv, d_send, d_recv,
    p_send, p_recv, a_send, a_recv, ka_send, ka_recv, kz_send, kz_recv, kc_send, kc_recv,
):
    dp = lax.axis_index("dp")
    z = lax.axis_index("fsdp")
    core = lax.rem(dp, 2)
    mate = dp + 1 - 2 * core
    chip = dp // 2
    far = n.nz // 2
    up = lax.rem(z + 1, n.nz)
    down = lax.rem(z + n.nz - 1, n.nz)
    other = 1 - core
    mine = pl.ds(pl.multiple_of(core * n.half, 128), n.half)
    theirs = pl.ds(pl.multiple_of(other * n.half, 128), n.half)

    greet(n, dp, z, list(range(1, n.nz)))

    to_mate = [
        remote(kgrad_ref.at[other], mate_k, m_send.at[0], m_recv.at[0], mate, z),
        remote(cot_ref, mate_cot, m_send.at[1], m_recv.at[1], mate, z),
        remote(act_ref.at[:, theirs], mate_act, m_send.at[2], m_recv.at[2], mate, z),
    ]
    for copy in to_mate:
        copy.start()
    home[dp] = back_ref[dp]
    exchange_start(n, dp, z, back_ref, home, h_send, h_recv)

    def chips(body):
        lax.fori_loop(1, n.chips, lambda step, carry: (body(lax.rem(chip + step, n.chips)), carry)[1], 0)

    to_mate[0].wait_recv()
    mate_k[...] += kgrad_ref[core]

    def k_rows(at):
        return pl.ds(pl.multiple_of(at * n.krow, 8), n.krow)

    def k_scatter(at, slot):
        return remote(mate_k.at[k_rows(at)], k_in.at[slot], ka_send.at[at], ka_recv.at[slot], 2 * at + core, z)

    chips(lambda at: k_scatter(at, chip).start())

    to_mate[1].wait_recv()
    to_mate[2].wait_recv()
    width = 2 * n.shard
    turn = (((0,), (0,)), ((), ()))

    def product(i, carry):
        cols = pl.ds(pl.multiple_of(i * width, 128), width)
        total = lax.dot_general(cot_ref[:, cols], act_ref[:, mine], turn, preferred_element_type=F32)
        total = total + lax.dot_general(mate_cot[:, cols], mate_act[...], turn, preferred_element_type=F32)
        part[2 * i] = total[: n.shard]
        part[2 * i + 1] = total[n.shard :]
        return carry

    lax.fori_loop(0, n.nz // 2, product, 0)

    low, high = slice(0, n.quarter), slice(n.quarter, n.half)

    def up_hop(step):
        lanes = pl.ds(0, n.quarter if step == 0 else n.half)
        return remote(
            up_out.at[step, :, lanes], up_in.at[step, :, lanes], u_send.at[step], u_recv.at[step], dp, up
        )

    def down_hop(step):
        lanes = pl.ds(n.quarter, n.quarter) if step == 0 else pl.ds(0, n.half)
        return remote(
            down_out.at[step, :, lanes], down_in.at[step, :, lanes], d_send.at[step], d_recv.at[step], dp, down
        )

    across = lax.rem(z + far, n.nz)
    up_out[0, :, low] = part[across, :, low].astype(BF16)
    up_hop(0).start()
    down_out[0, :, high] = part[across, :, high].astype(BF16)
    down_hop(0).start()

    def k_sum(step, carry):
        return carry + k_in[lax.rem(chip + step, n.chips)]

    def k_over_z(slot, to):
        return remote(k_z.at[z], k_z.at[slot], kz_send.at[to], kz_recv.at[slot], dp, to)

    for step in range(1, far):
        target = lax.rem(z + far - step, n.nz)
        up_hop(step - 1).wait_recv()
        if step == 1:
            up_out[step, :, low] = (part[target, :, low] + up_in[0, :, low].astype(F32)).astype(BF16)
            up_out[step, :, high] = part[target, :, high].astype(BF16)
        else:
            up_out[step] = (part[target] + up_in[step - 1].astype(F32)).astype(BF16)
        up_hop(step).start()
        target = lax.rem(z + n.nz - far + step, n.nz)
        down_hop(step - 1).wait_recv()
        if step == 1:
            down_out[step, :, high] = (part[target, :, high] + down_in[0, :, high].astype(F32)).astype(BF16)
            down_out[step, :, low] = part[target, :, low].astype(BF16)
        else:
            down_out[step] = (part[target] + down_in[step - 1].astype(F32)).astype(BF16)
        down_hop(step).start()
        if step == 1:
            chips(lambda at: k_scatter(chip, at).wait_recv())
            k_in[chip] = mate_k[k_rows(chip), :]
            k_z[z] = lax.fori_loop(1, n.chips, k_sum, k_in[chip])
            for hop in range(1, n.nz):
                k_over_z(z, lax.rem(z + hop, n.nz)).start()

    for hop in range(1, n.nz):
        src = lax.rem(z + hop, n.nz)
        k_over_z(src, src).wait_recv()
    total = k_z[0]
    for i in range(1, n.nz):
        total = total + k_z[i]
    k_all[chip] = total * scale

    def k_gather(slot, to):
        return remote(k_all.at[slot], k_all.at[slot], kc_send.at[to], kc_recv.at[slot], 2 * to + core, z)

    chips(lambda at: k_gather(chip, at).start())

    up_hop(far - 1).wait_recv()
    down_hop(far - 1).wait_recv()
    if far == 1:
        part[z, :, low] += up_in[0, :, low].astype(F32)
        part[z, :, high] += down_in[0, :, high].astype(F32)
    else:
        part[z] += up_in[far - 1].astype(F32) + down_in[far - 1].astype(F32)

    for i in range(n.cuts):
        for l in range(n.ltiles):
            value = part[z, n.prow * i : n.prow * (i + 1), 128 * l : 128 * (l + 1)]
            own_f[i * n.ltiles + l] = value
            own_b[i * n.ltiles + l] = value.astype(BF16)

    def scatter(at, slot):
        return remote(own_b.at[at], piece_in.at[slot], p_send.at[at], p_recv.at[slot], 2 * at + core, z)

    def gather(slot, to):
        return remote(all_b.at[slot], all_b.at[slot], a_send.at[to], a_recv.at[slot], 2 * to + core, z)

    def scatter_start(at):
        @pl.when(at < n.pieces)
        def _():
            scatter(at, chip).start()

    chips(scatter_start)

    exchange_arrive(n, dp, z, back_ref, home, h_send, h_recv)
    code = code_ref[...]
    place = lax.broadcasted_iota(jnp.int32, (n.rows, 16 * n.nb), 1)
    blocks = jnp.concatenate(
        [home[:, 16 * g : 16 * (g + 1), :].reshape(16 * n.nb, 128) for g in range(n.groups)], axis=1
    )
    for jj in range(4):
        rows = dot(one_hot(place == code + 4 * jj), blocks).astype(BF16)
        for g in range(n.groups):
            frames_out[:, 128 * (4 * g + jj) : 128 * (4 * g + jj + 1)] = rows[:, 128 * g : 128 * (g + 1)]

    @pl.when(chip < n.pieces)
    def _():
        chips(lambda at: scatter(chip, at).wait_recv())
        total = lax.fori_loop(
            1, n.chips, lambda step, carry: carry + piece_in[lax.rem(chip + step, n.chips)].astype(F32), own_f[chip]
        )
        all_b[chip] = (total * scale).astype(BF16)
        chips(lambda at: gather(chip, at).start())

    def gather_arrive(at):
        @pl.when(at < n.pieces)
        def _():
            gather(at, at).wait_recv()

    chips(lambda at: k_gather(at, at).wait_recv())
    swap_k = remote(k_all, k_mate, m_send.at[3], m_recv.at[3], mate, z)
    swap_k.start()
    chips(gather_arrive)
    swap = remote(all_b, mate_b, m_send.at[4], m_recv.at[4], mate, z)
    swap.start()

    def lay(source, half):
        for i in range(n.cuts):
            for l in range(n.ltiles):
                cols = pl.ds(pl.multiple_of(half * n.half + 128 * l, 128), 128)
                weight_out[n.prow * i : n.prow * (i + 1), cols] = source[i * n.ltiles + l].astype(F32)

    lay(all_b, core)
    ksum_out[core] = k_all[...]
    swap_k.wait_recv()
    ksum_out[other] = k_mate[...]
    swap.wait_recv()
    lay(mate_b, other)

    swap.wait_send()
    swap_k.wait_send()
    for copy in to_mate:
        copy.wait_send()
    for step in range(far):
        up_hop(step).wait_send()
        down_hop(step).wait_send()
    for hop in range(1, n.nz):
        k_over_z(z, lax.rem(z + hop, n.nz)).wait_send()
    chips(lambda at: k_scatter(at, chip).wait_send())
    chips(lambda at: k_gather(chip, at).wait_send())

    def scatter_sent(at):
        @pl.when(at < n.pieces)
        def _():
            scatter(at, chip).wait_send()

    chips(scatter_sent)

    @pl.when(chip < n.pieces)
    def _():
        chips(lambda at: gather(chip, at).wait_send())

    exchange_sent(n, dp, z, back_ref, home, h_send, h_recv)


def finish(n, scale, code_col, back, act, cot, kgrad):
    far = n.nz // 2
    dma = pltpu.SemaphoreType.DMA
    vmem = pl.BlockSpec(memory_space=pltpu.VMEM)
    ring = pltpu.VMEM((far, n.shard, n.half), BF16)
    chips = dma((n.chips,))
    return pl.pallas_call(
        functools.partial(finish_kernel, n, scale),
        out_shape=(
            jax.ShapeDtypeStruct((n.rows, n.ch), BF16),
            jax.ShapeDtypeStruct((n.shard, n.ch), F32),
            jax.ShapeDtypeStruct((2, n.chips, n.krow, 128), F32),
        ),
        in_specs=[vmem] * 5,
        out_specs=(vmem,) * 3,
        scratch_shapes=[
            pltpu.VMEM((n.nb, n.slab, 128), BF16),
            pltpu.VMEM((n.rows, n.half), BF16),
            pltpu.VMEM((n.rows, n.ch), BF16),
            pltpu.VMEM((n.kall, 128), F32),
            pltpu.VMEM((n.nz, n.shard, n.half), F32),
            ring, ring, ring, ring,
            pltpu.VMEM((n.chips, n.prow, 128), F32),
            pltpu.VMEM((n.chips, n.prow, 128), BF16),
            pltpu.VMEM((n.chips, n.prow, 128), BF16),
            pltpu.VMEM((n.pieces, n.prow, 128), BF16),
            pltpu.VMEM((n.pieces, n.prow, 128), BF16),
            pltpu.VMEM((n.chips, n.krow, 128), F32),
            pltpu.VMEM((n.nz, n.krow, 128), F32),
            pltpu.VMEM((n.chips, n.krow, 128), F32),
            pltpu.VMEM((n.chips, n.krow, 128), F32),
            dma((n.nd,)), dma((n.nd,)),
            dma((5,)), dma((5,)),
            dma((far,)), dma((far,)), dma((far,)), dma((far,)),
            chips, chips, chips, chips, chips, chips,
            dma((n.nz,)), dma((n.nz,)),
            chips, chips,
        ],
        compiler_params=pltpu.CompilerParams(
            collective_id=1, has_side_effects=True, vmem_limit_bytes=VMEM_BYTES
        ),
    )(code_col, back, act, cot, kgrad)


def on_device(frames, destination, utt_lengths, cotangent, weight, kernel, norm_gain, norm_shift):
    n = Sizes(lax.axis_size("dp"), lax.axis_size("fsdp"), frames.shape[0], frames.shape[1], weight.shape[0])
    owner = destination // n.nb
    slot = destination % n.nb
    row = jnp.arange(n.rows, dtype=jnp.int32) % BLOCK
    code = jnp.repeat(owner, BLOCK) * 16 + row
    here = owner[None, :] == jnp.arange(n.nd, dtype=jnp.int32)[:, None]
    slots = jnp.sum(jnp.where(here, slot[None, :], 0), axis=1).astype(F32)
    slots = jnp.broadcast_to(slots[:, None, None], (n.nd, 1, 128))
    arrived, labels, whole = dispatch(n, code[None, :], slots, frames, weight)
    tiled = kernel.reshape(TAPS, n.tiles, 128).transpose(1, 0, 2)
    back, act, kgrad = compute(
        n, utt_lengths, arrived, labels, whole, cotangent, tiled,
        norm_gain.reshape(n.tiles, 1, 128), norm_shift.reshape(n.tiles, 1, 128),
    )
    scale = 1.0 / math.sqrt(n.rows * n.nd * n.nz)
    grad_input, grad_weight, ksum = finish(n, scale, code[:, None], back, act, cotangent, kgrad)
    ksum = ksum.reshape(2, n.kall, 128)[:, : KROWS * n.ltiles].reshape(n.tiles, KROWS, 128)
    ksum = ksum.transpose(1, 0, 2).reshape(KROWS, n.ch)
    return grad_input, grad_weight, ksum[:TAPS], ksum[TAPS], ksum[TAPS + 1]


def solution(mesh):
    placed = (
        P(("dp", "fsdp"), None),
        P(("dp", "fsdp")),
        P(("dp", "fsdp"), None),
        P(("dp", "fsdp"), None),
        P("fsdp", None),
        P(),
        P(),
        P(),
    )
    return jax.shard_map(
        on_device,
        mesh=mesh,
        in_specs=placed,
        out_specs=(P(("dp", "fsdp"), None), P("fsdp", None), P(), P(), P()),
        check_vma=False,
    )
```

```python
import functools
import math

import jax
import jax.numpy as jnp
from jax import lax
from jax.experimental import pallas as pl
from jax.experimental.pallas import tpu as pltpu
from jax.sharding import PartitionSpec as P

EPSILON = 1e-05
MESH = pl.DeviceIdType.MESH
F32 = jnp.float32
BF16 = jnp.bfloat16
BLOCK = 4
TAPS = 31
HALO = 16
KROWS = 40
VMEM_BYTES = 56 * 1024 * 1024


class Sizes:
    def __init__(self, dp_size, fsdp_size, rows, channels, shard):
        self.nd = dp_size
        self.nz = fsdp_size
        self.rows = rows
        self.ch = channels
        self.shard = shard
        self.nb = rows // BLOCK
        self.tiles = channels // 128
        self.groups = self.tiles // 4
        self.slab = 4 * self.tiles
        self.chips = dp_size // 2
        self.half = channels // 2
        self.ltiles = self.half // 128
        self.quarter = self.half // 2
        self.nx = 4 if self.chips >= 32 else 2
        self.ny = self.chips // self.nx
        self.prow = shard // self.nx
        self.used = rows + 4 * HALO
        self.padded = self.used + 2 * HALO
        self.span = 80 if self.used % 80 == 0 else 48
        self.krow = 8 * (-(-(5 * self.ltiles) // self.chips))
        self.kall = self.krow * self.chips


def one_hot(mask):
    return jnp.where(mask, 1.0, 0.0).astype(BF16)


def dot(a, b):
    return jnp.dot(a, b, preferred_element_type=F32)


def remote(src, dst, send, recv, dp, z):
    return pltpu.make_async_remote_copy(
        src_ref=src, dst_ref=dst, send_sem=send, recv_sem=recv, device_id=(dp, z), device_id_type=MESH
    )


def padded_place(frame, ends):
    place = frame + HALO
    for end in ends:
        place = place + jnp.where(frame >= end, HALO, 0)
    return place


def module_kernel(
    n, scale,
    dest_ref, utt_ref, frames_ref, cot_ref, weight_ref, taps_ref, gain_ref, shift_ref,
    frames_out, weight_out, taps_out, gain_out, shift_out,
    outgoing, arrived, label_out, label_in, labels, whole,
    xs, filt, hidden, gf, slope, spread, actp, go, k8, kgrad, cot_pad, cot_turned, mate_cot, act_both, act_send,
    part, up_out, up_in, down_out, down_in, back, home,
    x_out, x_in, y_own, y_out, y_in, y_all, x_all, x_mate, mate_k, k_in, k_z, k_all, k_mate,
    b_send, b_recv, l_send, l_recv, h_send, h_recv,
    gu_send, gu_recv, gd_send, gd_recv, gm_send, gm_recv, m_send, m_recv,
    u_send, u_recv, d_send, d_recv,
    xr_send, xr_recv, yr_send, yr_recv, yg_send, yg_recv, xg_send, xg_recv,
    ka_send, ka_recv, kz_send, kz_recv, kc_send, kc_recv,
):
    dp = lax.axis_index("dp")
    z = lax.axis_index("fsdp")
    core = lax.rem(dp, 2)
    other = 1 - core
    mate = dp + 1 - 2 * core
    chip = dp // 2
    cx = chip // n.ny
    cy = lax.rem(chip, n.ny)
    far = n.nz // 2
    up = lax.rem(z + 1, n.nz)
    down = lax.rem(z + n.nz - 1, n.nz)
    hrow = n.shard // 2
    lanes = 16 * n.nb
    spans = range(n.used // n.span)
    mine = pl.ds(pl.multiple_of(core * n.half, 128), n.half)
    theirs = pl.ds(pl.multiple_of(other * n.half, 128), n.half)

    barrier = pltpu.get_barrier_semaphore()

    def along_dp(step, carry):
        pl.semaphore_signal(
            barrier, inc=1, device_id=(lax.rem(dp + step, n.nd), z), device_id_type=MESH
        )
        return carry

    lax.fori_loop(1, n.nd, along_dp, 0)
    for step in range(1, n.nz):
        pl.semaphore_signal(
            barrier, inc=1, device_id=(dp, lax.rem(z + step, n.nz)), device_id_type=MESH
        )

    whole[z] = weight_ref[...]

    lane128 = lax.broadcasted_iota(jnp.int32, (1, 128), 1)
    lane_rows = lax.broadcasted_iota(jnp.int32, (1, n.rows), 1)

    def read_block(b, carry):
        code, owners, slots = carry
        dest = dest_ref[b]
        owner = dest // n.nb
        slot = dest - owner * n.nb
        code = jnp.where(lane_rows // BLOCK == b, owner * 16, code)
        owners = jnp.where(lane128 == b, owner, owners)
        slots = jnp.where(lane128 == b, slot, slots)
        return code, owners, slots

    start = (jnp.zeros((1, n.rows), jnp.int32), jnp.full((1, 128), -1, jnp.int32), jnp.zeros((1, 128), jnp.int32))
    code, owners, slots = lax.fori_loop(0, n.nb, read_block, start)
    code = code + lane_rows % BLOCK
    owner_iota = lax.broadcasted_iota(jnp.int32, (n.nd, 128), 0)
    slot_of = jnp.sum(jnp.where(owner_iota == owners, slots, 0).astype(F32), axis=1, keepdims=True)
    slot_of = jnp.broadcast_to(slot_of, (n.nd, 128))
    for i in range(n.nd):
        label_out[i] = slot_of[i : i + 1]

    mats = [
        jnp.concatenate(
            [frames_ref[:, 128 * (4 * g + jj) : 128 * (4 * g + jj + 1)] for g in range(n.groups)], axis=1
        )
        for jj in range(4)
    ]
    chunk_rows = min(256, lanes)
    per_chunk = chunk_rows // 16

    def sort_chunk(chunk, carry):
        place = lax.broadcasted_iota(jnp.int32, (chunk_rows, n.rows), 0) + chunk * chunk_rows
        total = dot(one_hot(place == code), mats[0])
        for jj in range(1, 4):
            total = total + dot(one_hot(place == code + 4 * jj), mats[jj])
        for g in range(n.groups):
            piece = total[:, 128 * g : 128 * (g + 1)].astype(BF16).reshape(per_chunk, 16, 128)
            outgoing[pl.ds(chunk * per_chunk, per_chunk), 16 * g : 16 * (g + 1), :] = piece
        return carry

    lax.fori_loop(0, lanes // chunk_rows, sort_chunk, 0)

    pl.semaphore_wait(barrier, n.nd - 1 + n.nz - 1)

    def gather_hop(step, block, first, count, to, send, recv):
        rows = pl.ds(pl.multiple_of(core * hrow + first, 16), count)
        return remote(whole.at[block, rows], whole.at[block, rows], send.at[step], recv.at[step], dp, to)

    def gather_up(step, block):
        last = step == far - 1
        return gather_hop(step, block, 0, hrow // 2 if last else hrow, up, gu_send, gu_recv)

    def gather_down(step, block):
        last = step == far - 1
        return gather_hop(step, block, hrow // 2 if last else 0, hrow // 2 if last else hrow, down, gd_send, gd_recv)

    def gather_mate(slot, block, half):
        rows = pl.ds(pl.multiple_of(half * hrow, 16), hrow)
        return remote(whole.at[block, rows], whole.at[block, rows], gm_send.at[slot], gm_recv.at[slot], mate, z)

    def below(step):
        return lax.rem(z + n.nz - step - 1, n.nz)

    def above(step):
        return lax.rem(z + step + 1, n.nz)

    def gather_pass(step):
        gather_up(step, below(step)).wait_recv()
        if step < far - 1:
            gather_up(step + 1, below(step)).start()
            gather_mate(2 * step, below(step), core).start()
        gather_down(step, above(step)).wait_recv()
        if step < far - 1:
            gather_down(step + 1, above(step)).start()
            gather_mate(2 * step + 1, above(step), core).start()
        else:
            gather_mate(2 * step, above(step), core).start()

    gather_up(0, z).start()
    gather_down(0, z).start()

    def block_to(peer):
        return remote(outgoing.at[peer], arrived.at[dp], b_send.at[peer], b_recv.at[dp], peer, z)

    def block_from(peer):
        return remote(outgoing.at[peer], arrived.at[peer], b_send.at[peer], b_recv.at[peer], peer, z)

    def label_to(peer):
        return remote(label_out.at[peer], label_in.at[dp], l_send.at[peer], l_recv.at[dp], peer, z)

    def label_from(peer):
        return remote(label_out.at[peer], label_in.at[peer], l_send.at[peer], l_recv.at[peer], peer, z)

    def peers(body):
        def step_to(step, carry):
            body(lax.rem(dp + step, n.nd))
            return carry

        lax.fori_loop(1, n.nd, step_to, 0)

    def chips(body):
        def step_to(step, carry):
            body(lax.rem(chip + step, n.chips))
            return carry

        lax.fori_loop(1, n.chips, step_to, 0)

    def send_block(peer):
        label_to(peer).start()
        block_to(peer).start()

    peers(send_block)
    swap_cot = remote(cot_ref, mate_cot, m_send.at[0], m_recv.at[0], mate, z)
    swap_cot.start()
    arrived[dp] = outgoing[dp]
    label_in[dp] = label_out[dp]

    ends = [utt_ref[0, 0]]
    for i in range(1, 3):
        ends.append(ends[-1] + utt_ref[0, i])
    frame_row = padded_place(lane_rows, ends)
    pad_mat = one_hot(lax.broadcasted_iota(jnp.int32, (n.padded, n.rows), 0) == frame_row)
    cot_pad[...] = dot(pad_mat, cot_ref[...]).astype(BF16)
    cot_turned[:, : n.rows] = cot_ref[...].T
    kgrad[...] = jnp.zeros_like(kgrad)
    actp[...] = jnp.zeros_like(actp)
    go[...] = jnp.zeros_like(go)
    gf[:, :HALO, :] = jnp.zeros((n.tiles, HALO, 128), F32)
    gf[:, n.padded - HALO :, :] = jnp.zeros((n.tiles, HALO, 128), F32)
    swap_cot.wait_recv()
    cot_turned[:, n.rows :] = mate_cot[...].T

    for step in range(far - 1):
        gather_pass(step)

    peers(lambda peer: label_from(peer).wait_recv())
    chunks = []
    for q in range(n.nb // 8):
        row = jnp.zeros((1, 128), F32)
        for s in range(8):
            row = row + jnp.where(lane128 // 16 == s, label_in[8 * q + s], 0.0)
        chunks.append(row)
    slot_row = jnp.concatenate(chunks, axis=1).astype(jnp.int32)
    lane_all = lax.broadcasted_iota(jnp.int32, (1, lanes), 1)
    place_row = padded_place(slot_row * BLOCK + lane_all % 4, ends)

    def lay_label(src, carry):
        labels[pl.ds(pl.multiple_of(16 * src, 16), 16), :] = jnp.broadcast_to(label_in[src], (16, 128))
        return carry

    lax.fori_loop(0, n.nb, lay_label, 0)

    peers(lambda peer: block_from(peer).wait_recv())
    blocks = jnp.concatenate(
        [arrived[:, 16 * g : 16 * (g + 1), :].reshape(lanes, 128) for g in range(n.groups)], axis=1
    )
    row_iota = lax.broadcasted_iota(jnp.int32, (n.padded, lanes), 0)

    def put(jj, carry):
        owned = dot(one_hot(row_iota == jnp.where((lane_all // 4) % 4 == jj, place_row, -1)), blocks)
        for g in range(n.groups):
            xs[4 * g + jj] = owned[:, 128 * g : 128 * (g + 1)]
        return carry

    lax.fori_loop(0, 4, put, 0)

    def filter_tile(j, carry):
        taps = taps_ref[:, pl.ds(pl.multiple_of(j * 128, 128), 128)]
        for b in spans:
            base = 1 + n.span * b
            total = jnp.zeros((n.span, 128), F32)
            for s in range(8):
                window = xs[j, base + s : base + s + n.span + 24, :]
                for m in range(4):
                    k = s + 8 * m
                    if k < TAPS:
                        total = total + taps[k : k + 1] * window[8 * m : 8 * m + n.span]
            filt[j, HALO + n.span * b : HALO + n.span * (b + 1), :] = total
        return carry

    lax.fori_loop(0, n.tiles, filter_tile, 0)

    def norm_span(b, carry):
        rows = pl.ds(pl.multiple_of(HALO + n.span * b, 16), n.span)
        total = filt[0, rows, :]
        for j in range(1, n.tiles):
            total = total + filt[j, rows, :]
        mean = jnp.sum(total, axis=1, keepdims=True) * (1.0 / n.ch)
        square = jnp.zeros((n.span, 128), F32)
        for j in range(n.tiles):
            centred = filt[j, rows, :] - mean
            square = square + centred * centred
        variance = jnp.sum(square, axis=1, keepdims=True) * (1.0 / n.ch)
        inverse = 1.0 / jnp.sqrt(variance + EPSILON)
        spread[rows, :] = jnp.broadcast_to(inverse, (n.span, 128))
        for j in range(n.tiles):
            whitened = (filt[j, rows, :] - mean) * inverse
            normed = whitened * gain_ref[:, 128 * j : 128 * (j + 1)] + shift_ref[:, 128 * j : 128 * (j + 1)]
            logistic = 1.0 / (1.0 + jnp.exp(-normed))
            activated = normed * logistic
            actp[rows, 128 * j : 128 * (j + 1)] = activated.astype(BF16)
            filt[j, rows, :] = whitened
            slope[j, rows, :] = logistic * (1.0 + normed * (1.0 - logistic))
        return carry

    lax.fori_loop(0, n.used // n.span, norm_span, 0)

    frame_col = padded_place(lax.broadcasted_iota(jnp.int32, (n.rows, 1), 0), ends)
    take = one_hot(lax.broadcasted_iota(jnp.int32, (n.rows, n.padded), 1) == frame_col)
    act_send[...] = dot(take, actp[:, theirs]).astype(BF16)
    swap_act = remote(act_send, act_both.at[pl.ds(n.rows, n.rows)], m_send.at[1], m_recv.at[1], mate, z)
    swap_act.start()
    act_both[: n.rows] = dot(take, actp[:, mine]).astype(BF16)

    gather_pass(far - 1)
    for step in range(far):
        gather_mate(2 * step, below(step) if step < far - 1 else above(step), other).wait_recv()
        if step < far - 1:
            gather_mate(2 * step + 1, above(step), other).wait_recv()
    width = 512
    per = width // 128

    def project(i, carry):
        cols = pl.ds(pl.multiple_of(i * width, width), width)
        piece = dot(cot_pad[...], whole[:, :, cols].reshape(n.ch, width))
        for q in range(per):
            hidden[per * i + q] = piece[:, 128 * q : 128 * (q + 1)]
        return carry

    lax.fori_loop(0, n.ch // width, project, 0)

    swap_act.wait_recv()

    def product(target):
        part[target] = dot(cot_turned[pl.ds(pl.multiple_of(target * n.shard, 16), n.shard), :], act_both[...])

    chunk_of = [slice(0, n.quarter), slice(n.quarter, n.half)]

    def ring_hop(way, chunk, step):
        out, into, send, recv, to = (
            (up_out, up_in, u_send, u_recv, up) if way == 0 else (down_out, down_in, d_send, d_recv, down)
        )
        at = far * chunk + step
        return remote(out.at[chunk, step], into.at[chunk, step], send.at[at], recv.at[at], dp, to)

    def ring_target(way, chunk, step):
        ahead = (far if way == chunk else far - 1) - step
        return lax.rem(z + ahead, n.nz) if way == 0 else lax.rem(z + n.nz - ahead, n.nz)

    def ring_steps(way, chunk):
        return far if way == chunk else far - 1

    def ring_step(step):
        for way, chunk in ((0, 0), (1, 1), (0, 1), (1, 0)):
            if step < ring_steps(way, chunk):
                out, into = (up_out, up_in) if way == 0 else (down_out, down_in)
                value = part[ring_target(way, chunk, step), :, chunk_of[chunk]]
                if step > 0:
                    ring_hop(way, chunk, step - 1).wait_recv()
                    value = value + into[chunk, step - 1].astype(F32)
                out[chunk, step] = value.astype(BF16)
                ring_hop(way, chunk, step).start()

    product(lax.rem(z + far, n.nz))
    if far > 1:
        product(lax.rem(z + far - 1, n.nz))
        product(lax.rem(z + n.nz - far + 1, n.nz))
    ring_step(0)

    def products(i, carry):
        product(lax.rem(z + n.nz - far + 2 + i, n.nz))
        return carry

    if far > 1:
        lax.fori_loop(0, n.nz - 3, products, 0)
    else:
        product(z)

    def norm_back(b, carry):
        rows = pl.ds(pl.multiple_of(HALO + n.span * b, 16), n.span)
        first = jnp.zeros((n.span, 128), F32)
        second = jnp.zeros((n.span, 128), F32)
        for j in range(n.tiles):
            whitened = filt[j, rows, :]
            grad_normed = hidden[j, rows, :] * slope[j, rows, :]
            scaled = grad_normed * gain_ref[:, 128 * j : 128 * (j + 1)]
            hidden[j, rows, :] = scaled
            first = first + scaled
            second = second + scaled * whitened
            half, at = j // n.ltiles, (j % n.ltiles) * KROWS
            kgrad[half, at + TAPS : at + TAPS + 1, :] += jnp.sum(grad_normed * whitened, axis=0, keepdims=True)
            kgrad[half, at + TAPS + 1 : at + TAPS + 2, :] += jnp.sum(grad_normed, axis=0, keepdims=True)
        mean1 = jnp.sum(first, axis=1, keepdims=True) * (1.0 / n.ch)
        mean2 = jnp.sum(second, axis=1, keepdims=True) * (1.0 / n.ch)
        inverse = spread[rows, :]
        for j in range(n.tiles):
            gf[j, rows, :] = inverse * (hidden[j, rows, :] - mean1 - filt[j, rows, :] * mean2)
        return carry

    lax.fori_loop(0, n.used // n.span, norm_back, 0)

    def back_tile(j, carry):
        taps = taps_ref[:, pl.ds(pl.multiple_of(j * 128, 128), 128)]
        for b in spans:
            base = 1 + n.span * b
            here = slice(HALO + n.span * b, HALO + n.span * (b + 1))
            signal = xs[j, here, :]
            total = jnp.zeros((n.span, 128), F32)
            for s in range(8):
                window = gf[j, base + s : base + s + n.span + 24, :]
                for m in range(4):
                    k = TAPS - 1 - s - 8 * m
                    if k >= 0:
                        shifted = window[8 * m : 8 * m + n.span]
                        total = total + taps[k : k + 1] * shifted
                        product = jnp.sum((shifted * signal).reshape(n.span // 8, 8, 128), axis=0)
                        if b == 0:
                            k8[k] = product
                        else:
                            k8[k] += product
            go[j, here, :] = total.astype(BF16)
        at = pl.multiple_of(lax.rem(j, n.ltiles) * KROWS, 8)
        kgrad[j // n.ltiles, pl.ds(at, TAPS), :] = jnp.sum(k8[...], axis=1)
        return carry

    third = n.tiles // 3
    lax.fori_loop(0, third, back_tile, 0)
    if far > 1:
        ring_step(1)
    lax.fori_loop(third, n.tiles, back_tile, 0)
    swap_k = remote(kgrad.at[other], mate_k, m_send.at[2], m_recv.at[2], mate, z)
    swap_k.start()
    if far > 2:
        ring_step(2)

    def gather_chunk(chunk, carry):
        at = pl.ds(pl.multiple_of(chunk * chunk_rows, chunk_rows), chunk_rows)
        slot = labels[at, :][:, :1].astype(jnp.int32)
        sub = lax.broadcasted_iota(jnp.int32, (chunk_rows, 1), 0)
        place = padded_place(slot * BLOCK + sub % 4, ends)
        cols = lax.broadcasted_iota(jnp.int32, (chunk_rows, n.padded), 1)
        total = None
        for jj in range(4):
            rhs = jnp.concatenate([go[4 * g + jj] for g in range(n.groups)], axis=1)
            piece = dot(one_hot(cols == jnp.where((sub // 4) % 4 == jj, place, -1)), rhs)
            total = piece if total is None else total + piece
        for g in range(n.groups):
            piece = total[:, 128 * g : 128 * (g + 1)].astype(BF16).reshape(per_chunk, 16, 128)
            back[pl.ds(chunk * per_chunk, per_chunk), 16 * g : 16 * (g + 1), :] = piece
        return carry

    lax.fori_loop(0, lanes // chunk_rows, gather_chunk, 0)

    def home_to(peer):
        return remote(back.at[peer], home.at[dp], h_send.at[peer], h_recv.at[dp], peer, z)

    def home_from(peer):
        return remote(back.at[peer], home.at[peer], h_send.at[peer], h_recv.at[peer], peer, z)

    peers(lambda peer: home_to(peer).start())
    home[dp] = back[dp]

    swap_k.wait_recv()
    mate_k[...] += kgrad[core]

    def k_rows(at):
        return pl.ds(pl.multiple_of(at * n.krow, 8), n.krow)

    def k_scatter(at, slot):
        return remote(mate_k.at[k_rows(at)], k_in.at[slot], ka_send.at[at], ka_recv.at[slot], 2 * at + core, z)

    def k_over_z(slot, to):
        return remote(k_z.at[z], k_z.at[slot], kz_send.at[to], kz_recv.at[slot], dp, to)

    def k_gather(slot, to):
        return remote(k_all.at[slot], k_all.at[slot], kc_send.at[to], kc_recv.at[slot], 2 * to + core, z)

    chips(lambda at: k_scatter(at, chip).start())

    for step in range(3, far):
        ring_step(step)

    for way, chunk in ((1, 0), (0, 1), (0, 0), (1, 1)):
        steps = ring_steps(way, chunk)
        if steps > 0:
            into = up_in if way == 0 else down_in
            ring_hop(way, chunk, steps - 1).wait_recv()
            part[z, :, chunk_of[chunk]] += into[chunk, steps - 1].astype(F32)

    def along_x(step):
        there = lax.rem(cx + step, n.nx)
        return there, (there * n.ny + cy) * 2 + core

    def along_y(step):
        there = lax.rem(cy + step, n.ny)
        return there, (cx * n.ny + there) * 2 + core

    def x_scatter(step, arriving):
        there, peer = along_x(step)
        slot = there if arriving else cx
        return remote(x_out.at[there], x_in.at[slot], xr_send.at[there], xr_recv.at[slot], peer, z)

    def y_scatter(step, arriving):
        there, peer = along_y(step)
        slot = there if arriving else cy
        return there, remote(y_out.at[there], y_in.at[slot], yr_send.at[there], yr_recv.at[slot], peer, z)

    def y_gather(step, arriving):
        there, peer = along_y(step)
        slot = there if arriving else cy
        return there, remote(y_all.at[slot], y_all.at[slot], yg_send.at[there], yg_recv.at[slot], peer, z)

    def x_gather(step, arriving):
        there, peer = along_x(step)
        slot = there if arriving else cx
        return remote(x_all.at[slot], x_all.at[slot], xg_send.at[there], xg_recv.at[slot], peer, z)

    for i in range(n.nx):
        x_out[i] = part[z, n.prow * i : n.prow * (i + 1), :].astype(BF16)
    for step in range(1, n.nx):
        x_scatter(step, False).start()

    chips(lambda at: k_scatter(chip, at).wait_recv())
    k_in[chip] = mate_k[k_rows(chip), :]

    def k_sum(step, carry):
        return carry + k_in[lax.rem(chip + step, n.chips)]

    k_z[z] = lax.fori_loop(1, n.chips, k_sum, k_in[chip])
    for hop in range(1, n.nz):
        k_over_z(z, lax.rem(z + hop, n.nz)).start()

    band = part[z, pl.ds(pl.multiple_of(cx * n.prow, 16), n.prow), :]
    for step in range(1, n.nx):
        x_scatter(step, True).wait_recv()
        band = band + x_in[lax.rem(cx + step, n.nx)].astype(F32)
    for l in range(n.ltiles):
        y_own[l] = band[:, 128 * l : 128 * (l + 1)]
        y_out[l] = band[:, 128 * l : 128 * (l + 1)].astype(BF16)
    for step in range(1, n.ny):
        there, copy = y_scatter(step, False)

        @pl.when(there < n.ltiles)
        def _():
            copy.start()

    for hop in range(1, n.nz):
        src = lax.rem(z + hop, n.nz)
        k_over_z(src, src).wait_recv()
    small = k_z[0]
    for i in range(1, n.nz):
        small = small + k_z[i]
    k_all[chip] = small * scale
    chips(lambda at: k_gather(chip, at).start())

    @pl.when(cy < n.ltiles)
    def _():
        total = y_own[cy]
        for step in range(1, n.ny):
            there, copy = y_scatter(step, True)
            copy.wait_recv()
            total = total + y_in[there].astype(F32)
        y_all[cy] = (total * scale).astype(BF16)
        for step in range(1, n.ny):
            y_gather(step, False)[1].start()

    for step in range(1, n.ny):
        there, copy = y_gather(step, True)

        @pl.when(there < n.ltiles)
        def _():
            copy.wait_recv()

    for l in range(n.ltiles):
        x_all[cx, :, 128 * l : 128 * (l + 1)] = y_all[l]
    for step in range(1, n.nx):
        x_gather(step, False).start()

    chips(lambda at: k_gather(at, at).wait_recv())
    swap_all = remote(k_all, k_mate, m_send.at[3], m_recv.at[3], mate, z)
    swap_all.start()

    for step in range(1, n.nx):
        x_gather(step, True).wait_recv()
    swap_weight = remote(x_all, x_mate, m_send.at[4], m_recv.at[4], mate, z)
    swap_weight.start()

    def lay_weight(source, half):
        cols = pl.ds(pl.multiple_of(half * n.half, 128), n.half)
        for i in range(n.nx):
            weight_out[n.prow * i : n.prow * (i + 1), cols] = source[i].astype(F32)

    def lay_small(source, half):
        rows = source[...].reshape(n.kall, 128)
        for l in range(n.ltiles):
            cols = pl.ds(pl.multiple_of(half * n.half + 128 * l, 128), 128)
            taps_out[:, cols] = rows[KROWS * l : KROWS * l + TAPS]
            gain_out[:, cols] = rows[KROWS * l + TAPS : KROWS * l + TAPS + 1]
            shift_out[:, cols] = rows[KROWS * l + TAPS + 1 : KROWS * l + TAPS + 2]

    lay_weight(x_all, core)
    lay_small(k_all, core)

    peers(lambda peer: home_from(peer).wait_recv())
    sub_rows = lax.broadcasted_iota(jnp.int32, (n.rows, 1), 0)

    def read_owner(b, carry):
        return jnp.where(sub_rows // BLOCK == b, (dest_ref[b] // n.nb) * 16, carry)

    code_col = lax.fori_loop(0, n.nb, read_owner, jnp.zeros((n.rows, 1), jnp.int32)) + sub_rows % BLOCK
    place = lax.broadcasted_iota(jnp.int32, (n.rows, lanes), 1)
    blocks = jnp.concatenate(
        [home[:, 16 * g : 16 * (g + 1), :].reshape(lanes, 128) for g in range(n.groups)], axis=1
    )
    for jj in range(4):
        rows = dot(one_hot(place == code_col + 4 * jj), blocks).astype(BF16)
        for g in range(n.groups):
            frames_out[:, 128 * (4 * g + jj) : 128 * (4 * g + jj + 1)] = rows[:, 128 * g : 128 * (g + 1)]

    swap_all.wait_recv()
    lay_small(k_mate, other)
    swap_weight.wait_recv()
    lay_weight(x_mate, other)

    for copy in (swap_cot, swap_act, swap_k, swap_all, swap_weight):
        copy.wait_send()
    for step in range(far):
        gather_up(step, z).wait_send()
        gather_down(step, z).wait_send()
        gather_mate(2 * step, z, core).wait_send()
        if step < far - 1:
            gather_mate(2 * step + 1, z, core).wait_send()
    for way in range(2):
        for chunk in range(2):
            for step in range(ring_steps(way, chunk)):
                ring_hop(way, chunk, step).wait_send()
    for step in range(1, n.nx):
        x_scatter(step, False).wait_send()
        x_gather(step, False).wait_send()
    for step in range(1, n.ny):
        there, copy = y_scatter(step, False)

        @pl.when(there < n.ltiles)
        def _():
            copy.wait_send()

    @pl.when(cy < n.ltiles)
    def _():
        for step in range(1, n.ny):
            y_gather(step, False)[1].wait_send()

    for hop in range(1, n.nz):
        k_over_z(z, lax.rem(z + hop, n.nz)).wait_send()

    def small_sent(at):
        k_scatter(at, chip).wait_send()
        k_gather(chip, at).wait_send()

    chips(small_sent)

    def blocks_sent(peer):
        label_to(peer).wait_send()
        block_to(peer).wait_send()
        home_to(peer).wait_send()

    peers(blocks_sent)


def on_device(frames, destination, utt_lengths, cotangent, weight, kernel, norm_gain, norm_shift):
    n = Sizes(lax.axis_size("dp"), lax.axis_size("fsdp"), frames.shape[0], frames.shape[1], weight.shape[0])
    scale = 1.0 / math.sqrt(n.rows * n.nd * n.nz)
    far = n.nz // 2
    vmem = pl.BlockSpec(memory_space=pltpu.VMEM)
    smem = pl.BlockSpec(memory_space=pltpu.SMEM)

    def dma(count):
        return [pltpu.SemaphoreType.DMA((count,))] * 2

    def buf(*shape, dtype=F32):
        return pltpu.VMEM(shape, dtype)

    blocks = buf(n.nb, n.slab, 128, dtype=BF16)
    label = buf(n.nd, 1, 128)
    plane = buf(n.tiles, n.padded, 128)
    ring = buf(2, far, n.shard, n.quarter, dtype=BF16)
    band = buf(n.nx, n.prow, n.half, dtype=BF16)
    tile = buf(n.ny, n.prow, 128, dtype=BF16)
    small = buf(n.chips, n.krow, 128)
    grads = pl.pallas_call(
        functools.partial(module_kernel, n, scale),
        out_shape=(
            jax.ShapeDtypeStruct((n.rows, n.ch), BF16),
            jax.ShapeDtypeStruct((n.shard, n.ch), F32),
            jax.ShapeDtypeStruct((TAPS, n.ch), F32),
            jax.ShapeDtypeStruct((1, n.ch), F32),
            jax.ShapeDtypeStruct((1, n.ch), F32),
        ),
        in_specs=[smem, smem] + [vmem] * 6,
        out_specs=(vmem,) * 5,
        scratch_shapes=[
            blocks, blocks, label, label, buf(16 * n.nb, 128), buf(n.nz, n.shard, n.ch, dtype=BF16),
            plane, plane, plane, plane, plane, buf(n.padded, 128), buf(n.padded, n.ch, dtype=BF16),
            buf(n.tiles, n.padded, 128, dtype=BF16), buf(TAPS, 8, 128), buf(2, n.kall, 128),
            buf(n.padded, n.ch, dtype=BF16), buf(n.ch, 2 * n.rows, dtype=BF16), buf(n.rows, n.ch, dtype=BF16),
            buf(2 * n.rows, n.half, dtype=BF16), buf(n.rows, n.half, dtype=BF16),
            buf(n.nz, n.shard, n.half), ring, ring, ring, ring, blocks, blocks,
            band, band, buf(n.ltiles, n.prow, 128), tile, tile, tile, band, band,
            buf(n.kall, 128), small, buf(n.nz, n.krow, 128), small, small,
            *dma(n.nd), *dma(n.nd), *dma(n.nd),
            *dma(far), *dma(far), *dma(2 * far), *dma(5),
            *dma(2 * far), *dma(2 * far),
            *dma(n.nx), *dma(n.ny), *dma(n.ny), *dma(n.nx),
            *dma(n.chips), *dma(n.nz), *dma(n.chips),
        ],
        compiler_params=pltpu.CompilerParams(
            collective_id=0, has_side_effects=True, vmem_limit_bytes=VMEM_BYTES
        ),
    )(destination, utt_lengths, frames, cotangent, weight, kernel, norm_gain[None, :], norm_shift[None, :])
    return grads[0], grads[1], grads[2], grads[3][0], grads[4][0]


def solution(mesh):
    placed = (
        P(("dp", "fsdp"), None),
        P(("dp", "fsdp")),
        P(("dp", "fsdp"), None),
        P(("dp", "fsdp"), None),
        P("fsdp", None),
        P(),
        P(),
        P(),
    )
    return jax.shard_map(
        on_device,
        mesh=mesh,
        in_specs=placed,
        out_specs=(P(("dp", "fsdp"), None), P("fsdp", None), P(), P(), P()),
        check_vma=False,
    )
```

```python
import functools
import math

import jax
import jax.numpy as jnp
from jax import lax
from jax.experimental import pallas as pl
from jax.experimental.pallas import tpu as pltpu
from jax.sharding import PartitionSpec as P

EPSILON = 1e-05
MESH = pl.DeviceIdType.MESH
F32 = jnp.float32
BF16 = jnp.bfloat16
BLOCK = 4
TAPS = 31
HALO = 16
KROWS = 40
VMEM_BYTES = 56 * 1024 * 1024


class Sizes:
    def __init__(self, dp_size, fsdp_size, rows, channels, shard):
        self.nd = dp_size
        self.nz = fsdp_size
        self.rows = rows
        self.ch = channels
        self.shard = shard
        self.nb = rows // BLOCK
        self.tiles = channels // 128
        self.groups = self.tiles // 4
        self.slab = 4 * self.tiles
        self.chips = dp_size // 2
        self.half = channels // 2
        self.ltiles = self.half // 128
        self.quarter = self.half // 2
        self.nx = 4 if self.chips >= 32 else 2
        self.ny = self.chips // self.nx
        self.prow = shard // self.nx
        self.used = rows + 4 * HALO
        self.padded = self.used + 2 * HALO
        self.span = 80 if self.used % 80 == 0 else 48
        self.krow = 8 * (-(-(5 * self.ltiles) // self.chips))
        self.kall = self.krow * self.chips


def one_hot(mask):
    return jnp.where(mask, 1.0, 0.0).astype(BF16)


def dot(a, b):
    return jnp.dot(a, b, preferred_element_type=F32)


def remote(src, dst, send, recv, dp, z):
    return pltpu.make_async_remote_copy(
        src_ref=src, dst_ref=dst, send_sem=send, recv_sem=recv, device_id=(dp, z), device_id_type=MESH
    )


def padded_place(frame, ends):
    place = frame + HALO
    for end in ends:
        place = place + jnp.where(frame >= end, HALO, 0)
    return place


def module_kernel(
    n, scale,
    dest_ref, utt_ref, frames_ref, cot_ref, weight_ref, taps_ref, gain_ref, shift_ref,
    frames_out, weight_out, taps_out, gain_out, shift_out,
    outgoing, arrived, label_out, label_in, labels, whole, unsort, setting, taking,
    xs, filt, hidden, gf, slope, spread, actp, go, k8, kgrad, cot_pad, cot_turned, mate_cot, act_both, act_send,
    part, up_out, up_in, down_out, down_in, back, home,
    x_out, x_in, y_own, y_out, y_in, y_all, x_all, x_mate, mate_k, k_in, k_z, k_all, k_mate,
    b_send, b_recv, l_send, l_recv, h_send, h_recv,
    gu_send, gu_recv, gd_send, gd_recv, gm_send, gm_recv, m_send, m_recv,
    u_send, u_recv, d_send, d_recv,
    xr_send, xr_recv, yr_send, yr_recv, yg_send, yg_recv, xg_send, xg_recv,
    ka_send, ka_recv, kz_send, kz_recv, kc_send, kc_recv,
):
    dp = lax.axis_index("dp")
    z = lax.axis_index("fsdp")
    core = lax.rem(dp, 2)
    other = 1 - core
    mate = dp + 1 - 2 * core
    chip = dp // 2
    cx = chip // n.ny
    cy = lax.rem(chip, n.ny)
    far = n.nz // 2
    up = lax.rem(z + 1, n.nz)
    down = lax.rem(z + n.nz - 1, n.nz)
    hrow = n.shard // 2
    lanes = 16 * n.nb
    spans = range(n.used // n.span)
    mine = pl.ds(pl.multiple_of(core * n.half, 128), n.half)
    theirs = pl.ds(pl.multiple_of(other * n.half, 128), n.half)

    barrier = pltpu.get_barrier_semaphore()

    def along_dp(step, carry):
        pl.semaphore_signal(
            barrier, inc=1, device_id=(lax.rem(dp + step, n.nd), z), device_id_type=MESH
        )
        return carry

    lax.fori_loop(1, n.nd, along_dp, 0)
    for step in range(1, n.nz):
        pl.semaphore_signal(
            barrier, inc=1, device_id=(dp, lax.rem(z + step, n.nz)), device_id_type=MESH
        )

    whole[z] = weight_ref[...]

    lane_rows = lax.broadcasted_iota(jnp.int32, (1, n.rows), 1)
    dest = dest_ref[...].reshape(1, n.nb)
    owners = dest // n.nb
    slots = dest - owners * n.nb
    owner_iota = lax.broadcasted_iota(jnp.int32, (n.nd, n.nb), 0)
    slot_of = jnp.sum(jnp.where(owner_iota == owners, slots, 0).astype(F32), axis=1, keepdims=True)
    slot_of = jnp.broadcast_to(slot_of, (n.nd, 128))
    for i in range(n.nd):
        label_out[i] = slot_of[i : i + 1]
    four = one_hot(
        lax.broadcasted_iota(jnp.int32, (n.nb, n.rows), 0)
        == lax.broadcasted_iota(jnp.int32, (n.nb, n.rows), 1) // BLOCK
    )
    wide = dot(jnp.broadcast_to(owners.astype(F32), (16, n.nb)).astype(BF16), four)[:1]
    code = wide.astype(jnp.int32) * 16 + lane_rows % BLOCK

    mats = [
        jnp.concatenate(
            [frames_ref[:, 128 * (4 * g + jj) : 128 * (4 * g + jj + 1)] for g in range(n.groups)], axis=1
        )
        for jj in range(4)
    ]
    chunk_rows = min(256, lanes)
    per_chunk = chunk_rows // 16

    def sort_chunk(chunk, carry):
        place = lax.broadcasted_iota(jnp.int32, (chunk_rows, n.rows), 0) + chunk * chunk_rows
        total = dot(one_hot(place == code), mats[0])
        for jj in range(1, 4):
            total = total + dot(one_hot(place == code + 4 * jj), mats[jj])
        for g in range(n.groups):
            piece = total[:, 128 * g : 128 * (g + 1)].astype(BF16).reshape(per_chunk, 16, 128)
            outgoing[pl.ds(chunk * per_chunk, per_chunk), 16 * g : 16 * (g + 1), :] = piece
        return carry

    lax.fori_loop(0, lanes // chunk_rows, sort_chunk, 0)

    pl.semaphore_wait(barrier, n.nd - 1 + n.nz - 1)

    def gather_hop(step, block, first, count, to, send, recv):
        rows = pl.ds(pl.multiple_of(core * hrow + first, 16), count)
        return remote(whole.at[block, rows], whole.at[block, rows], send.at[step], recv.at[step], dp, to)

    def gather_up(step, block):
        last = step == far - 1
        return gather_hop(step, block, 0, hrow // 2 if last else hrow, up, gu_send, gu_recv)

    def gather_down(step, block):
        last = step == far - 1
        return gather_hop(step, block, hrow // 2 if last else 0, hrow // 2 if last else hrow, down, gd_send, gd_recv)

    def gather_mate(slot, block, half):
        rows = pl.ds(pl.multiple_of(half * hrow, 16), hrow)
        return remote(whole.at[block, rows], whole.at[block, rows], gm_send.at[slot], gm_recv.at[slot], mate, z)

    def below(step):
        return lax.rem(z + n.nz - step - 1, n.nz)

    def above(step):
        return lax.rem(z + step + 1, n.nz)

    def gather_pass(step):
        gather_up(step, below(step)).wait_recv()
        if step < far - 1:
            gather_up(step + 1, below(step)).start()
            gather_mate(2 * step, below(step), core).start()
        gather_down(step, above(step)).wait_recv()
        if step < far - 1:
            gather_down(step + 1, above(step)).start()
            gather_mate(2 * step + 1, above(step), core).start()
        else:
            gather_mate(2 * step, above(step), core).start()

    gather_up(0, z).start()
    gather_down(0, z).start()

    def block_to(peer):
        return remote(outgoing.at[peer], arrived.at[dp], b_send.at[peer], b_recv.at[dp], peer, z)

    def block_from(peer):
        return remote(outgoing.at[peer], arrived.at[peer], b_send.at[peer], b_recv.at[peer], peer, z)

    def label_to(peer):
        return remote(label_out.at[peer], label_in.at[dp], l_send.at[peer], l_recv.at[dp], peer, z)

    def label_from(peer):
        return remote(label_out.at[peer], label_in.at[peer], l_send.at[peer], l_recv.at[peer], peer, z)

    def peers(body):
        def step_to(step, carry):
            body(lax.rem(dp + step, n.nd))
            return carry

        lax.fori_loop(1, n.nd, step_to, 0)

    def chips(body):
        def step_to(step, carry):
            body(lax.rem(chip + step, n.chips))
            return carry

        lax.fori_loop(1, n.chips, step_to, 0)

    def send_block(peer):
        label_to(peer).start()
        block_to(peer).start()

    peers(send_block)
    swap_cot = remote(cot_ref, mate_cot, m_send.at[0], m_recv.at[0], mate, z)
    swap_cot.start()
    arrived[dp] = outgoing[dp]
    label_in[dp] = label_out[dp]

    ends = [utt_ref[0, 0]]
    for i in range(1, 3):
        ends.append(ends[-1] + utt_ref[0, i])
    frame_row = padded_place(lane_rows, ends)
    pad_mat = one_hot(lax.broadcasted_iota(jnp.int32, (n.padded, n.rows), 0) == frame_row)
    cot_pad[...] = dot(pad_mat, cot_ref[...]).astype(BF16)
    cot_turned[:, : n.rows] = cot_ref[...].T
    kgrad[...] = jnp.zeros_like(kgrad)
    actp[...] = jnp.zeros_like(actp)
    go[...] = jnp.zeros_like(go)
    gf[:, :HALO, :] = jnp.zeros((n.tiles, HALO, 128), F32)
    gf[:, n.padded - HALO :, :] = jnp.zeros((n.tiles, HALO, 128), F32)
    sub_rows = lax.broadcasted_iota(jnp.int32, (n.rows, 1), 0)
    near = lax.broadcasted_iota(jnp.int32, (n.rows, n.nb), 1) == sub_rows // BLOCK
    code_col = jnp.sum(jnp.where(near, owners, 0).astype(F32), axis=1, keepdims=True)
    code_col = code_col.astype(jnp.int32) * 16 + sub_rows % BLOCK
    order = lax.broadcasted_iota(jnp.int32, (n.rows, lanes), 1)
    for jj in range(4):
        unsort[n.rows * jj : n.rows * (jj + 1)] = one_hot(order == code_col + 4 * jj)
    swap_cot.wait_recv()
    cot_turned[:, n.rows :] = mate_cot[...].T

    if far > 1:
        gather_pass(0)

    peers(lambda peer: label_from(peer).wait_recv())
    lane128 = lax.broadcasted_iota(jnp.int32, (1, 128), 1)
    chunks = []
    for q in range(n.nb // 8):
        row = jnp.zeros((1, 128), F32)
        for s in range(8):
            row = row + jnp.where(lane128 // 16 == s, label_in[8 * q + s], 0.0)
        chunks.append(row)
    slot_row = jnp.concatenate(chunks, axis=1).astype(jnp.int32)
    lane_all = lax.broadcasted_iota(jnp.int32, (1, lanes), 1)
    place_row = padded_place(slot_row * BLOCK + lane_all % 4, ends)

    def lay_label(src, carry):
        labels[pl.ds(pl.multiple_of(16 * src, 16), 16), :] = jnp.broadcast_to(label_in[src], (16, 128))
        return carry

    lax.fori_loop(0, n.nb, lay_label, 0)

    row_iota = lax.broadcasted_iota(jnp.int32, (n.padded, lanes), 0)

    def setter(jj, carry):
        mask = row_iota == jnp.where((lane_all // 4) % 4 == jj, place_row, -1)
        setting[pl.ds(pl.multiple_of(jj * n.padded, 16), n.padded), :] = one_hot(mask)
        return carry

    lax.fori_loop(0, 4, setter, 0)

    def taker(chunk, carry):
        at = pl.ds(pl.multiple_of(chunk * chunk_rows, chunk_rows), chunk_rows)
        slot = labels[at, :][:, :1].astype(jnp.int32)
        sub = lax.broadcasted_iota(jnp.int32, (chunk_rows, 1), 0)
        place = padded_place(slot * BLOCK + sub % 4, ends)
        cols = lax.broadcasted_iota(jnp.int32, (chunk_rows, n.padded), 1)
        for jj in range(4):
            taking[jj, at, :] = one_hot(cols == jnp.where((sub // 4) % 4 == jj, place, -1))
        return carry

    lax.fori_loop(0, lanes // chunk_rows, taker, 0)

    if far > 2:
        gather_pass(1)

    peers(lambda peer: block_from(peer).wait_recv())
    blocks = jnp.concatenate(
        [arrived[:, 16 * g : 16 * (g + 1), :].reshape(lanes, 128) for g in range(n.groups)], axis=1
    )

    def put(jj, carry):
        owned = dot(setting[pl.ds(pl.multiple_of(jj * n.padded, 16), n.padded), :], blocks)
        for g in range(n.groups):
            xs[4 * g + jj] = owned[:, 128 * g : 128 * (g + 1)]
        return carry

    lax.fori_loop(0, 4, put, 0)

    for step in range(2, far - 1):
        gather_pass(step)

    def filter_tile(j, carry):
        taps = taps_ref[:, pl.ds(pl.multiple_of(j * 128, 128), 128)]
        for b in spans:
            base = 1 + n.span * b
            total = jnp.zeros((n.span, 128), F32)
            for s in range(8):
                window = xs[j, base + s : base + s + n.span + 24, :]
                for m in range(4):
                    k = s + 8 * m
                    if k < TAPS:
                        total = total + taps[k : k + 1] * window[8 * m : 8 * m + n.span]
            filt[j, HALO + n.span * b : HALO + n.span * (b + 1), :] = total
        return carry

    lax.fori_loop(0, n.tiles, filter_tile, 0)
    gather_pass(far - 1)

    def norm_span(b, carry):
        rows = pl.ds(pl.multiple_of(HALO + n.span * b, 16), n.span)
        total = filt[0, rows, :]
        for j in range(1, n.tiles):
            total = total + filt[j, rows, :]
        mean = jnp.sum(total, axis=1, keepdims=True) * (1.0 / n.ch)
        square = jnp.zeros((n.span, 128), F32)
        for j in range(n.tiles):
            centred = filt[j, rows, :] - mean
            square = square + centred * centred
        variance = jnp.sum(square, axis=1, keepdims=True) * (1.0 / n.ch)
        inverse = 1.0 / jnp.sqrt(variance + EPSILON)
        spread[rows, :] = jnp.broadcast_to(inverse, (n.span, 128))
        for j in range(n.tiles):
            whitened = (filt[j, rows, :] - mean) * inverse
            normed = whitened * gain_ref[128 * j : 128 * (j + 1)].reshape(1, 128) + shift_ref[128 * j : 128 * (j + 1)].reshape(1, 128)
            logistic = 1.0 / (1.0 + jnp.exp(-normed))
            activated = normed * logistic
            actp[rows, 128 * j : 128 * (j + 1)] = activated.astype(BF16)
            filt[j, rows, :] = whitened
            slope[j, rows, :] = logistic * (1.0 + normed * (1.0 - logistic))
        return carry

    lax.fori_loop(0, n.used // n.span, norm_span, 0)

    frame_col = padded_place(lax.broadcasted_iota(jnp.int32, (n.rows, 1), 0), ends)
    take = one_hot(lax.broadcasted_iota(jnp.int32, (n.rows, n.padded), 1) == frame_col)
    act_send[...] = dot(take, actp[:, theirs]).astype(BF16)
    swap_act = remote(act_send, act_both.at[pl.ds(n.rows, n.rows)], m_send.at[1], m_recv.at[1], mate, z)
    swap_act.start()
    act_both[: n.rows] = dot(take, actp[:, mine]).astype(BF16)

    for step in range(far):
        gather_mate(2 * step, below(step) if step < far - 1 else above(step), other).wait_recv()
        if step < far - 1:
            gather_mate(2 * step + 1, above(step), other).wait_recv()
    width = 512
    per = width // 128

    def project(i, carry):
        cols = pl.ds(pl.multiple_of(i * width, width), width)
        piece = dot(cot_pad[...], whole[:, :, cols].reshape(n.ch, width))
        for q in range(per):
            hidden[per * i + q] = piece[:, 128 * q : 128 * (q + 1)]
        return carry

    lax.fori_loop(0, n.ch // width, project, 0)

    swap_act.wait_recv()

    def product(target):
        part[target] = dot(cot_turned[pl.ds(pl.multiple_of(target * n.shard, 16), n.shard), :], act_both[...])

    chunk_of = [slice(0, n.quarter), slice(n.quarter, n.half)]

    def ring_hop(way, chunk, step):
        out, into, send, recv, to = (
            (up_out, up_in, u_send, u_recv, up) if way == 0 else (down_out, down_in, d_send, d_recv, down)
        )
        at = far * chunk + step
        return remote(out.at[chunk, step], into.at[chunk, step], send.at[at], recv.at[at], dp, to)

    def ring_target(way, chunk, step):
        ahead = (far if way == chunk else far - 1) - step
        return lax.rem(z + ahead, n.nz) if way == 0 else lax.rem(z + n.nz - ahead, n.nz)

    def ring_steps(way, chunk):
        return far if way == chunk else far - 1

    def ring_step(step):
        for way, chunk in ((0, 0), (1, 1), (0, 1), (1, 0)):
            if step < ring_steps(way, chunk):
                out, into = (up_out, up_in) if way == 0 else (down_out, down_in)
                value = part[ring_target(way, chunk, step), :, chunk_of[chunk]]
                if step > 0:
                    ring_hop(way, chunk, step - 1).wait_recv()
                    value = value + into[chunk, step - 1].astype(F32)
                out[chunk, step] = value.astype(BF16)
                ring_hop(way, chunk, step).start()

    product(lax.rem(z + far, n.nz))
    if far > 1:
        product(lax.rem(z + far - 1, n.nz))
        product(lax.rem(z + n.nz - far + 1, n.nz))
    ring_step(0)

    def norm_back(b, carry):
        rows = pl.ds(pl.multiple_of(HALO + n.span * b, 16), n.span)
        first = jnp.zeros((n.span, 128), F32)
        second = jnp.zeros((n.span, 128), F32)
        for j in range(n.tiles):
            whitened = filt[j, rows, :]
            grad_normed = hidden[j, rows, :] * slope[j, rows, :]
            scaled = grad_normed * gain_ref[128 * j : 128 * (j + 1)].reshape(1, 128)
            hidden[j, rows, :] = scaled
            first = first + scaled
            second = second + scaled * whitened
            half, at = j // n.ltiles, (j % n.ltiles) * KROWS
            kgrad[half, at + TAPS : at + TAPS + 1, :] += jnp.sum(grad_normed * whitened, axis=0, keepdims=True)
            kgrad[half, at + TAPS + 1 : at + TAPS + 2, :] += jnp.sum(grad_normed, axis=0, keepdims=True)
        mean1 = jnp.sum(first, axis=1, keepdims=True) * (1.0 / n.ch)
        mean2 = jnp.sum(second, axis=1, keepdims=True) * (1.0 / n.ch)
        inverse = spread[rows, :]
        for j in range(n.tiles):
            gf[j, rows, :] = inverse * (hidden[j, rows, :] - mean1 - filt[j, rows, :] * mean2)
        return carry

    lax.fori_loop(0, n.used // n.span, norm_back, 0)

    def products(i, carry):
        product(lax.rem(z + n.nz - far + 2 + i, n.nz))
        return carry

    if far > 1:
        lax.fori_loop(0, n.nz - 3, products, 0)
    else:
        product(z)

    def back_tile(j, carry):
        taps = taps_ref[:, pl.ds(pl.multiple_of(j * 128, 128), 128)]
        for b in spans:
            base = 1 + n.span * b
            here = slice(HALO + n.span * b, HALO + n.span * (b + 1))
            signal = xs[j, here, :]
            total = jnp.zeros((n.span, 128), F32)
            for s in range(8):
                window = gf[j, base + s : base + s + n.span + 24, :]
                for m in range(4):
                    k = TAPS - 1 - s - 8 * m
                    if k >= 0:
                        shifted = window[8 * m : 8 * m + n.span]
                        total = total + taps[k : k + 1] * shifted
                        product = jnp.sum((shifted * signal).reshape(n.span // 8, 8, 128), axis=0)
                        if b == 0:
                            k8[k] = product
                        else:
                            k8[k] += product
            go[j, here, :] = total.astype(BF16)
        at = pl.multiple_of(lax.rem(j, n.ltiles) * KROWS, 8)
        kgrad[j // n.ltiles, pl.ds(at, TAPS), :] = jnp.sum(k8[...], axis=1)
        return carry

    third = n.tiles // 3
    lax.fori_loop(0, third, back_tile, 0)
    if far > 1:
        ring_step(1)
    lax.fori_loop(third, n.tiles, back_tile, 0)
    swap_k = remote(kgrad.at[other], mate_k, m_send.at[2], m_recv.at[2], mate, z)
    swap_k.start()
    if far > 2:
        ring_step(2)

    def gather_chunk(chunk, carry):
        at = pl.ds(pl.multiple_of(chunk * chunk_rows, chunk_rows), chunk_rows)
        total = None
        for jj in range(4):
            rhs = jnp.concatenate([go[4 * g + jj] for g in range(n.groups)], axis=1)
            piece = dot(taking[jj, at, :], rhs)
            total = piece if total is None else total + piece
        for g in range(n.groups):
            piece = total[:, 128 * g : 128 * (g + 1)].astype(BF16).reshape(per_chunk, 16, 128)
            back[pl.ds(chunk * per_chunk, per_chunk), 16 * g : 16 * (g + 1), :] = piece
        return carry

    lax.fori_loop(0, lanes // chunk_rows, gather_chunk, 0)

    def home_to(peer):
        return remote(back.at[peer], home.at[dp], h_send.at[peer], h_recv.at[dp], peer, z)

    def home_from(peer):
        return remote(back.at[peer], home.at[peer], h_send.at[peer], h_recv.at[peer], peer, z)

    peers(lambda peer: home_to(peer).start())
    home[dp] = back[dp]

    swap_k.wait_recv()
    mate_k[...] += kgrad[core]

    def k_rows(at):
        return pl.ds(pl.multiple_of(at * n.krow, 8), n.krow)

    def k_scatter(at, slot):
        return remote(mate_k.at[k_rows(at)], k_in.at[slot], ka_send.at[at], ka_recv.at[slot], 2 * at + core, z)

    def k_over_z(slot, to):
        return remote(k_z.at[z], k_z.at[slot], kz_send.at[to], kz_recv.at[slot], dp, to)

    def k_gather(slot, to):
        return remote(k_all.at[slot], k_all.at[slot], kc_send.at[to], kc_recv.at[slot], 2 * to + core, z)

    chips(lambda at: k_scatter(at, chip).start())

    for step in range(3, far):
        ring_step(step)

    chips(lambda at: k_scatter(chip, at).wait_recv())
    k_in[chip] = mate_k[k_rows(chip), :]

    def k_sum(step, carry):
        return carry + k_in[lax.rem(chip + step, n.chips)]

    k_z[z] = lax.fori_loop(1, n.chips, k_sum, k_in[chip])
    for hop in range(1, n.nz):
        k_over_z(z, lax.rem(z + hop, n.nz)).start()

    for way, chunk in ((1, 0), (0, 1), (0, 0), (1, 1)):
        steps = ring_steps(way, chunk)
        if steps > 0:
            into = up_in if way == 0 else down_in
            ring_hop(way, chunk, steps - 1).wait_recv()
            part[z, :, chunk_of[chunk]] += into[chunk, steps - 1].astype(F32)

    def along_x(step):
        there = lax.rem(cx + step, n.nx)
        return there, (there * n.ny + cy) * 2 + core

    def along_y(step):
        there = lax.rem(cy + step, n.ny)
        return there, (cx * n.ny + there) * 2 + core

    def x_scatter(step, arriving):
        there, peer = along_x(step)
        slot = there if arriving else cx
        return remote(x_out.at[there], x_in.at[slot], xr_send.at[there], xr_recv.at[slot], peer, z)

    def y_scatter(step, arriving):
        there, peer = along_y(step)
        slot = there if arriving else cy
        return there, remote(y_out.at[there], y_in.at[slot], yr_send.at[there], yr_recv.at[slot], peer, z)

    def y_gather(step, arriving):
        there, peer = along_y(step)
        slot = there if arriving else cy
        return there, remote(y_all.at[slot], y_all.at[slot], yg_send.at[there], yg_recv.at[slot], peer, z)

    def x_gather(step, arriving):
        there, peer = along_x(step)
        slot = there if arriving else cx
        return remote(x_all.at[slot], x_all.at[slot], xg_send.at[there], xg_recv.at[slot], peer, z)

    for i in range(n.nx):
        x_out[i] = part[z, n.prow * i : n.prow * (i + 1), :].astype(BF16)
    for step in range(1, n.nx):
        x_scatter(step, False).start()

    for hop in range(1, n.nz):
        src = lax.rem(z + hop, n.nz)
        k_over_z(src, src).wait_recv()
    small = k_z[0]
    for i in range(1, n.nz):
        small = small + k_z[i]
    k_all[chip] = small * scale
    chips(lambda at: k_gather(chip, at).start())

    band = part[z, pl.ds(pl.multiple_of(cx * n.prow, 16), n.prow), :]
    for step in range(1, n.nx):
        x_scatter(step, True).wait_recv()
        band = band + x_in[lax.rem(cx + step, n.nx)].astype(F32)
    for l in range(n.ltiles):
        y_own[l] = band[:, 128 * l : 128 * (l + 1)]
        y_out[l] = band[:, 128 * l : 128 * (l + 1)].astype(BF16)
    for step in range(1, n.ny):
        there, copy = y_scatter(step, False)

        @pl.when(there < n.ltiles)
        def _():
            copy.start()

    @pl.when(cy < n.ltiles)
    def _():
        total = y_own[cy]
        for step in range(1, n.ny):
            there, copy = y_scatter(step, True)
            copy.wait_recv()
            total = total + y_in[there].astype(F32)
        y_all[cy] = (total * scale).astype(BF16)
        for step in range(1, n.ny):
            y_gather(step, False)[1].start()

    for step in range(1, n.ny):
        there, copy = y_gather(step, True)

        @pl.when(there < n.ltiles)
        def _():
            copy.wait_recv()

    for l in range(n.ltiles):
        x_all[cx, :, 128 * l : 128 * (l + 1)] = y_all[l]
    for step in range(1, n.nx):
        x_gather(step, False).start()

    chips(lambda at: k_gather(at, at).wait_recv())
    swap_all = remote(k_all, k_mate, m_send.at[3], m_recv.at[3], mate, z)
    swap_all.start()

    peers(lambda peer: home_from(peer).wait_recv())
    blocks = jnp.concatenate(
        [home[:, 16 * g : 16 * (g + 1), :].reshape(lanes, 128) for g in range(n.groups)], axis=1
    )
    for jj in range(4):
        rows = dot(unsort[n.rows * jj : n.rows * (jj + 1)], blocks).astype(BF16)
        for g in range(n.groups):
            frames_out[:, 128 * (4 * g + jj) : 128 * (4 * g + jj + 1)] = rows[:, 128 * g : 128 * (g + 1)]

    for step in range(1, n.nx):
        x_gather(step, True).wait_recv()
    swap_weight = remote(x_all, x_mate, m_send.at[4], m_recv.at[4], mate, z)
    swap_weight.start()

    def lay_weight(source, half):
        cols = pl.ds(pl.multiple_of(half * n.half, 128), n.half)
        for i in range(n.nx):
            weight_out[n.prow * i : n.prow * (i + 1), cols] = source[i]

    def lay_small(source, half):
        rows = source[...].reshape(n.kall, 128)
        for l in range(n.ltiles):
            cols = pl.ds(pl.multiple_of(half * n.half + 128 * l, 128), 128)
            taps_out[:, cols] = rows[KROWS * l : KROWS * l + TAPS]
            gain_out[cols] = rows[KROWS * l + TAPS : KROWS * l + TAPS + 1].reshape(128)
            shift_out[cols] = rows[KROWS * l + TAPS + 1 : KROWS * l + TAPS + 2].reshape(128)

    lay_weight(x_all, core)
    lay_small(k_all, core)

    swap_all.wait_recv()
    lay_small(k_mate, other)
    swap_weight.wait_recv()
    lay_weight(x_mate, other)

    for copy in (swap_cot, swap_act, swap_k, swap_all, swap_weight):
        copy.wait_send()
    for step in range(far):
        gather_up(step, z).wait_send()
        gather_down(step, z).wait_send()
        gather_mate(2 * step, z, core).wait_send()
        if step < far - 1:
            gather_mate(2 * step + 1, z, core).wait_send()
    for way in range(2):
        for chunk in range(2):
            for step in range(ring_steps(way, chunk)):
                ring_hop(way, chunk, step).wait_send()
    for step in range(1, n.nx):
        x_scatter(step, False).wait_send()
        x_gather(step, False).wait_send()
    for step in range(1, n.ny):
        there, copy = y_scatter(step, False)

        @pl.when(there < n.ltiles)
        def _():
            copy.wait_send()

    @pl.when(cy < n.ltiles)
    def _():
        for step in range(1, n.ny):
            y_gather(step, False)[1].wait_send()

    for hop in range(1, n.nz):
        k_over_z(z, lax.rem(z + hop, n.nz)).wait_send()

    def small_sent(at):
        k_scatter(at, chip).wait_send()
        k_gather(chip, at).wait_send()

    chips(small_sent)

    def blocks_sent(peer):
        label_to(peer).wait_send()
        block_to(peer).wait_send()
        home_to(peer).wait_send()

    peers(blocks_sent)


def on_device(frames, destination, utt_lengths, cotangent, weight, kernel, norm_gain, norm_shift):
    n = Sizes(lax.axis_size("dp"), lax.axis_size("fsdp"), frames.shape[0], frames.shape[1], weight.shape[0])
    scale = 1.0 / math.sqrt(n.rows * n.nd * n.nz)
    far = n.nz // 2
    lanes = 16 * n.nb
    vmem = pl.BlockSpec(memory_space=pltpu.VMEM)
    smem = pl.BlockSpec(memory_space=pltpu.SMEM)

    def dma(count):
        return [pltpu.SemaphoreType.DMA((count,))] * 2

    def buf(*shape, dtype=F32):
        return pltpu.VMEM(shape, dtype)

    blocks = buf(n.nb, n.slab, 128, dtype=BF16)
    label = buf(n.nd, 1, 128)
    plane = buf(n.tiles, n.padded, 128)
    ring = buf(2, far, n.shard, n.quarter, dtype=BF16)
    band = buf(n.nx, n.prow, n.half, dtype=BF16)
    tile = buf(n.ny, n.prow, 128, dtype=BF16)
    small = buf(n.chips, n.krow, 128)
    grads = pl.pallas_call(
        functools.partial(module_kernel, n, scale),
        out_shape=(
            jax.ShapeDtypeStruct((n.rows, n.ch), BF16),
            jax.ShapeDtypeStruct((n.shard, n.ch), BF16),
            jax.ShapeDtypeStruct((TAPS, n.ch), F32),
            jax.ShapeDtypeStruct((n.ch,), F32),
            jax.ShapeDtypeStruct((n.ch,), F32),
        ),
        in_specs=[vmem, smem] + [vmem] * 6,
        out_specs=(vmem,) * 5,
        scratch_shapes=[
            blocks, blocks, label, label, buf(16 * n.nb, 128), buf(n.nz, n.shard, n.ch, dtype=BF16),
            buf(4 * n.rows, lanes, dtype=BF16), buf(4 * n.padded, lanes, dtype=BF16), buf(4, lanes, n.padded, dtype=BF16),
            plane, plane, plane, plane, plane, buf(n.padded, 128), buf(n.padded, n.ch, dtype=BF16),
            buf(n.tiles, n.padded, 128, dtype=BF16), buf(TAPS, 8, 128), buf(2, n.kall, 128),
            buf(n.padded, n.ch, dtype=BF16), buf(n.ch, 2 * n.rows, dtype=BF16), buf(n.rows, n.ch, dtype=BF16),
            buf(2 * n.rows, n.half, dtype=BF16), buf(n.rows, n.half, dtype=BF16),
            buf(n.nz, n.shard, n.half), ring, ring, ring, ring, blocks, blocks,
            band, band, buf(n.ltiles, n.prow, 128), tile, tile, tile, band, band,
            buf(n.kall, 128), small, buf(n.nz, n.krow, 128), small, small,
            *dma(n.nd), *dma(n.nd), *dma(n.nd),
            *dma(far), *dma(far), *dma(2 * far), *dma(5),
            *dma(2 * far), *dma(2 * far),
            *dma(n.nx), *dma(n.ny), *dma(n.ny), *dma(n.nx),
            *dma(n.chips), *dma(n.nz), *dma(n.chips),
        ],
        compiler_params=pltpu.CompilerParams(
            collective_id=0, has_side_effects=True, vmem_limit_bytes=VMEM_BYTES
        ),
    )(destination, utt_lengths, frames, cotangent, weight, kernel, norm_gain, norm_shift)
    return grads[0], grads[1].astype(F32), grads[2], grads[3], grads[4]


def solution(mesh):
    placed = (
        P(("dp", "fsdp"), None),
        P(("dp", "fsdp")),
        P(("dp", "fsdp"), None),
        P(("dp", "fsdp"), None),
        P("fsdp", None),
        P(),
        P(),
        P(),
    )
    return jax.shard_map(
        on_device,
        mesh=mesh,
        in_specs=placed,
        out_specs=(P(("dp", "fsdp"), None), P("fsdp", None), P(), P(), P()),
        check_vma=False,
    )
```

```python
import functools
import math

import jax
import jax.numpy as jnp
from jax import lax
from jax.experimental import pallas as pl
from jax.experimental.pallas import tpu as pltpu
from jax.sharding import PartitionSpec as P

EPSILON = 1e-05
MESH = pl.DeviceIdType.MESH
F32 = jnp.float32
BF16 = jnp.bfloat16
BLOCK = 4
TAPS = 31
HALO = 16
KROWS = 40
VMEM_BYTES = 56 * 1024 * 1024


class Sizes:
    def __init__(self, dp_size, fsdp_size, rows, channels, shard):
        self.nd = dp_size
        self.nz = fsdp_size
        self.rows = rows
        self.ch = channels
        self.shard = shard
        self.nb = rows // BLOCK
        self.tiles = channels // 128
        self.groups = self.tiles // 4
        self.slab = 4 * self.tiles
        self.chips = dp_size // 2
        self.half = channels // 2
        self.ltiles = self.half // 128
        self.quarter = self.half // 2
        self.nx = 4 if self.chips >= 32 else 2
        self.ny = self.chips // self.nx
        self.prow = shard // self.nx
        self.used = rows + 4 * HALO
        self.padded = self.used + 2 * HALO
        self.span = 80 if self.used % 80 == 0 else 48
        self.krow = 8 * (-(-(5 * self.ltiles) // self.chips))
        self.kall = self.krow * self.chips


def one_hot(mask):
    return jnp.where(mask, 1.0, 0.0).astype(BF16)


def dot(a, b):
    return jnp.dot(a, b, preferred_element_type=F32)


def remote(src, dst, send, recv, dp, z):
    return pltpu.make_async_remote_copy(
        src_ref=src, dst_ref=dst, send_sem=send, recv_sem=recv, device_id=(dp, z), device_id_type=MESH
    )


def await_bytes(ref, count, sem):
    part = ref.at[pl.ds(0, count)]
    pltpu.make_async_copy(part, part, sem).wait()


def padded_place(frame, ends):
    place = frame + HALO
    for end in ends:
        place = place + jnp.where(frame >= end, HALO, 0)
    return place


def module_kernel(
    n, scale,
    dest_ref, utt_ref, frames_hbm, cot_hbm, weight_hbm, taps_ref, gain_ref, shift_ref,
    frames_out, weight_out, taps_out, gain_out, shift_out,
    frames_ref, cot_ref,
    outgoing, arrived, label_out, label_in, labels, whole, unsort, setting, taking,
    xs, filt, hidden, gf, slope, spread, actp, go, k8, kgrad, cot_pad, cot_turned, mate_cot, act_both, act_send,
    part, up_out, up_in, down_out, down_in, back, home,
    x_out, x_in, y_own, y_out, y_in, y_all, x_all, x_mate, mate_k, k_in, k_z, k_all, k_mate,
    io, b_send, b_recv, l_send, l_recv, h_send, h_recv,
    gu_send, gu_recv, gd_send, gd_recv, gm_send, gm_recv, m_send, m_recv,
    u_send, u_recv, d_send, d_recv,
    xr_send, xr_recv, yr_send, yr_recv, yg_send, yg_recv, xg_send, xg_recv,
    ka_send, ka_recv, kz_send, kz_recv, kc_send, kc_recv,
):
    dp = lax.axis_index("dp")
    z = lax.axis_index("fsdp")
    core = lax.rem(dp, 2)
    other = 1 - core
    mate = dp + 1 - 2 * core
    chip = dp // 2
    cx = chip // n.ny
    cy = lax.rem(chip, n.ny)
    far = n.nz // 2
    up = lax.rem(z + 1, n.nz)
    down = lax.rem(z + n.nz - 1, n.nz)
    hrow = n.shard // 2
    lanes = 16 * n.nb
    spans = range(n.used // n.span)
    mine = pl.ds(pl.multiple_of(core * n.half, 128), n.half)
    theirs = pl.ds(pl.multiple_of(other * n.half, 128), n.half)

    loads = [
        pltpu.make_async_copy(frames_hbm, frames_ref, io.at[0]),
        pltpu.make_async_copy(weight_hbm, whole.at[z], io.at[1]),
        pltpu.make_async_copy(cot_hbm, cot_ref, io.at[2]),
    ]
    for load in loads:
        load.start()

    barrier = pltpu.get_barrier_semaphore()

    def along_dp(step, carry):
        pl.semaphore_signal(
            barrier, inc=1, device_id=(lax.rem(dp + step, n.nd), z), device_id_type=MESH
        )
        return carry

    lax.fori_loop(1, n.nd, along_dp, 0)
    for step in range(1, n.nz):
        pl.semaphore_signal(
            barrier, inc=1, device_id=(dp, lax.rem(z + step, n.nz)), device_id_type=MESH
        )

    lane_rows = lax.broadcasted_iota(jnp.int32, (1, n.rows), 1)
    dest = dest_ref[...].reshape(1, n.nb)
    owners = dest // n.nb
    slots = dest - owners * n.nb
    owner_iota = lax.broadcasted_iota(jnp.int32, (n.nd, n.nb), 0)
    slot_of = jnp.sum(jnp.where(owner_iota == owners, slots, 0).astype(F32), axis=1, keepdims=True)
    slot_of = jnp.broadcast_to(slot_of, (n.nd, 128))
    for i in range(n.nd):
        label_out[i] = slot_of[i : i + 1]
    four = one_hot(
        lax.broadcasted_iota(jnp.int32, (n.nb, n.rows), 0)
        == lax.broadcasted_iota(jnp.int32, (n.nb, n.rows), 1) // BLOCK
    )
    wide = dot(jnp.broadcast_to(owners.astype(F32), (16, n.nb)).astype(BF16), four)[:1]
    code = wide.astype(jnp.int32) * 16 + lane_rows % BLOCK

    loads[0].wait()
    mats = [
        jnp.concatenate(
            [frames_ref[:, 128 * (4 * g + jj) : 128 * (4 * g + jj + 1)] for g in range(n.groups)], axis=1
        )
        for jj in range(4)
    ]
    chunk_rows = min(256, lanes)
    per_chunk = chunk_rows // 16

    def sort_chunk(chunk, carry):
        place = lax.broadcasted_iota(jnp.int32, (chunk_rows, n.rows), 0) + chunk * chunk_rows
        total = dot(one_hot(place == code), mats[0])
        for jj in range(1, 4):
            total = total + dot(one_hot(place == code + 4 * jj), mats[jj])
        for g in range(n.groups):
            piece = total[:, 128 * g : 128 * (g + 1)].astype(BF16).reshape(per_chunk, 16, 128)
            outgoing[pl.ds(chunk * per_chunk, per_chunk), 16 * g : 16 * (g + 1), :] = piece
        return carry

    lax.fori_loop(0, lanes // chunk_rows, sort_chunk, 0)

    loads[1].wait()
    pl.semaphore_wait(barrier, n.nd - 1 + n.nz - 1)

    def gather_hop(step, block, first, count, to, send, recv):
        rows = pl.ds(pl.multiple_of(core * hrow + first, 16), count)
        return remote(whole.at[block, rows], whole.at[block, rows], send.at[step], recv.at[step], dp, to)

    def gather_up(step, block):
        last = step == far - 1
        return gather_hop(step, block, 0, hrow // 2 if last else hrow, up, gu_send, gu_recv)

    def gather_down(step, block):
        last = step == far - 1
        return gather_hop(step, block, hrow // 2 if last else 0, hrow // 2 if last else hrow, down, gd_send, gd_recv)

    def gather_mate(block, half):
        rows = pl.ds(pl.multiple_of(half * hrow, 16), hrow)
        return remote(whole.at[block, rows], whole.at[block, rows], gm_send.at[0], gm_recv.at[0], mate, z)

    def below(step):
        return lax.rem(z + n.nz - step - 1, n.nz)

    def above(step):
        return lax.rem(z + step + 1, n.nz)

    def gather_pass(step):
        gather_up(step, below(step)).wait_recv()
        if step < far - 1:
            gather_up(step + 1, below(step)).start()
            gather_mate(below(step), core).start()
        gather_down(step, above(step)).wait_recv()
        if step < far - 1:
            gather_down(step + 1, above(step)).start()
            gather_mate(above(step), core).start()
        else:
            gather_mate(above(step), core).start()

    gather_up(0, z).start()
    gather_down(0, z).start()

    def block_to(peer):
        return remote(outgoing.at[peer], arrived.at[dp], b_send.at[0], b_recv.at[0], peer, z)

    def label_to(peer):
        return remote(label_out.at[peer], label_in.at[dp], l_send.at[0], l_recv.at[0], peer, z)

    def peers(body):
        def step_to(step, carry):
            body(lax.rem(dp + step, n.nd))
            return carry

        lax.fori_loop(1, n.nd, step_to, 0)

    def chips(body):
        def step_to(step, carry):
            body(lax.rem(chip + step, n.chips))
            return carry

        lax.fori_loop(1, n.chips, step_to, 0)

    def send_block(peer):
        label_to(peer).start()
        block_to(peer).start()

    peers(send_block)
    loads[2].wait()
    swap_cot = remote(cot_ref, mate_cot, m_send.at[0], m_recv.at[0], mate, z)
    swap_cot.start()
    arrived[dp] = outgoing[dp]
    label_in[dp] = label_out[dp]

    ends = [utt_ref[0, 0]]
    for i in range(1, 3):
        ends.append(ends[-1] + utt_ref[0, i])
    frame_row = padded_place(lane_rows, ends)
    pad_mat = one_hot(lax.broadcasted_iota(jnp.int32, (n.padded, n.rows), 0) == frame_row)
    cot_pad[...] = dot(pad_mat, cot_ref[...]).astype(BF16)
    cot_turned[:, : n.rows] = cot_ref[...].T
    kgrad[...] = jnp.zeros_like(kgrad)
    actp[...] = jnp.zeros_like(actp)
    go[...] = jnp.zeros_like(go)
    gf[:, :HALO, :] = jnp.zeros((n.tiles, HALO, 128), F32)
    gf[:, n.padded - HALO :, :] = jnp.zeros((n.tiles, HALO, 128), F32)
    sub_rows = lax.broadcasted_iota(jnp.int32, (n.rows, 1), 0)
    near = lax.broadcasted_iota(jnp.int32, (n.rows, n.nb), 1) == sub_rows // BLOCK
    code_col = jnp.sum(jnp.where(near, owners, 0).astype(F32), axis=1, keepdims=True)
    code_col = code_col.astype(jnp.int32) * 16 + sub_rows % BLOCK
    order = lax.broadcasted_iota(jnp.int32, (n.rows, lanes), 1)
    for jj in range(4):
        unsort[n.rows * jj : n.rows * (jj + 1)] = one_hot(order == code_col + 4 * jj)
    swap_cot.wait_recv()
    cot_turned[:, n.rows :] = mate_cot[...].T

    if far > 1:
        gather_pass(0)

    await_bytes(label_in, n.nd - 1, l_recv.at[0])
    lane128 = lax.broadcasted_iota(jnp.int32, (1, 128), 1)
    chunks = []
    for q in range(n.nb // 8):
        row = jnp.zeros((1, 128), F32)
        for s in range(8):
            row = row + jnp.where(lane128 // 16 == s, label_in[8 * q + s], 0.0)
        chunks.append(row)
    slot_row = jnp.concatenate(chunks, axis=1).astype(jnp.int32)
    lane_all = lax.broadcasted_iota(jnp.int32, (1, lanes), 1)
    place_row = padded_place(slot_row * BLOCK + lane_all % 4, ends)

    def lay_label(src, carry):
        labels[pl.ds(pl.multiple_of(16 * src, 16), 16), :] = jnp.broadcast_to(label_in[src], (16, 128))
        return carry

    lax.fori_loop(0, n.nb, lay_label, 0)

    row_iota = lax.broadcasted_iota(jnp.int32, (n.padded, lanes), 0)

    def setter(jj, carry):
        mask = row_iota == jnp.where((lane_all // 4) % 4 == jj, place_row, -1)
        setting[pl.ds(pl.multiple_of(jj * n.padded, 16), n.padded), :] = one_hot(mask)
        return carry

    lax.fori_loop(0, 4, setter, 0)

    def taker(chunk, carry):
        at = pl.ds(pl.multiple_of(chunk * chunk_rows, chunk_rows), chunk_rows)
        slot = labels[at, :][:, :1].astype(jnp.int32)
        sub = lax.broadcasted_iota(jnp.int32, (chunk_rows, 1), 0)
        place = padded_place(slot * BLOCK + sub % 4, ends)
        cols = lax.broadcasted_iota(jnp.int32, (chunk_rows, n.padded), 1)
        for jj in range(4):
            taking[jj, at, :] = one_hot(cols == jnp.where((sub // 4) % 4 == jj, place, -1))
        return carry

    lax.fori_loop(0, lanes // chunk_rows, taker, 0)

    if far > 2:
        gather_pass(1)

    await_bytes(arrived, n.nd - 1, b_recv.at[0])
    blocks = jnp.concatenate(
        [arrived[:, 16 * g : 16 * (g + 1), :].reshape(lanes, 128) for g in range(n.groups)], axis=1
    )

    def put(jj, carry):
        owned = dot(setting[pl.ds(pl.multiple_of(jj * n.padded, 16), n.padded), :], blocks)
        for g in range(n.groups):
            xs[4 * g + jj] = owned[:, 128 * g : 128 * (g + 1)]
        return carry

    lax.fori_loop(0, 4, put, 0)

    for step in range(2, far - 1):
        gather_pass(step)

    def filter_tile(j, carry):
        taps = taps_ref[:, pl.ds(pl.multiple_of(j * 128, 128), 128)]
        for b in spans:
            base = 1 + n.span * b
            total = jnp.zeros((n.span, 128), F32)
            for s in range(8):
                window = xs[j, base + s : base + s + n.span + 24, :]
                for m in range(4):
                    k = s + 8 * m
                    if k < TAPS:
                        total = total + taps[k : k + 1] * window[8 * m : 8 * m + n.span]
            filt[j, HALO + n.span * b : HALO + n.span * (b + 1), :] = total
        return carry

    lax.fori_loop(0, n.tiles, filter_tile, 0)
    gather_pass(far - 1)

    def norm_span(b, carry):
        rows = pl.ds(pl.multiple_of(HALO + n.span * b, 16), n.span)
        total = filt[0, rows, :]
        for j in range(1, n.tiles):
            total = total + filt[j, rows, :]
        mean = jnp.sum(total, axis=1, keepdims=True) * (1.0 / n.ch)
        square = jnp.zeros((n.span, 128), F32)
        for j in range(n.tiles):
            centred = filt[j, rows, :] - mean
            square = square + centred * centred
        variance = jnp.sum(square, axis=1, keepdims=True) * (1.0 / n.ch)
        inverse = 1.0 / jnp.sqrt(variance + EPSILON)
        spread[rows, :] = jnp.broadcast_to(inverse, (n.span, 128))
        for j in range(n.tiles):
            whitened = (filt[j, rows, :] - mean) * inverse
            normed = whitened * gain_ref[128 * j : 128 * (j + 1)].reshape(1, 128) + shift_ref[128 * j : 128 * (j + 1)].reshape(1, 128)
            logistic = 1.0 / (1.0 + jnp.exp(-normed))
            activated = normed * logistic
            actp[rows, 128 * j : 128 * (j + 1)] = activated.astype(BF16)
            filt[j, rows, :] = whitened
            slope[j, rows, :] = logistic * (1.0 + normed * (1.0 - logistic))
        return carry

    lax.fori_loop(0, n.used // n.span, norm_span, 0)

    frame_col = padded_place(lax.broadcasted_iota(jnp.int32, (n.rows, 1), 0), ends)
    take = one_hot(lax.broadcasted_iota(jnp.int32, (n.rows, n.padded), 1) == frame_col)
    act_send[...] = dot(take, actp[:, theirs]).astype(BF16)
    swap_act = remote(act_send, act_both.at[pl.ds(n.rows, n.rows)], m_send.at[1], m_recv.at[1], mate, z)
    swap_act.start()
    act_both[: n.rows] = dot(take, actp[:, mine]).astype(BF16)

    await_bytes(whole.at[:, pl.ds(0, hrow)], n.nz - 1, gm_recv.at[0])
    width = 512
    per = width // 128

    def project(i, carry):
        cols = pl.ds(pl.multiple_of(i * width, width), width)
        piece = dot(cot_pad[...], whole[:, :, cols].reshape(n.ch, width))
        for q in range(per):
            hidden[per * i + q] = piece[:, 128 * q : 128 * (q + 1)]
        return carry

    lax.fori_loop(0, n.ch // width, project, 0)

    swap_act.wait_recv()

    def product(target):
        part[target] = dot(cot_turned[pl.ds(pl.multiple_of(target * n.shard, 16), n.shard), :], act_both[...])

    chunk_of = [slice(0, n.quarter), slice(n.quarter, n.half)]

    def ring_hop(way, chunk, step):
        out, into, send, recv, to = (
            (up_out, up_in, u_send, u_recv, up) if way == 0 else (down_out, down_in, d_send, d_recv, down)
        )
        at = far * chunk + step
        return remote(out.at[chunk, step], into.at[chunk, step], send.at[at], recv.at[at], dp, to)

    def ring_target(way, chunk, step):
        ahead = (far if way == chunk else far - 1) - step
        return lax.rem(z + ahead, n.nz) if way == 0 else lax.rem(z + n.nz - ahead, n.nz)

    def ring_steps(way, chunk):
        return far if way == chunk else far - 1

    def ring_step(step):
        for way, chunk in ((0, 0), (1, 1), (0, 1), (1, 0)):
            if step < ring_steps(way, chunk):
                out, into = (up_out, up_in) if way == 0 else (down_out, down_in)
                value = part[ring_target(way, chunk, step), :, chunk_of[chunk]]
                if step > 0:
                    ring_hop(way, chunk, step - 1).wait_recv()
                    value = value + into[chunk, step - 1].astype(F32)
                out[chunk, step] = value.astype(BF16)
                ring_hop(way, chunk, step).start()

    product(lax.rem(z + far, n.nz))
    if far > 1:
        product(lax.rem(z + far - 1, n.nz))
        product(lax.rem(z + n.nz - far + 1, n.nz))
    ring_step(0)

    def norm_back(b, carry):
        rows = pl.ds(pl.multiple_of(HALO + n.span * b, 16), n.span)
        first = jnp.zeros((n.span, 128), F32)
        second = jnp.zeros((n.span, 128), F32)
        for j in range(n.tiles):
            whitened = filt[j, rows, :]
            grad_normed = hidden[j, rows, :] * slope[j, rows, :]
            scaled = grad_normed * gain_ref[128 * j : 128 * (j + 1)].reshape(1, 128)
            hidden[j, rows, :] = scaled
            first = first + scaled
            second = second + scaled * whitened
            half, at = j // n.ltiles, (j % n.ltiles) * KROWS
            kgrad[half, at + TAPS : at + TAPS + 1, :] += jnp.sum(grad_normed * whitened, axis=0, keepdims=True)
            kgrad[half, at + TAPS + 1 : at + TAPS + 2, :] += jnp.sum(grad_normed, axis=0, keepdims=True)
        mean1 = jnp.sum(first, axis=1, keepdims=True) * (1.0 / n.ch)
        mean2 = jnp.sum(second, axis=1, keepdims=True) * (1.0 / n.ch)
        inverse = spread[rows, :]
        for j in range(n.tiles):
            gf[j, rows, :] = inverse * (hidden[j, rows, :] - mean1 - filt[j, rows, :] * mean2)
        return carry

    lax.fori_loop(0, n.used // n.span, norm_back, 0)

    def products(i, carry):
        product(lax.rem(z + n.nz - far + 2 + i, n.nz))
        return carry

    if far > 1:
        lax.fori_loop(0, n.nz - 3, products, 0)
    else:
        product(z)

    def back_tile(j, carry):
        taps = taps_ref[:, pl.ds(pl.multiple_of(j * 128, 128), 128)]
        for b in spans:
            base = 1 + n.span * b
            here = slice(HALO + n.span * b, HALO + n.span * (b + 1))
            signal = xs[j, here, :]
            total = jnp.zeros((n.span, 128), F32)
            for s in range(8):
                window = gf[j, base + s : base + s + n.span + 24, :]
                for m in range(4):
                    k = TAPS - 1 - s - 8 * m
                    if k >= 0:
                        shifted = window[8 * m : 8 * m + n.span]
                        total = total + taps[k : k + 1] * shifted
                        product = jnp.sum((shifted * signal).reshape(n.span // 8, 8, 128), axis=0)
                        if b == 0:
                            k8[k] = product
                        else:
                            k8[k] += product
            go[j, here, :] = total.astype(BF16)
        at = pl.multiple_of(lax.rem(j, n.ltiles) * KROWS, 8)
        kgrad[j // n.ltiles, pl.ds(at, TAPS), :] = jnp.sum(k8[...], axis=1)
        return carry

    third = n.tiles // 3
    lax.fori_loop(0, third, back_tile, 0)
    if far > 1:
        ring_step(1)
    lax.fori_loop(third, n.tiles, back_tile, 0)
    swap_k = remote(kgrad.at[other], mate_k, m_send.at[2], m_recv.at[2], mate, z)
    swap_k.start()
    if far > 2:
        ring_step(2)

    def gather_chunk(chunk, carry):
        at = pl.ds(pl.multiple_of(chunk * chunk_rows, chunk_rows), chunk_rows)
        total = None
        for jj in range(4):
            rhs = jnp.concatenate([go[4 * g + jj] for g in range(n.groups)], axis=1)
            piece = dot(taking[jj, at, :], rhs)
            total = piece if total is None else total + piece
        for g in range(n.groups):
            piece = total[:, 128 * g : 128 * (g + 1)].astype(BF16).reshape(per_chunk, 16, 128)
            back[pl.ds(chunk * per_chunk, per_chunk), 16 * g : 16 * (g + 1), :] = piece
        return carry

    lax.fori_loop(0, lanes // chunk_rows, gather_chunk, 0)

    def home_to(peer):
        return remote(back.at[peer], home.at[dp], h_send.at[0], h_recv.at[0], peer, z)

    swap_k.wait_recv()
    mate_k[...] += kgrad[core]

    def k_rows(at):
        return pl.ds(pl.multiple_of(at * n.krow, 8), n.krow)

    def k_scatter(at, slot):
        return remote(mate_k.at[k_rows(at)], k_in.at[slot], ka_send.at[0], ka_recv.at[0], 2 * at + core, z)

    def k_over_z(slot, to):
        return remote(k_z.at[z], k_z.at[slot], kz_send.at[0], kz_recv.at[0], dp, to)

    def k_gather(slot, to):
        return remote(k_all.at[slot], k_all.at[slot], kc_send.at[0], kc_recv.at[0], 2 * to + core, z)

    chips(lambda at: k_scatter(at, chip).start())

    peers(lambda peer: home_to(peer).start())
    home[dp] = back[dp]


    for step in range(3, far):
        ring_step(step)

    await_bytes(k_in, n.chips - 1, ka_recv.at[0])
    k_in[chip] = mate_k[k_rows(chip), :]

    def k_sum(step, carry):
        return carry + k_in[lax.rem(chip + step, n.chips)]

    k_z[z] = lax.fori_loop(1, n.chips, k_sum, k_in[chip])
    for hop in range(1, n.nz):
        k_over_z(z, lax.rem(z + hop, n.nz)).start()

    for way, chunk in ((1, 0), (0, 1), (0, 0), (1, 1)):
        steps = ring_steps(way, chunk)
        if steps > 0:
            into = up_in if way == 0 else down_in
            ring_hop(way, chunk, steps - 1).wait_recv()
            part[z, :, chunk_of[chunk]] += into[chunk, steps - 1].astype(F32)

    def along_x(step):
        there = lax.rem(cx + step, n.nx)
        return there, (there * n.ny + cy) * 2 + core

    def along_y(step):
        there = lax.rem(cy + step, n.ny)
        return there, (cx * n.ny + there) * 2 + core

    def x_scatter(step):
        there, peer = along_x(step)
        return remote(x_out.at[there], x_in.at[cx], xr_send.at[0], xr_recv.at[0], peer, z)

    def y_scatter(step):
        there, peer = along_y(step)
        return there, remote(y_out.at[there], y_in.at[cy], yr_send.at[0], yr_recv.at[0], peer, z)

    def y_gather(step):
        there, peer = along_y(step)
        return remote(y_all.at[cy], y_all.at[cy], yg_send.at[0], yg_recv.at[0], peer, z)

    def x_gather(step):
        there, peer = along_x(step)
        return remote(x_all.at[cx], x_all.at[cx], xg_send.at[0], xg_recv.at[0], peer, z)

    for i in range(n.nx):
        x_out[i] = part[z, n.prow * i : n.prow * (i + 1), :].astype(BF16)
    for step in range(1, n.nx):
        x_scatter(step).start()

    await_bytes(k_z, n.nz - 1, kz_recv.at[0])
    small = k_z[0]
    for i in range(1, n.nz):
        small = small + k_z[i]
    k_all[chip] = small * scale
    chips(lambda at: k_gather(chip, at).start())

    band = part[z, pl.ds(pl.multiple_of(cx * n.prow, 16), n.prow), :]
    await_bytes(x_in, n.nx - 1, xr_recv.at[0])
    for step in range(1, n.nx):
        band = band + x_in[lax.rem(cx + step, n.nx)].astype(F32)
    for l in range(n.ltiles):
        y_own[l] = band[:, 128 * l : 128 * (l + 1)]
        y_out[l] = band[:, 128 * l : 128 * (l + 1)].astype(BF16)
    for step in range(1, n.ny):
        there, copy = y_scatter(step)

        @pl.when(there < n.ltiles)
        def _():
            copy.start()

    @pl.when(cy < n.ltiles)
    def _():
        await_bytes(y_in, n.ny - 1, yr_recv.at[0])
        total = y_own[cy]
        for step in range(1, n.ny):
            total = total + y_in[lax.rem(cy + step, n.ny)].astype(F32)
        y_all[cy] = (total * scale).astype(BF16)
        for step in range(1, n.ny):
            y_gather(step).start()

    def others_along_y(ref, sem):
        @pl.when(cy < n.ltiles)
        def _():
            await_bytes(ref, n.ltiles - 1, sem)

        @pl.when(cy >= n.ltiles)
        def _():
            await_bytes(ref, n.ltiles, sem)

    others_along_y(y_all, yg_recv.at[0])

    for l in range(n.ltiles):
        x_all[cx, :, 128 * l : 128 * (l + 1)] = y_all[l]
    for step in range(1, n.nx):
        x_gather(step).start()

    await_bytes(k_all, n.chips - 1, kc_recv.at[0])
    swap_all = remote(k_all, k_mate, m_send.at[3], m_recv.at[3], mate, z)
    swap_all.start()

    await_bytes(home, n.nd - 1, h_recv.at[0])
    blocks = jnp.concatenate(
        [home[:, 16 * g : 16 * (g + 1), :].reshape(lanes, 128) for g in range(n.groups)], axis=1
    )
    for jj in range(4):
        rows = dot(unsort[n.rows * jj : n.rows * (jj + 1)], blocks).astype(BF16)
        for g in range(n.groups):
            frames_ref[:, 128 * (4 * g + jj) : 128 * (4 * g + jj + 1)] = rows[:, 128 * g : 128 * (g + 1)]
    store = pltpu.make_async_copy(frames_ref, frames_out, io.at[3])
    store.start()

    await_bytes(x_all, n.nx - 1, xg_recv.at[0])
    swap_weight = remote(x_all, x_mate, m_send.at[4], m_recv.at[4], mate, z)
    swap_weight.start()

    def lay_weight(source, half):
        cols = pl.ds(pl.multiple_of(half * n.half, 128), n.half)
        for i in range(n.nx):
            weight_out[n.prow * i : n.prow * (i + 1), cols] = source[i]

    def lay_small(source, half):
        rows = source[...].reshape(n.kall, 128)
        for l in range(n.ltiles):
            cols = pl.ds(pl.multiple_of(half * n.half + 128 * l, 128), 128)
            taps_out[:, cols] = rows[KROWS * l : KROWS * l + TAPS]
            gain_out[cols] = rows[KROWS * l + TAPS : KROWS * l + TAPS + 1].reshape(128)
            shift_out[cols] = rows[KROWS * l + TAPS + 1 : KROWS * l + TAPS + 2].reshape(128)

    lay_weight(x_all, core)
    lay_small(k_all, core)

    swap_all.wait_recv()
    lay_small(k_mate, other)
    swap_weight.wait_recv()
    lay_weight(x_mate, other)

    for copy in (swap_cot, swap_act, swap_k, swap_all, swap_weight):
        copy.wait_send()
    for step in range(far):
        gather_up(step, z).wait_send()
        gather_down(step, z).wait_send()
    for way in range(2):
        for chunk in range(2):
            for step in range(ring_steps(way, chunk)):
                ring_hop(way, chunk, step).wait_send()
    await_bytes(x_in, n.nx - 1, xr_send.at[0])
    await_bytes(x_all, n.nx - 1, xg_send.at[0])
    others_along_y(y_out, yr_send.at[0])

    @pl.when(cy < n.ltiles)
    def _():
        await_bytes(y_all, n.ny - 1, yg_send.at[0])

    await_bytes(whole.at[:, pl.ds(0, hrow)], n.nz - 1, gm_send.at[0])
    await_bytes(k_z, n.nz - 1, kz_send.at[0])
    await_bytes(k_in, n.chips - 1, ka_send.at[0])
    await_bytes(k_all, n.chips - 1, kc_send.at[0])
    await_bytes(label_out, n.nd - 1, l_send.at[0])
    await_bytes(outgoing, n.nd - 1, b_send.at[0])
    await_bytes(back, n.nd - 1, h_send.at[0])
    store.wait()


def on_device(frames, destination, utt_lengths, cotangent, weight, kernel, norm_gain, norm_shift):
    n = Sizes(lax.axis_size("dp"), lax.axis_size("fsdp"), frames.shape[0], frames.shape[1], weight.shape[0])
    scale = 1.0 / math.sqrt(n.rows * n.nd * n.nz)
    far = n.nz // 2
    lanes = 16 * n.nb
    vmem = pl.BlockSpec(memory_space=pltpu.VMEM)
    smem = pl.BlockSpec(memory_space=pltpu.SMEM)
    hbm = pl.BlockSpec(memory_space=pl.ANY)

    def dma(count):
        return [pltpu.SemaphoreType.DMA((count,))] * 2

    def buf(*shape, dtype=F32):
        return pltpu.VMEM(shape, dtype)

    blocks = buf(n.nb, n.slab, 128, dtype=BF16)
    label = buf(n.nd, 1, 128)
    plane = buf(n.tiles, n.padded, 128)
    ring = buf(2, far, n.shard, n.quarter, dtype=BF16)
    band = buf(n.nx, n.prow, n.half, dtype=BF16)
    tile = buf(n.ny, n.prow, 128, dtype=BF16)
    small = buf(n.chips, n.krow, 128)
    grads = pl.pallas_call(
        functools.partial(module_kernel, n, scale),
        out_shape=(
            jax.ShapeDtypeStruct((n.rows, n.ch), BF16),
            jax.ShapeDtypeStruct((n.shard, n.ch), BF16),
            jax.ShapeDtypeStruct((TAPS, n.ch), F32),
            jax.ShapeDtypeStruct((n.ch,), F32),
            jax.ShapeDtypeStruct((n.ch,), F32),
        ),
        in_specs=[vmem, smem, hbm, hbm, hbm, vmem, vmem, vmem],
        out_specs=(hbm, vmem, vmem, vmem, vmem),
        scratch_shapes=[
            buf(n.rows, n.ch, dtype=BF16), buf(n.rows, n.ch, dtype=BF16),
            blocks, blocks, label, label, buf(16 * n.nb, 128), buf(n.nz, n.shard, n.ch, dtype=BF16),
            buf(4 * n.rows, lanes, dtype=BF16), buf(4 * n.padded, lanes, dtype=BF16), buf(4, lanes, n.padded, dtype=BF16),
            plane, plane, plane, plane, plane, buf(n.padded, 128), buf(n.padded, n.ch, dtype=BF16),
            buf(n.tiles, n.padded, 128, dtype=BF16), buf(TAPS, 8, 128), buf(2, n.kall, 128),
            buf(n.padded, n.ch, dtype=BF16), buf(n.ch, 2 * n.rows, dtype=BF16), buf(n.rows, n.ch, dtype=BF16),
            buf(2 * n.rows, n.half, dtype=BF16), buf(n.rows, n.half, dtype=BF16),
            buf(n.nz, n.shard, n.half), ring, ring, ring, ring, blocks, blocks,
            band, band, buf(n.ltiles, n.prow, 128), tile, tile, tile, band, band,
            buf(n.kall, 128), small, buf(n.nz, n.krow, 128), small, small,
            pltpu.SemaphoreType.DMA((4,)), *dma(1), *dma(1), *dma(1),
            *dma(far), *dma(far), *dma(1), *dma(5),
            *dma(2 * far), *dma(2 * far),
            *dma(1), *dma(1), *dma(1), *dma(1),
            *dma(1), *dma(1), *dma(1),
        ],
        compiler_params=pltpu.CompilerParams(
            collective_id=0, has_side_effects=True, vmem_limit_bytes=VMEM_BYTES
        ),
    )(destination, utt_lengths, frames, cotangent, weight, kernel, norm_gain, norm_shift)
    return grads[0], grads[1].astype(F32), grads[2], grads[3], grads[4]


def solution(mesh):
    placed = (
        P(("dp", "fsdp"), None),
        P(("dp", "fsdp")),
        P(("dp", "fsdp"), None),
        P(("dp", "fsdp"), None),
        P("fsdp", None),
        P(),
        P(),
        P(),
    )
    return jax.shard_map(
        on_device,
        mesh=mesh,
        in_specs=placed,
        out_specs=(P(("dp", "fsdp"), None), P("fsdp", None), P(), P(), P()),
        check_vma=False,
    )
```

```python
import functools
import math

import jax
import jax.numpy as jnp
from jax import lax
from jax.experimental import pallas as pl
from jax.experimental.pallas import tpu as pltpu
from jax.sharding import PartitionSpec as P

EPSILON = 1e-05
MESH = pl.DeviceIdType.MESH
F32 = jnp.float32
BF16 = jnp.bfloat16
BLOCK = 4
TAPS = 31
HALO = 16
KROWS = 40
VMEM_BYTES = 56 * 1024 * 1024


class Sizes:
    def __init__(self, dp_size, fsdp_size, rows, channels, shard):
        self.nd = dp_size
        self.nz = fsdp_size
        self.rows = rows
        self.ch = channels
        self.shard = shard
        self.nb = rows // BLOCK
        self.tiles = channels // 128
        self.groups = self.tiles // 4
        self.slab = 4 * self.tiles
        self.chips = dp_size // 2
        self.half = channels // 2
        self.ltiles = self.half // 128
        self.quarter = self.half // 2
        self.nx = 4 if self.chips >= 32 else 2
        self.ny = self.chips // self.nx
        self.prow = shard // self.nx
        self.used = rows + 4 * HALO
        self.padded = self.used + 2 * HALO
        self.span = 80 if self.used % 80 == 0 else 48
        self.krow = 8 * (-(-(5 * self.ltiles) // self.chips))
        self.kall = self.krow * self.chips


def one_hot(mask):
    return jnp.where(mask, 1.0, 0.0).astype(BF16)


def dot(a, b):
    return jnp.dot(a, b, preferred_element_type=F32)


def remote(src, dst, send, recv, dp, z):
    return pltpu.make_async_remote_copy(
        src_ref=src, dst_ref=dst, send_sem=send, recv_sem=recv, device_id=(dp, z), device_id_type=MESH
    )


def await_bytes(ref, count, sem):
    part = ref.at[pl.ds(0, count)]
    pltpu.make_async_copy(part, part, sem).wait()


def padded_place(frame, ends):
    place = frame + HALO
    for end in ends:
        place = place + jnp.where(frame >= end, HALO, 0)
    return place


def module_kernel(
    n, scale,
    dest_ref, utt_ref, frames_hbm, cot_hbm, weight_hbm, taps_ref, gain_ref, shift_ref,
    frames_out, weight_out, small_out,
    frames_ref, cot_ref,
    outgoing, arrived, label_out, label_in, labels, whole, unsort, setting, taking,
    xs, filt, hidden, gf, slope, spread, actp, go, k8, kgrad, cot_pad, cot_turned, mate_cot, act_both, act_send,
    part, up_out, up_in, down_out, down_in, back, home,
    x_out, x_in, y_own, y_out, y_in, y_all, x_all, x_mate, mate_k, k_in, k_z, k_all, k_mate,
    io, b_send, b_recv, l_send, l_recv, h_send, h_recv,
    gu_send, gu_recv, gd_send, gd_recv, gm_send, gm_recv, m_send, m_recv,
    u_send, u_recv, d_send, d_recv,
    xr_send, xr_recv, yr_send, yr_recv, yg_send, yg_recv, xg_send, xg_recv,
    ka_send, ka_recv, kz_send, kz_recv, kc_send, kc_recv,
):
    dp = lax.axis_index("dp")
    z = lax.axis_index("fsdp")
    core = lax.rem(dp, 2)
    other = 1 - core
    mate = dp + 1 - 2 * core
    chip = dp // 2
    cx = chip // n.ny
    cy = lax.rem(chip, n.ny)
    far = n.nz // 2
    up = lax.rem(z + 1, n.nz)
    down = lax.rem(z + n.nz - 1, n.nz)
    hrow = n.shard // 2
    lanes = 16 * n.nb
    spans = range(n.used // n.span)
    mine = pl.ds(pl.multiple_of(core * n.half, 128), n.half)
    theirs = pl.ds(pl.multiple_of(other * n.half, 128), n.half)

    loads = [
        pltpu.make_async_copy(frames_hbm, frames_ref, io.at[0]),
        pltpu.make_async_copy(weight_hbm, whole.at[z], io.at[1]),
        pltpu.make_async_copy(cot_hbm, cot_ref, io.at[2]),
    ]
    for load in loads:
        load.start()

    barrier = pltpu.get_barrier_semaphore()

    def along_dp(step, carry):
        pl.semaphore_signal(
            barrier, inc=1, device_id=(lax.rem(dp + step, n.nd), z), device_id_type=MESH
        )
        return carry

    lax.fori_loop(1, n.nd, along_dp, 0)
    for step in range(1, n.nz):
        pl.semaphore_signal(
            barrier, inc=1, device_id=(dp, lax.rem(z + step, n.nz)), device_id_type=MESH
        )

    lane_rows = lax.broadcasted_iota(jnp.int32, (1, n.rows), 1)
    dest = dest_ref[...].reshape(1, n.nb)
    owners = dest // n.nb
    slots = dest - owners * n.nb
    owner_iota = lax.broadcasted_iota(jnp.int32, (n.nd, n.nb), 0)
    slot_of = jnp.sum(jnp.where(owner_iota == owners, slots, 0).astype(F32), axis=1, keepdims=True)
    slot_of = jnp.broadcast_to(slot_of, (n.nd, 128))
    for i in range(n.nd):
        label_out[i] = slot_of[i : i + 1]
    four = one_hot(
        lax.broadcasted_iota(jnp.int32, (n.nb, n.rows), 0)
        == lax.broadcasted_iota(jnp.int32, (n.nb, n.rows), 1) // BLOCK
    )
    wide = dot(jnp.broadcast_to(owners.astype(F32), (16, n.nb)).astype(BF16), four)[:1]
    code = wide.astype(jnp.int32) * 16 + lane_rows % BLOCK

    loads[0].wait()
    mats = [
        jnp.concatenate(
            [frames_ref[:, 128 * (4 * g + jj) : 128 * (4 * g + jj + 1)] for g in range(n.groups)], axis=1
        )
        for jj in range(4)
    ]
    chunk_rows = min(256, lanes)
    per_chunk = chunk_rows // 16

    def sort_chunk(chunk, carry):
        place = lax.broadcasted_iota(jnp.int32, (chunk_rows, n.rows), 0) + chunk * chunk_rows
        total = dot(one_hot(place == code), mats[0])
        for jj in range(1, 4):
            total = total + dot(one_hot(place == code + 4 * jj), mats[jj])
        for g in range(n.groups):
            piece = total[:, 128 * g : 128 * (g + 1)].astype(BF16).reshape(per_chunk, 16, 128)
            outgoing[pl.ds(chunk * per_chunk, per_chunk), 16 * g : 16 * (g + 1), :] = piece
        return carry

    lax.fori_loop(0, lanes // chunk_rows, sort_chunk, 0)

    loads[1].wait()
    pl.semaphore_wait(barrier, n.nd - 1 + n.nz - 1)

    hchunk = hrow // 2

    def gather_hop(way, chunk, step, block):
        send, recv, to = (gu_send, gu_recv, up) if way == 0 else (gd_send, gd_recv, down)
        rows = pl.ds(pl.multiple_of(core * hrow + chunk * hchunk, 16), hchunk)
        at = far * chunk + step
        return remote(whole.at[block, rows], whole.at[block, rows], send.at[at], recv.at[at], dp, to)

    def gather_mate(chunk, block):
        rows = pl.ds(pl.multiple_of(core * hrow + chunk * hchunk, 16), hchunk)
        return remote(whole.at[block, rows], whole.at[block, rows], gm_send.at[0], gm_recv.at[0], mate, z)

    def gather_block(way, step):
        return lax.rem(z + n.nz - step - 1, n.nz) if way == 0 else lax.rem(z + step + 1, n.nz)

    ways = ((0, 0), (1, 1), (0, 1), (1, 0))

    def ring_steps(way, chunk):
        return far if way == chunk else far - 1

    def gather_pass(step):
        for way, chunk in ways:
            if step < ring_steps(way, chunk):
                block = gather_block(way, step)
                gather_hop(way, chunk, step, block).wait_recv()
                if step + 1 < ring_steps(way, chunk):
                    gather_hop(way, chunk, step + 1, block).start()
                gather_mate(chunk, block).start()

    for way, chunk in ways:
        if ring_steps(way, chunk) > 0:
            gather_hop(way, chunk, 0, z).start()

    def block_to(peer):
        return remote(outgoing.at[peer], arrived.at[dp], b_send.at[0], b_recv.at[0], peer, z)

    def label_to(peer):
        return remote(label_out.at[peer], label_in.at[dp], l_send.at[0], l_recv.at[0], peer, z)

    def peers(body):
        def step_to(step, carry):
            body(lax.rem(dp + step, n.nd))
            return carry

        lax.fori_loop(1, n.nd, step_to, 0)

    def chips(body):
        def step_to(step, carry):
            body(lax.rem(chip + step, n.chips))
            return carry

        lax.fori_loop(1, n.chips, step_to, 0)

    def send_block(peer):
        label_to(peer).start()
        block_to(peer).start()

    peers(send_block)
    loads[2].wait()
    swap_cot = remote(cot_ref, mate_cot, m_send.at[0], m_recv.at[0], mate, z)
    swap_cot.start()
    arrived[dp] = outgoing[dp]
    label_in[dp] = label_out[dp]

    ends = [utt_ref[0, 0]]
    for i in range(1, 3):
        ends.append(ends[-1] + utt_ref[0, i])
    frame_row = padded_place(lane_rows, ends)
    pad_mat = one_hot(lax.broadcasted_iota(jnp.int32, (n.padded, n.rows), 0) == frame_row)
    cot_pad[...] = dot(pad_mat, cot_ref[...]).astype(BF16)
    cot_turned[:, : n.rows] = cot_ref[...].T
    kgrad[...] = jnp.zeros_like(kgrad)
    actp[...] = jnp.zeros_like(actp)
    go[...] = jnp.zeros_like(go)
    gf[:, :HALO, :] = jnp.zeros((n.tiles, HALO, 128), F32)
    gf[:, n.padded - HALO :, :] = jnp.zeros((n.tiles, HALO, 128), F32)
    sub_rows = lax.broadcasted_iota(jnp.int32, (n.rows, 1), 0)
    near = lax.broadcasted_iota(jnp.int32, (n.rows, n.nb), 1) == sub_rows // BLOCK
    code_col = jnp.sum(jnp.where(near, owners, 0).astype(F32), axis=1, keepdims=True)
    code_col = code_col.astype(jnp.int32) * 16 + sub_rows % BLOCK
    order = lax.broadcasted_iota(jnp.int32, (n.rows, lanes), 1)
    for jj in range(4):
        unsort[n.rows * jj : n.rows * (jj + 1)] = one_hot(order == code_col + 4 * jj)
    swap_cot.wait_recv()
    cot_turned[:, n.rows :] = mate_cot[...].T

    if far > 1:
        gather_pass(0)

    await_bytes(label_in, n.nd - 1, l_recv.at[0])
    lane128 = lax.broadcasted_iota(jnp.int32, (1, 128), 1)
    chunks = []
    for q in range(n.nb // 8):
        row = jnp.zeros((1, 128), F32)
        for s in range(8):
            row = row + jnp.where(lane128 // 16 == s, label_in[8 * q + s], 0.0)
        chunks.append(row)
    slot_row = jnp.concatenate(chunks, axis=1).astype(jnp.int32)
    lane_all = lax.broadcasted_iota(jnp.int32, (1, lanes), 1)
    place_row = padded_place(slot_row * BLOCK + lane_all % 4, ends)

    def lay_label(src, carry):
        labels[pl.ds(pl.multiple_of(16 * src, 16), 16), :] = jnp.broadcast_to(label_in[src], (16, 128))
        return carry

    lax.fori_loop(0, n.nb, lay_label, 0)

    row_iota = lax.broadcasted_iota(jnp.int32, (n.padded, lanes), 0)

    def setter(jj, carry):
        mask = row_iota == jnp.where((lane_all // 4) % 4 == jj, place_row, -1)
        setting[pl.ds(pl.multiple_of(jj * n.padded, 16), n.padded), :] = one_hot(mask)
        return carry

    lax.fori_loop(0, 4, setter, 0)

    def taker(chunk, carry):
        at = pl.ds(pl.multiple_of(chunk * chunk_rows, chunk_rows), chunk_rows)
        slot = labels[at, :][:, :1].astype(jnp.int32)
        sub = lax.broadcasted_iota(jnp.int32, (chunk_rows, 1), 0)
        place = padded_place(slot * BLOCK + sub % 4, ends)
        cols = lax.broadcasted_iota(jnp.int32, (chunk_rows, n.padded), 1)
        for jj in range(4):
            taking[jj, at, :] = one_hot(cols == jnp.where((sub // 4) % 4 == jj, place, -1))
        return carry

    lax.fori_loop(0, lanes // chunk_rows, taker, 0)

    if far > 2:
        gather_pass(1)

    await_bytes(arrived, n.nd - 1, b_recv.at[0])
    blocks = jnp.concatenate(
        [arrived[:, 16 * g : 16 * (g + 1), :].reshape(lanes, 128) for g in range(n.groups)], axis=1
    )

    def put(jj, carry):
        owned = dot(setting[pl.ds(pl.multiple_of(jj * n.padded, 16), n.padded), :], blocks)
        for g in range(n.groups):
            xs[4 * g + jj] = owned[:, 128 * g : 128 * (g + 1)]
        return carry

    lax.fori_loop(0, 4, put, 0)

    for step in range(2, far - 1):
        gather_pass(step)

    def filter_tile(j, carry):
        taps = taps_ref[:, pl.ds(pl.multiple_of(j * 128, 128), 128)]
        for b in spans:
            base = 1 + n.span * b
            total = jnp.zeros((n.span, 128), F32)
            for s in range(8):
                window = xs[j, base + s : base + s + n.span + 24, :]
                for m in range(4):
                    k = s + 8 * m
                    if k < TAPS:
                        total = total + taps[k : k + 1] * window[8 * m : 8 * m + n.span]
            filt[j, HALO + n.span * b : HALO + n.span * (b + 1), :] = total
        return carry

    lax.fori_loop(0, n.tiles, filter_tile, 0)
    gather_pass(far - 1)

    def norm_span(b, carry):
        rows = pl.ds(pl.multiple_of(HALO + n.span * b, 16), n.span)
        total = filt[0, rows, :]
        for j in range(1, n.tiles):
            total = total + filt[j, rows, :]
        mean = jnp.sum(total, axis=1, keepdims=True) * (1.0 / n.ch)
        square = jnp.zeros((n.span, 128), F32)
        for j in range(n.tiles):
            centred = filt[j, rows, :] - mean
            square = square + centred * centred
        variance = jnp.sum(square, axis=1, keepdims=True) * (1.0 / n.ch)
        inverse = 1.0 / jnp.sqrt(variance + EPSILON)
        spread[rows, :] = jnp.broadcast_to(inverse, (n.span, 128))
        for j in range(n.tiles):
            whitened = (filt[j, rows, :] - mean) * inverse
            normed = whitened * gain_ref[128 * j : 128 * (j + 1)].reshape(1, 128) + shift_ref[128 * j : 128 * (j + 1)].reshape(1, 128)
            logistic = 1.0 / (1.0 + jnp.exp(-normed))
            activated = normed * logistic
            actp[rows, 128 * j : 128 * (j + 1)] = activated.astype(BF16)
            filt[j, rows, :] = whitened
            slope[j, rows, :] = logistic * (1.0 + normed * (1.0 - logistic))
        return carry

    lax.fori_loop(0, n.used // n.span, norm_span, 0)

    frame_col = padded_place(lax.broadcasted_iota(jnp.int32, (n.rows, 1), 0), ends)
    take = one_hot(lax.broadcasted_iota(jnp.int32, (n.rows, n.padded), 1) == frame_col)
    act_send[...] = dot(take, actp[:, theirs]).astype(BF16)
    swap_act = remote(act_send, act_both.at[pl.ds(n.rows, n.rows)], m_send.at[1], m_recv.at[1], mate, z)
    swap_act.start()
    act_both[: n.rows] = dot(take, actp[:, mine]).astype(BF16)

    await_bytes(whole.at[:, pl.ds(0, hrow)], n.nz - 1, gm_recv.at[0])
    width = 512
    per = width // 128

    def project(i, carry):
        cols = pl.ds(pl.multiple_of(i * width, width), width)
        piece = dot(cot_pad[...], whole[:, :, cols].reshape(n.ch, width))
        for q in range(per):
            hidden[per * i + q] = piece[:, 128 * q : 128 * (q + 1)]
        return carry

    lax.fori_loop(0, n.ch // width, project, 0)

    swap_act.wait_recv()

    def product(target):
        part[target] = dot(cot_turned[pl.ds(pl.multiple_of(target * n.shard, 16), n.shard), :], act_both[...])

    chunk_of = [slice(0, n.quarter), slice(n.quarter, n.half)]

    def ring_hop(way, chunk, step):
        out, into, send, recv, to = (
            (up_out, up_in, u_send, u_recv, up) if way == 0 else (down_out, down_in, d_send, d_recv, down)
        )
        at = far * chunk + step
        return remote(out.at[chunk, step], into.at[chunk, step], send.at[at], recv.at[at], dp, to)

    def ring_target(way, chunk, step):
        ahead = (far if way == chunk else far - 1) - step
        return lax.rem(z + ahead, n.nz) if way == 0 else lax.rem(z + n.nz - ahead, n.nz)

    def ring_step(step):
        for way, chunk in ways:
            if step < ring_steps(way, chunk):
                out, into = (up_out, up_in) if way == 0 else (down_out, down_in)
                value = part[ring_target(way, chunk, step), :, chunk_of[chunk]]
                if step > 0:
                    ring_hop(way, chunk, step - 1).wait_recv()
                    value = value + into[chunk, step - 1].astype(F32)
                out[chunk, step] = value.astype(BF16)
                ring_hop(way, chunk, step).start()

    product(lax.rem(z + far, n.nz))
    if far > 1:
        product(lax.rem(z + far - 1, n.nz))
        product(lax.rem(z + n.nz - far + 1, n.nz))
    ring_step(0)

    def norm_back(b, carry):
        rows = pl.ds(pl.multiple_of(HALO + n.span * b, 16), n.span)
        first = jnp.zeros((n.span, 128), F32)
        second = jnp.zeros((n.span, 128), F32)
        for j in range(n.tiles):
            whitened = filt[j, rows, :]
            grad_normed = hidden[j, rows, :] * slope[j, rows, :]
            scaled = grad_normed * gain_ref[128 * j : 128 * (j + 1)].reshape(1, 128)
            hidden[j, rows, :] = scaled
            first = first + scaled
            second = second + scaled * whitened
            half, at = j // n.ltiles, (j % n.ltiles) * KROWS
            kgrad[half, at + TAPS : at + TAPS + 1, :] += jnp.sum(grad_normed * whitened, axis=0, keepdims=True)
            kgrad[half, at + TAPS + 1 : at + TAPS + 2, :] += jnp.sum(grad_normed, axis=0, keepdims=True)
        mean1 = jnp.sum(first, axis=1, keepdims=True) * (1.0 / n.ch)
        mean2 = jnp.sum(second, axis=1, keepdims=True) * (1.0 / n.ch)
        inverse = spread[rows, :]
        for j in range(n.tiles):
            gf[j, rows, :] = inverse * (hidden[j, rows, :] - mean1 - filt[j, rows, :] * mean2)
        return carry

    lax.fori_loop(0, n.used // n.span, norm_back, 0)

    def products(i, carry):
        product(lax.rem(z + n.nz - far + 2 + i, n.nz))
        return carry

    if far > 1:
        lax.fori_loop(0, n.nz - 3, products, 0)
    else:
        product(z)

    def back_tile(j, carry):
        taps = taps_ref[:, pl.ds(pl.multiple_of(j * 128, 128), 128)]
        for b in spans:
            base = 1 + n.span * b
            here = slice(HALO + n.span * b, HALO + n.span * (b + 1))
            signal = xs[j, here, :]
            total = jnp.zeros((n.span, 128), F32)
            for s in range(8):
                window = gf[j, base + s : base + s + n.span + 24, :]
                for m in range(4):
                    k = TAPS - 1 - s - 8 * m
                    if k >= 0:
                        shifted = window[8 * m : 8 * m + n.span]
                        total = total + taps[k : k + 1] * shifted
                        product = jnp.sum((shifted * signal).reshape(n.span // 8, 8, 128), axis=0)
                        if b == 0:
                            k8[k] = product
                        else:
                            k8[k] += product
            go[j, here, :] = total.astype(BF16)
        at = pl.multiple_of(lax.rem(j, n.ltiles) * KROWS, 8)
        kgrad[j // n.ltiles, pl.ds(at, TAPS), :] = jnp.sum(k8[...], axis=1)
        return carry

    def home_to(peer, group):
        rows = pl.ds(16 * group, 16)
        return remote(
            back.at[peer, rows], home.at[dp, rows], h_send.at[group], h_recv.at[group], peer, z
        )

    def k_rows(at):
        return pl.ds(pl.multiple_of(at * n.krow, 8), n.krow)

    def k_scatter(at, slot):
        return remote(mate_k.at[k_rows(at)], k_in.at[slot], ka_send.at[0], ka_recv.at[0], 2 * at + core, z)

    def k_over_z(slot, to):
        return remote(k_z.at[z], k_z.at[slot], kz_send.at[0], kz_recv.at[0], dp, to)

    def k_gather(slot, to):
        return remote(k_all.at[slot], k_all.at[slot], kc_send.at[0], kc_recv.at[0], 2 * to + core, z)

    swap_k = remote(kgrad.at[other], mate_k, m_send.at[2], m_recv.at[2], mate, z)
    for group in range(n.groups):
        lax.fori_loop(4 * group, 4 * group + 4, back_tile, 0)
        if group == n.groups - 1:
            swap_k.start()
        if group + 1 < far:
            ring_step(group + 1)

        def gather_chunk(chunk, carry):
            at = pl.ds(pl.multiple_of(chunk * chunk_rows, chunk_rows), chunk_rows)
            total = dot(taking[0, at, :], go[4 * group])
            for jj in range(1, 4):
                total = total + dot(taking[jj, at, :], go[4 * group + jj])
            piece = total.astype(BF16).reshape(per_chunk, 16, 128)
            back[pl.ds(chunk * per_chunk, per_chunk), 16 * group : 16 * (group + 1), :] = piece
            return carry

        lax.fori_loop(0, lanes // chunk_rows, gather_chunk, 0)
        if group == n.groups - 1:
            swap_k.wait_recv()
            mate_k[...] += kgrad[core]
            chips(lambda at: k_scatter(at, chip).start())
        peers(lambda peer: home_to(peer, group).start())
    home[dp] = back[dp]


    for step in range(n.groups + 1, far):
        ring_step(step)

    await_bytes(k_in, n.chips - 1, ka_recv.at[0])
    k_in[chip] = mate_k[k_rows(chip), :]

    def k_sum(step, carry):
        return carry + k_in[lax.rem(chip + step, n.chips)]

    k_z[z] = lax.fori_loop(1, n.chips, k_sum, k_in[chip])
    for hop in range(1, n.nz):
        k_over_z(z, lax.rem(z + hop, n.nz)).start()

    for way, chunk in ((1, 0), (0, 1), (0, 0), (1, 1)):
        steps = ring_steps(way, chunk)
        if steps > 0:
            into = up_in if way == 0 else down_in
            ring_hop(way, chunk, steps - 1).wait_recv()
            part[z, :, chunk_of[chunk]] += into[chunk, steps - 1].astype(F32)

    def along_x(step):
        there = lax.rem(cx + step, n.nx)
        return there, (there * n.ny + cy) * 2 + core

    def along_y(step):
        there = lax.rem(cy + step, n.ny)
        return there, (cx * n.ny + there) * 2 + core

    def x_scatter(step):
        there, peer = along_x(step)
        return remote(x_out.at[there], x_in.at[cx], xr_send.at[0], xr_recv.at[0], peer, z)

    def y_scatter(step):
        there, peer = along_y(step)
        return there, remote(y_out.at[there], y_in.at[cy], yr_send.at[0], yr_recv.at[0], peer, z)

    def y_gather(step):
        there, peer = along_y(step)
        return remote(y_all.at[cy], y_all.at[cy], yg_send.at[0], yg_recv.at[0], peer, z)

    def x_gather(step):
        there, peer = along_x(step)
        return remote(x_all.at[cx], x_all.at[cx], xg_send.at[0], xg_recv.at[0], peer, z)

    for i in range(n.nx):
        x_out[i] = part[z, n.prow * i : n.prow * (i + 1), :].astype(BF16)
    for step in range(1, n.nx):
        x_scatter(step).start()

    await_bytes(k_z, n.nz - 1, kz_recv.at[0])
    small = k_z[0]
    for i in range(1, n.nz):
        small = small + k_z[i]
    k_all[chip] = small * scale
    chips(lambda at: k_gather(chip, at).start())

    band = part[z, pl.ds(pl.multiple_of(cx * n.prow, 16), n.prow), :]
    await_bytes(x_in, n.nx - 1, xr_recv.at[0])
    for step in range(1, n.nx):
        band = band + x_in[lax.rem(cx + step, n.nx)].astype(F32)
    for l in range(n.ltiles):
        y_own[l] = band[:, 128 * l : 128 * (l + 1)]
        y_out[l] = band[:, 128 * l : 128 * (l + 1)].astype(BF16)
    for step in range(1, n.ny):
        there, copy = y_scatter(step)

        @pl.when(there < n.ltiles)
        def _():
            copy.start()

    @pl.when(cy < n.ltiles)
    def _():
        await_bytes(y_in, n.ny - 1, yr_recv.at[0])
        total = y_own[cy]
        for step in range(1, n.ny):
            total = total + y_in[lax.rem(cy + step, n.ny)].astype(F32)
        y_all[cy] = (total * scale).astype(BF16)
        for step in range(1, n.ny):
            y_gather(step).start()

    def others_along_y(ref, sem):
        @pl.when(cy < n.ltiles)
        def _():
            await_bytes(ref, n.ltiles - 1, sem)

        @pl.when(cy >= n.ltiles)
        def _():
            await_bytes(ref, n.ltiles, sem)

    others_along_y(y_all, yg_recv.at[0])

    for l in range(n.ltiles):
        x_all[cx, :, 128 * l : 128 * (l + 1)] = y_all[l]
    for step in range(1, n.nx):
        x_gather(step).start()

    await_bytes(k_all, n.chips - 1, kc_recv.at[0])
    swap_all = remote(k_all, k_mate, m_send.at[3], m_recv.at[3], mate, z)
    swap_all.start()

    def unsort_group(group):
        rows = slice(16 * group, 16 * (group + 1))
        await_bytes(home.at[:, pl.ds(16 * group, 16)], n.nd - 1, h_recv.at[group])
        block = home[:, rows, :].reshape(lanes, 128)
        for jj in range(4):
            tile = 4 * group + jj
            found = dot(unsort[n.rows * jj : n.rows * (jj + 1)], block).astype(BF16)
            frames_ref[:, 128 * tile : 128 * (tile + 1)] = found

    for group in range(n.groups - 1):
        unsort_group(group)
    await_bytes(x_all, n.nx - 1, xg_recv.at[0])
    swap_weight = remote(x_all, x_mate, m_send.at[4], m_recv.at[4], mate, z)
    swap_weight.start()

    def lay_weight(source, half):
        cols = pl.ds(pl.multiple_of(half * n.half, 128), n.half)
        for i in range(n.nx):
            weight_out[n.prow * i : n.prow * (i + 1), cols] = source[i]

    def lay_small(source, half):
        rows = source[...].reshape(n.kall, 128)
        for l in range(n.ltiles):
            cols = pl.ds(pl.multiple_of(half * n.half + 128 * l, 128), 128)
            small_out[:, cols] = rows[KROWS * l : KROWS * (l + 1)]

    unsort_group(n.groups - 1)
    store = pltpu.make_async_copy(frames_ref, frames_out, io.at[3])
    store.start()
    lay_weight(x_all, core)
    lay_small(k_all, core)

    swap_all.wait_recv()
    lay_small(k_mate, other)
    swap_weight.wait_recv()
    lay_weight(x_mate, other)

    for copy in (swap_cot, swap_act, swap_k, swap_all, swap_weight):
        copy.wait_send()
    for step in range(far):
        for way, chunk in ways:
            if step < ring_steps(way, chunk):
                gather_hop(way, chunk, step, z).wait_send()
    for way in range(2):
        for chunk in range(2):
            for step in range(ring_steps(way, chunk)):
                ring_hop(way, chunk, step).wait_send()
    await_bytes(x_in, n.nx - 1, xr_send.at[0])
    await_bytes(x_all, n.nx - 1, xg_send.at[0])
    others_along_y(y_out, yr_send.at[0])

    @pl.when(cy < n.ltiles)
    def _():
        await_bytes(y_all, n.ny - 1, yg_send.at[0])

    await_bytes(whole.at[:, pl.ds(0, hrow)], n.nz - 1, gm_send.at[0])
    await_bytes(k_z, n.nz - 1, kz_send.at[0])
    await_bytes(k_in, n.chips - 1, ka_send.at[0])
    await_bytes(k_all, n.chips - 1, kc_send.at[0])
    await_bytes(label_out, n.nd - 1, l_send.at[0])
    await_bytes(outgoing, n.nd - 1, b_send.at[0])
    for group in range(n.groups):
        await_bytes(back.at[:, pl.ds(16 * group, 16)], n.nd - 1, h_send.at[group])
    store.wait()


def finish_kernel(n, frames_ref, weight_ref, small_ref, frames_out, weight_out, taps_out, gain_out, shift_out):
    frames_out[...] = frames_ref[...]
    weight_out[...] = weight_ref[...].astype(F32)

    @pl.when(pl.program_id(0) == 0)
    def _():
        taps_out[...] = small_ref[:TAPS]
        gain_out[...] = small_ref[TAPS : TAPS + 1].reshape(n.ch)
        shift_out[...] = small_ref[TAPS + 1 : TAPS + 2].reshape(n.ch)


def finish(n, frames, weight, small):
    steps = 4
    band = pl.BlockSpec((n.rows // steps, n.ch), lambda i: (i, 0))
    shard = pl.BlockSpec((n.shard // steps, n.ch), lambda i: (i, 0))
    vector = pl.BlockSpec((n.ch,), lambda i: (0,))
    return pl.pallas_call(
        functools.partial(finish_kernel, n),
        grid=(steps,),
        out_shape=(
            jax.ShapeDtypeStruct((n.rows, n.ch), BF16),
            jax.ShapeDtypeStruct((n.shard, n.ch), F32),
            jax.ShapeDtypeStruct((TAPS, n.ch), F32),
            jax.ShapeDtypeStruct((n.ch,), F32),
            jax.ShapeDtypeStruct((n.ch,), F32),
        ),
        in_specs=[band, shard, pl.BlockSpec((KROWS, n.ch), lambda i: (0, 0))],
        out_specs=(band, shard, pl.BlockSpec((TAPS, n.ch), lambda i: (0, 0)), vector, vector),
    )(frames, weight, small)


def on_device(frames, destination, utt_lengths, cotangent, weight, kernel, norm_gain, norm_shift):
    n = Sizes(lax.axis_size("dp"), lax.axis_size("fsdp"), frames.shape[0], frames.shape[1], weight.shape[0])
    scale = 1.0 / math.sqrt(n.rows * n.nd * n.nz)
    far = n.nz // 2
    lanes = 16 * n.nb
    vmem = pl.BlockSpec(memory_space=pltpu.VMEM)
    smem = pl.BlockSpec(memory_space=pltpu.SMEM)
    hbm = pl.BlockSpec(memory_space=pl.ANY)

    def dma(count):
        return [pltpu.SemaphoreType.DMA((count,))] * 2

    def buf(*shape, dtype=F32):
        return pltpu.VMEM(shape, dtype)

    blocks = buf(n.nb, n.slab, 128, dtype=BF16)
    label = buf(n.nd, 1, 128)
    plane = buf(n.tiles, n.padded, 128)
    ring = buf(2, far, n.shard, n.quarter, dtype=BF16)
    band = buf(n.nx, n.prow, n.half, dtype=BF16)
    tile = buf(n.ny, n.prow, 128, dtype=BF16)
    small = buf(n.chips, n.krow, 128)
    grads = pl.pallas_call(
        functools.partial(module_kernel, n, scale),
        out_shape=(
            jax.ShapeDtypeStruct((n.rows, n.ch), BF16),
            jax.ShapeDtypeStruct((n.shard, n.ch), BF16),
            jax.ShapeDtypeStruct((KROWS, n.ch), F32),
        ),
        in_specs=[vmem, smem, hbm, hbm, hbm, vmem, vmem, vmem],
        out_specs=(hbm, vmem, vmem),
        scratch_shapes=[
            buf(n.rows, n.ch, dtype=BF16), buf(n.rows, n.ch, dtype=BF16),
            blocks, blocks, label, label, buf(16 * n.nb, 128), buf(n.nz, n.shard, n.ch, dtype=BF16),
            buf(4 * n.rows, lanes, dtype=BF16), buf(4 * n.padded, lanes, dtype=BF16), buf(4, lanes, n.padded, dtype=BF16),
            plane, plane, plane, plane, plane, buf(n.padded, 128), buf(n.padded, n.ch, dtype=BF16),
            buf(n.tiles, n.padded, 128, dtype=BF16), buf(TAPS, 8, 128), buf(2, n.kall, 128),
            buf(n.padded, n.ch, dtype=BF16), buf(n.ch, 2 * n.rows, dtype=BF16), buf(n.rows, n.ch, dtype=BF16),
            buf(2 * n.rows, n.half, dtype=BF16), buf(n.rows, n.half, dtype=BF16),
            buf(n.nz, n.shard, n.half), ring, ring, ring, ring, blocks, blocks,
            band, band, buf(n.ltiles, n.prow, 128), tile, tile, tile, band, band,
            buf(n.kall, 128), small, buf(n.nz, n.krow, 128), small, small,
            pltpu.SemaphoreType.DMA((4,)), *dma(1), *dma(1), *dma(n.groups),
            *dma(2 * far), *dma(2 * far), *dma(1), *dma(5),
            *dma(2 * far), *dma(2 * far),
            *dma(1), *dma(1), *dma(1), *dma(1),
            *dma(1), *dma(1), *dma(1),
        ],
        compiler_params=pltpu.CompilerParams(
            collective_id=0, has_side_effects=True, vmem_limit_bytes=VMEM_BYTES
        ),
    )(destination, utt_lengths, frames, cotangent, weight, kernel, norm_gain, norm_shift)
    return finish(n, *grads)


def solution(mesh):
    placed = (
        P(("dp", "fsdp"), None),
        P(("dp", "fsdp")),
        P(("dp", "fsdp"), None),
        P(("dp", "fsdp"), None),
        P("fsdp", None),
        P(),
        P(),
        P(),
    )
    return jax.shard_map(
        on_device,
        mesh=mesh,
        in_specs=placed,
        out_specs=(P(("dp", "fsdp"), None), P("fsdp", None), P(), P(), P()),
        check_vma=False,
    )
```

```python
import functools
import math

import jax
import jax.numpy as jnp
from jax import lax
from jax.experimental import pallas as pl
from jax.experimental.pallas import tpu as pltpu
from jax.sharding import PartitionSpec as P

EPSILON = 1e-05
MESH = pl.DeviceIdType.MESH
F32 = jnp.float32
BF16 = jnp.bfloat16
BLOCK = 4
TAPS = 31
HALO = 16
KROWS = 40
VMEM_BYTES = 56 * 1024 * 1024


class Sizes:
    def __init__(self, dp_size, fsdp_size, rows, channels, shard):
        self.nd = dp_size
        self.nz = fsdp_size
        self.rows = rows
        self.ch = channels
        self.shard = shard
        self.nb = rows // BLOCK
        self.tiles = channels // 128
        self.groups = self.tiles // 4
        self.slab = 4 * self.tiles
        self.chips = dp_size // 2
        self.half = channels // 2
        self.ltiles = self.half // 128
        self.quarter = self.half // 2
        self.nx = 4 if self.chips >= 32 else 2
        self.ny = self.chips // self.nx
        self.prow = shard // self.nx
        self.used = rows + 4 * HALO
        self.padded = self.used + 2 * HALO
        self.span = 80 if self.used % 80 == 0 else 48
        self.krow = 8 * (-(-(5 * self.ltiles) // self.chips))
        self.kall = self.krow * self.chips


def one_hot(mask):
    return jnp.where(mask, 1.0, 0.0).astype(BF16)


def dot(a, b):
    return jnp.dot(a, b, preferred_element_type=F32)


def remote(src, dst, send, recv, dp, z):
    return pltpu.make_async_remote_copy(
        src_ref=src, dst_ref=dst, send_sem=send, recv_sem=recv, device_id=(dp, z), device_id_type=MESH
    )


def await_bytes(ref, count, sem):
    part = ref.at[pl.ds(0, count)]
    pltpu.make_async_copy(part, part, sem).wait()


def padded_place(frame, ends):
    place = frame + HALO
    for end in ends:
        place = place + jnp.where(frame >= end, HALO, 0)
    return place


def module_kernel(
    n, scale,
    dest_ref, utt_ref, frames_hbm, cot_hbm, weight_hbm, taps_ref, gain_ref, shift_ref,
    frames_out, weight_out, small_out,
    frames_ref, cot_ref,
    outgoing, arrived, label_out, label_in, labels, whole, unsort, setting, taking,
    xs, filt, hidden, gf, slope, spread, actp, go, k8, kgrad, cot_pad, cot_turned, mate_cot, act_both, act_send,
    part, up_out, up_in, down_out, down_in, back, home,
    x_out, x_in, y_own, y_out, y_in, y_all, x_all, x_mate, mate_k, k_in, k_z, k_all, k_mate,
    io, b_send, b_recv, l_send, l_recv, h_send, h_recv,
    gu_send, gu_recv, gd_send, gd_recv, gm_send, gm_recv, m_send, m_recv,
    u_send, u_recv, d_send, d_recv,
    xr_send, xr_recv, yr_send, yr_recv, yg_send, yg_recv, xg_send, xg_recv,
    ka_send, ka_recv, kz_send, kz_recv, kc_send, kc_recv,
):
    dp = lax.axis_index("dp")
    z = lax.axis_index("fsdp")
    core = lax.rem(dp, 2)
    other = 1 - core
    mate = dp + 1 - 2 * core
    chip = dp // 2
    cx = chip // n.ny
    cy = lax.rem(chip, n.ny)
    far = n.nz // 2
    up = lax.rem(z + 1, n.nz)
    down = lax.rem(z + n.nz - 1, n.nz)
    hrow = n.shard // 2
    lanes = 16 * n.nb
    spans = range(n.used // n.span)
    mine = pl.ds(pl.multiple_of(core * n.half, 128), n.half)
    theirs = pl.ds(pl.multiple_of(other * n.half, 128), n.half)

    loads = [
        pltpu.make_async_copy(frames_hbm, frames_ref, io.at[0]),
        pltpu.make_async_copy(weight_hbm, whole.at[z], io.at[1]),
        pltpu.make_async_copy(cot_hbm, cot_ref, io.at[2]),
    ]
    for load in loads:
        load.start()

    barrier = pltpu.get_barrier_semaphore()

    def along_dp(step, carry):
        pl.semaphore_signal(
            barrier, inc=1, device_id=(lax.rem(dp + step, n.nd), z), device_id_type=MESH
        )
        return carry

    lax.fori_loop(1, n.nd, along_dp, 0)
    for step in range(1, n.nz):
        pl.semaphore_signal(
            barrier, inc=1, device_id=(dp, lax.rem(z + step, n.nz)), device_id_type=MESH
        )

    lane_rows = lax.broadcasted_iota(jnp.int32, (1, n.rows), 1)
    dest = dest_ref[...].reshape(1, n.nb)
    owners = dest // n.nb
    slots = dest - owners * n.nb
    owner_iota = lax.broadcasted_iota(jnp.int32, (n.nd, n.nb), 0)
    slot_of = jnp.sum(jnp.where(owner_iota == owners, slots, 0).astype(F32), axis=1, keepdims=True)
    slot_of = jnp.broadcast_to(slot_of, (n.nd, 128))
    for i in range(n.nd):
        label_out[i] = slot_of[i : i + 1]
    four = one_hot(
        lax.broadcasted_iota(jnp.int32, (n.nb, n.rows), 0)
        == lax.broadcasted_iota(jnp.int32, (n.nb, n.rows), 1) // BLOCK
    )
    wide = dot(jnp.broadcast_to(owners.astype(F32), (16, n.nb)).astype(BF16), four)[:1]
    code = wide.astype(jnp.int32) * 16 + lane_rows % BLOCK

    loads[0].wait()
    mats = [
        jnp.concatenate(
            [frames_ref[:, 128 * (4 * g + jj) : 128 * (4 * g + jj + 1)] for g in range(n.groups)], axis=1
        )
        for jj in range(4)
    ]
    chunk_rows = min(256, lanes)
    per_chunk = chunk_rows // 16

    def sort_chunk(chunk, carry):
        place = lax.broadcasted_iota(jnp.int32, (chunk_rows, n.rows), 0) + chunk * chunk_rows
        total = dot(one_hot(place == code), mats[0])
        for jj in range(1, 4):
            total = total + dot(one_hot(place == code + 4 * jj), mats[jj])
        for g in range(n.groups):
            piece = total[:, 128 * g : 128 * (g + 1)].astype(BF16).reshape(per_chunk, 16, 128)
            outgoing[pl.ds(chunk * per_chunk, per_chunk), 16 * g : 16 * (g + 1), :] = piece
        return carry

    lax.fori_loop(0, lanes // chunk_rows, sort_chunk, 0)

    loads[1].wait()
    pl.semaphore_wait(barrier, n.nd - 1 + n.nz - 1)

    hchunk = hrow // 2

    def gather_hop(way, chunk, step, block):
        send, recv, to = (gu_send, gu_recv, up) if way == 0 else (gd_send, gd_recv, down)
        rows = pl.ds(pl.multiple_of(core * hrow + chunk * hchunk, 16), hchunk)
        at = far * chunk + step
        return remote(whole.at[block, rows], whole.at[block, rows], send.at[at], recv.at[at], dp, to)

    def gather_mate(chunk, block):
        rows = pl.ds(pl.multiple_of(core * hrow + chunk * hchunk, 16), hchunk)
        return remote(whole.at[block, rows], whole.at[block, rows], gm_send.at[0], gm_recv.at[0], mate, z)

    def gather_block(way, step):
        return lax.rem(z + n.nz - step - 1, n.nz) if way == 0 else lax.rem(z + step + 1, n.nz)

    ways = ((0, 0), (1, 1), (0, 1), (1, 0))

    def ring_steps(way, chunk):
        return far if way == chunk else far - 1

    def gather_pass(step):
        for way, chunk in ways:
            if step < ring_steps(way, chunk):
                block = gather_block(way, step)
                gather_hop(way, chunk, step, block).wait_recv()
                if step + 1 < ring_steps(way, chunk):
                    gather_hop(way, chunk, step + 1, block).start()
                gather_mate(chunk, block).start()

    for way, chunk in ways:
        if ring_steps(way, chunk) > 0:
            gather_hop(way, chunk, 0, z).start()

    def block_to(peer):
        return remote(outgoing.at[peer], arrived.at[dp], b_send.at[0], b_recv.at[0], peer, z)

    def label_to(peer):
        return remote(label_out.at[peer], label_in.at[dp], l_send.at[0], l_recv.at[0], peer, z)

    def peers(body):
        def step_to(step, carry):
            body(lax.rem(dp + step, n.nd))
            return carry

        lax.fori_loop(1, n.nd, step_to, 0)

    def chips(body):
        def step_to(step, carry):
            body(lax.rem(chip + step, n.chips))
            return carry

        lax.fori_loop(1, n.chips, step_to, 0)

    def send_block(peer):
        label_to(peer).start()
        block_to(peer).start()

    peers(send_block)
    loads[2].wait()
    swap_cot = remote(cot_ref, mate_cot, m_send.at[0], m_recv.at[0], mate, z)
    swap_cot.start()
    arrived[dp] = outgoing[dp]
    label_in[dp] = label_out[dp]

    ends = [utt_ref[0, 0]]
    for i in range(1, 3):
        ends.append(ends[-1] + utt_ref[0, i])
    frame_row = padded_place(lane_rows, ends)
    pad_mat = one_hot(lax.broadcasted_iota(jnp.int32, (n.padded, n.rows), 0) == frame_row)
    cot_pad[...] = dot(pad_mat, cot_ref[...]).astype(BF16)
    cot_turned[:, : n.rows] = cot_ref[...].T
    kgrad[...] = jnp.zeros_like(kgrad)
    actp[...] = jnp.zeros_like(actp)
    go[...] = jnp.zeros_like(go)
    gf[:, :HALO, :] = jnp.zeros((n.tiles, HALO, 128), F32)
    gf[:, n.padded - HALO :, :] = jnp.zeros((n.tiles, HALO, 128), F32)
    sub_rows = lax.broadcasted_iota(jnp.int32, (n.rows, 1), 0)
    near = lax.broadcasted_iota(jnp.int32, (n.rows, n.nb), 1) == sub_rows // BLOCK
    code_col = jnp.sum(jnp.where(near, owners, 0).astype(F32), axis=1, keepdims=True)
    code_col = code_col.astype(jnp.int32) * 16 + sub_rows % BLOCK
    order = lax.broadcasted_iota(jnp.int32, (n.rows, lanes), 1)
    for jj in range(4):
        unsort[n.rows * jj : n.rows * (jj + 1)] = one_hot(order == code_col + 4 * jj)
    swap_cot.wait_recv()
    cot_turned[:, n.rows :] = mate_cot[...].T

    if far > 1:
        gather_pass(0)

    await_bytes(label_in, n.nd - 1, l_recv.at[0])
    lane128 = lax.broadcasted_iota(jnp.int32, (1, 128), 1)
    chunks = []
    for q in range(n.nb // 8):
        row = jnp.zeros((1, 128), F32)
        for s in range(8):
            row = row + jnp.where(lane128 // 16 == s, label_in[8 * q + s], 0.0)
        chunks.append(row)
    slot_row = jnp.concatenate(chunks, axis=1).astype(jnp.int32)
    lane_all = lax.broadcasted_iota(jnp.int32, (1, lanes), 1)
    place_row = padded_place(slot_row * BLOCK + lane_all % 4, ends)

    def lay_label(src, carry):
        labels[pl.ds(pl.multiple_of(16 * src, 16), 16), :] = jnp.broadcast_to(label_in[src], (16, 128))
        return carry

    lax.fori_loop(0, n.nb, lay_label, 0)

    row_iota = lax.broadcasted_iota(jnp.int32, (n.padded, lanes), 0)

    def setter(jj, carry):
        mask = row_iota == jnp.where((lane_all // 4) % 4 == jj, place_row, -1)
        setting[pl.ds(pl.multiple_of(jj * n.padded, 16), n.padded), :] = one_hot(mask)
        return carry

    lax.fori_loop(0, 4, setter, 0)

    def taker(chunk, carry):
        at = pl.ds(pl.multiple_of(chunk * chunk_rows, chunk_rows), chunk_rows)
        slot = labels[at, :][:, :1].astype(jnp.int32)
        sub = lax.broadcasted_iota(jnp.int32, (chunk_rows, 1), 0)
        place = padded_place(slot * BLOCK + sub % 4, ends)
        cols = lax.broadcasted_iota(jnp.int32, (chunk_rows, n.padded), 1)
        for jj in range(4):
            taking[jj, at, :] = one_hot(cols == jnp.where((sub // 4) % 4 == jj, place, -1))
        return carry

    lax.fori_loop(0, lanes // chunk_rows, taker, 0)

    if far > 2:
        gather_pass(1)

    await_bytes(arrived, n.nd - 1, b_recv.at[0])
    blocks = jnp.concatenate(
        [arrived[:, 16 * g : 16 * (g + 1), :].reshape(lanes, 128) for g in range(n.groups)], axis=1
    )

    def put(jj, carry):
        owned = dot(setting[pl.ds(pl.multiple_of(jj * n.padded, 16), n.padded), :], blocks)
        for g in range(n.groups):
            xs[4 * g + jj] = owned[:, 128 * g : 128 * (g + 1)]
        return carry

    lax.fori_loop(0, 4, put, 0)

    for step in range(2, far - 1):
        gather_pass(step)

    def filter_tile(j, carry):
        taps = taps_ref[:, pl.ds(pl.multiple_of(j * 128, 128), 128)]
        for b in spans:
            base = 1 + n.span * b
            total = jnp.zeros((n.span, 128), F32)
            for s in range(8):
                window = xs[j, base + s : base + s + n.span + 24, :]
                for m in range(4):
                    k = s + 8 * m
                    if k < TAPS:
                        total = total + taps[k : k + 1] * window[8 * m : 8 * m + n.span]
            filt[j, HALO + n.span * b : HALO + n.span * (b + 1), :] = total
        return carry

    lax.fori_loop(0, n.tiles, filter_tile, 0)

    def norm_span(b, carry):
        rows = pl.ds(pl.multiple_of(HALO + n.span * b, 16), n.span)
        total = filt[0, rows, :]
        for j in range(1, n.tiles):
            total = total + filt[j, rows, :]
        mean = jnp.sum(total, axis=1, keepdims=True) * (1.0 / n.ch)
        square = jnp.zeros((n.span, 128), F32)
        for j in range(n.tiles):
            centred = filt[j, rows, :] - mean
            square = square + centred * centred
        variance = jnp.sum(square, axis=1, keepdims=True) * (1.0 / n.ch)
        inverse = 1.0 / jnp.sqrt(variance + EPSILON)
        spread[rows, :] = jnp.broadcast_to(inverse, (n.span, 128))
        for j in range(n.tiles):
            whitened = (filt[j, rows, :] - mean) * inverse
            normed = whitened * gain_ref[128 * j : 128 * (j + 1)].reshape(1, 128) + shift_ref[128 * j : 128 * (j + 1)].reshape(1, 128)
            logistic = 1.0 / (1.0 + jnp.exp(-normed))
            activated = normed * logistic
            actp[rows, 128 * j : 128 * (j + 1)] = activated.astype(BF16)
            filt[j, rows, :] = whitened
            slope[j, rows, :] = logistic * (1.0 + normed * (1.0 - logistic))
        return carry

    lax.fori_loop(0, n.used // n.span, norm_span, 0)

    frame_col = padded_place(lax.broadcasted_iota(jnp.int32, (n.rows, 1), 0), ends)
    take = one_hot(lax.broadcasted_iota(jnp.int32, (n.rows, n.padded), 1) == frame_col)
    act_send[...] = dot(take, actp[:, theirs]).astype(BF16)
    swap_act = remote(act_send, act_both.at[pl.ds(n.rows, n.rows)], m_send.at[1], m_recv.at[1], mate, z)
    swap_act.start()
    act_both[: n.rows] = dot(take, actp[:, mine]).astype(BF16)

    def product(target):
        part[target] = dot(cot_turned[pl.ds(pl.multiple_of(target * n.shard, 16), n.shard), :], act_both[...])

    def product_of(target, core_rows):
        rows = pl.ds(pl.multiple_of(target * n.shard, 16), n.shard)
        return dot(cot_turned[rows, core_rows], act_both[core_rows, :])

    chunk_of = [slice(0, n.quarter), slice(n.quarter, n.half)]

    def ring_hop(way, chunk, step):
        out, into, send, recv, to = (
            (up_out, up_in, u_send, u_recv, up) if way == 0 else (down_out, down_in, d_send, d_recv, down)
        )
        at = far * chunk + step
        return remote(out.at[chunk, step], into.at[chunk, step], send.at[at], recv.at[at], dp, to)

    def ring_target(way, chunk, step):
        ahead = (far if way == chunk else far - 1) - step
        return lax.rem(z + ahead, n.nz) if way == 0 else lax.rem(z + n.nz - ahead, n.nz)

    def ring_step(step):
        for way, chunk in ways:
            if step < ring_steps(way, chunk):
                out, into = (up_out, up_in) if way == 0 else (down_out, down_in)
                value = part[ring_target(way, chunk, step), :, chunk_of[chunk]]
                if step > 0:
                    ring_hop(way, chunk, step - 1).wait_recv()
                    value = value + into[chunk, step - 1].astype(F32)
                out[chunk, step] = value.astype(BF16)
                ring_hop(way, chunk, step).start()

    first = [lax.rem(z + far, n.nz)]
    if far > 1:
        first += [lax.rem(z + far - 1, n.nz), lax.rem(z + n.nz - far + 1, n.nz)]
    for target in first:
        part[target] = product_of(target, slice(0, n.rows))
    swap_act.wait_recv()
    for target in first:
        part[target] += product_of(target, slice(n.rows, 2 * n.rows))
    ring_step(0)

    gather_pass(far - 1)
    await_bytes(whole.at[:, pl.ds(0, hrow)], n.nz - 1, gm_recv.at[0])
    width = 512
    per = width // 128

    def project(i, carry):
        cols = pl.ds(pl.multiple_of(i * width, width), width)
        piece = dot(cot_pad[...], whole[:, :, cols].reshape(n.ch, width))
        for q in range(per):
            hidden[per * i + q] = piece[:, 128 * q : 128 * (q + 1)]
        return carry

    lax.fori_loop(0, n.ch // width, project, 0)

    def norm_back(b, carry):
        rows = pl.ds(pl.multiple_of(HALO + n.span * b, 16), n.span)
        first = jnp.zeros((n.span, 128), F32)
        second = jnp.zeros((n.span, 128), F32)
        for j in range(n.tiles):
            whitened = filt[j, rows, :]
            grad_normed = hidden[j, rows, :] * slope[j, rows, :]
            scaled = grad_normed * gain_ref[128 * j : 128 * (j + 1)].reshape(1, 128)
            hidden[j, rows, :] = scaled
            first = first + scaled
            second = second + scaled * whitened
            half, at = j // n.ltiles, (j % n.ltiles) * KROWS
            kgrad[half, at + TAPS : at + TAPS + 1, :] += jnp.sum(grad_normed * whitened, axis=0, keepdims=True)
            kgrad[half, at + TAPS + 1 : at + TAPS + 2, :] += jnp.sum(grad_normed, axis=0, keepdims=True)
        mean1 = jnp.sum(first, axis=1, keepdims=True) * (1.0 / n.ch)
        mean2 = jnp.sum(second, axis=1, keepdims=True) * (1.0 / n.ch)
        inverse = spread[rows, :]
        for j in range(n.tiles):
            gf[j, rows, :] = inverse * (hidden[j, rows, :] - mean1 - filt[j, rows, :] * mean2)
        return carry

    lax.fori_loop(0, n.used // n.span, norm_back, 0)

    def products(i, carry):
        product(lax.rem(z + n.nz - far + 2 + i, n.nz))
        return carry

    if far > 1:
        lax.fori_loop(0, n.nz - 3, products, 0)
    else:
        product(z)

    def back_tile(j, carry):
        taps = taps_ref[:, pl.ds(pl.multiple_of(j * 128, 128), 128)]
        for b in spans:
            base = 1 + n.span * b
            here = slice(HALO + n.span * b, HALO + n.span * (b + 1))
            signal = xs[j, here, :]
            total = jnp.zeros((n.span, 128), F32)
            for s in range(8):
                window = gf[j, base + s : base + s + n.span + 24, :]
                for m in range(4):
                    k = TAPS - 1 - s - 8 * m
                    if k >= 0:
                        shifted = window[8 * m : 8 * m + n.span]
                        total = total + taps[k : k + 1] * shifted
                        product = jnp.sum((shifted * signal).reshape(n.span // 8, 8, 128), axis=0)
                        if b == 0:
                            k8[k] = product
                        else:
                            k8[k] += product
            go[j, here, :] = total.astype(BF16)
        at = pl.multiple_of(lax.rem(j, n.ltiles) * KROWS, 8)
        kgrad[j // n.ltiles, pl.ds(at, TAPS), :] = jnp.sum(k8[...], axis=1)
        return carry

    def home_to(peer, group):
        rows = pl.ds(16 * group, 16)
        return remote(
            back.at[peer, rows], home.at[dp, rows], h_send.at[group], h_recv.at[group], peer, z
        )

    def k_rows(at):
        return pl.ds(pl.multiple_of(at * n.krow, 8), n.krow)

    def k_scatter(at, slot):
        return remote(mate_k.at[k_rows(at)], k_in.at[slot], ka_send.at[0], ka_recv.at[0], 2 * at + core, z)

    def k_over_z(slot, to):
        return remote(k_z.at[z], k_z.at[slot], kz_send.at[0], kz_recv.at[0], dp, to)

    def k_gather(slot, to):
        return remote(k_all.at[slot], k_all.at[slot], kc_send.at[0], kc_recv.at[0], 2 * to + core, z)

    swap_k = remote(kgrad.at[other], mate_k, m_send.at[2], m_recv.at[2], mate, z)
    for group in range(n.groups):
        lax.fori_loop(4 * group, 4 * group + 4, back_tile, 0)
        if group == n.groups - 1:
            swap_k.start()
        if group + 1 < far:
            ring_step(group + 1)

        def gather_chunk(chunk, carry):
            at = pl.ds(pl.multiple_of(chunk * chunk_rows, chunk_rows), chunk_rows)
            total = dot(taking[0, at, :], go[4 * group])
            for jj in range(1, 4):
                total = total + dot(taking[jj, at, :], go[4 * group + jj])
            piece = total.astype(BF16).reshape(per_chunk, 16, 128)
            back[pl.ds(chunk * per_chunk, per_chunk), 16 * group : 16 * (group + 1), :] = piece
            return carry

        lax.fori_loop(0, lanes // chunk_rows, gather_chunk, 0)
        if group == n.groups - 1:
            swap_k.wait_recv()
            mate_k[...] += kgrad[core]
            chips(lambda at: k_scatter(at, chip).start())
        peers(lambda peer: home_to(peer, group).start())
    home[dp] = back[dp]


    for step in range(n.groups + 1, far):
        ring_step(step)

    await_bytes(k_in, n.chips - 1, ka_recv.at[0])
    k_in[chip] = mate_k[k_rows(chip), :]

    def k_sum(step, carry):
        return carry + k_in[lax.rem(chip + step, n.chips)]

    k_z[z] = lax.fori_loop(1, n.chips, k_sum, k_in[chip])
    for hop in range(1, n.nz):
        k_over_z(z, lax.rem(z + hop, n.nz)).start()

    for way, chunk in ((1, 0), (0, 1), (0, 0), (1, 1)):
        steps = ring_steps(way, chunk)
        if steps > 0:
            into = up_in if way == 0 else down_in
            ring_hop(way, chunk, steps - 1).wait_recv()
            part[z, :, chunk_of[chunk]] += into[chunk, steps - 1].astype(F32)

    def along_x(step):
        there = lax.rem(cx + step, n.nx)
        return there, (there * n.ny + cy) * 2 + core

    def along_y(step):
        there = lax.rem(cy + step, n.ny)
        return there, (cx * n.ny + there) * 2 + core

    def x_scatter(step):
        there, peer = along_x(step)
        return remote(x_out.at[there], x_in.at[cx], xr_send.at[0], xr_recv.at[0], peer, z)

    def y_scatter(step):
        there, peer = along_y(step)
        return there, remote(y_out.at[there], y_in.at[cy], yr_send.at[0], yr_recv.at[0], peer, z)

    def y_gather(step):
        there, peer = along_y(step)
        return remote(y_all.at[cy], y_all.at[cy], yg_send.at[0], yg_recv.at[0], peer, z)

    def x_gather(step):
        there, peer = along_x(step)
        return remote(x_all.at[cx], x_all.at[cx], xg_send.at[0], xg_recv.at[0], peer, z)

    for i in range(n.nx):
        x_out[i] = part[z, n.prow * i : n.prow * (i + 1), :].astype(BF16)
    for step in range(1, n.nx):
        x_scatter(step).start()

    await_bytes(k_z, n.nz - 1, kz_recv.at[0])
    small = k_z[0]
    for i in range(1, n.nz):
        small = small + k_z[i]
    k_all[chip] = small * scale
    chips(lambda at: k_gather(chip, at).start())

    band = part[z, pl.ds(pl.multiple_of(cx * n.prow, 16), n.prow), :]
    await_bytes(x_in, n.nx - 1, xr_recv.at[0])
    for step in range(1, n.nx):
        band = band + x_in[lax.rem(cx + step, n.nx)].astype(F32)
    for l in range(n.ltiles):
        y_own[l] = band[:, 128 * l : 128 * (l + 1)]
        y_out[l] = band[:, 128 * l : 128 * (l + 1)].astype(BF16)
    for step in range(1, n.ny):
        there, copy = y_scatter(step)

        @pl.when(there < n.ltiles)
        def _():
            copy.start()

    @pl.when(cy < n.ltiles)
    def _():
        await_bytes(y_in, n.ny - 1, yr_recv.at[0])
        total = y_own[cy]
        for step in range(1, n.ny):
            total = total + y_in[lax.rem(cy + step, n.ny)].astype(F32)
        y_all[cy] = (total * scale).astype(BF16)
        for step in range(1, n.ny):
            y_gather(step).start()

    def others_along_y(ref, sem):
        @pl.when(cy < n.ltiles)
        def _():
            await_bytes(ref, n.ltiles - 1, sem)

        @pl.when(cy >= n.ltiles)
        def _():
            await_bytes(ref, n.ltiles, sem)

    others_along_y(y_all, yg_recv.at[0])

    for l in range(n.ltiles):
        x_all[cx, :, 128 * l : 128 * (l + 1)] = y_all[l]
    for step in range(1, n.nx):
        x_gather(step).start()

    await_bytes(k_all, n.chips - 1, kc_recv.at[0])
    swap_all = remote(k_all, k_mate, m_send.at[3], m_recv.at[3], mate, z)
    swap_all.start()

    def unsort_group(group):
        rows = slice(16 * group, 16 * (group + 1))
        await_bytes(home.at[:, pl.ds(16 * group, 16)], n.nd - 1, h_recv.at[group])
        block = home[:, rows, :].reshape(lanes, 128)
        for jj in range(4):
            tile = 4 * group + jj
            found = dot(unsort[n.rows * jj : n.rows * (jj + 1)], block).astype(BF16)
            frames_ref[:, 128 * tile : 128 * (tile + 1)] = found

    for group in range(n.groups - 1):
        unsort_group(group)
    await_bytes(x_all, n.nx - 1, xg_recv.at[0])
    swap_weight = remote(x_all, x_mate, m_send.at[4], m_recv.at[4], mate, z)
    swap_weight.start()

    def lay_weight(source, half):
        cols = pl.ds(pl.multiple_of(half * n.half, 128), n.half)
        for i in range(n.nx):
            weight_out[n.prow * i : n.prow * (i + 1), cols] = source[i]

    def lay_small(source, half):
        rows = source[...].reshape(n.kall, 128)
        for l in range(n.ltiles):
            cols = pl.ds(pl.multiple_of(half * n.half + 128 * l, 128), 128)
            small_out[:, cols] = rows[KROWS * l : KROWS * (l + 1)]

    unsort_group(n.groups - 1)
    store = pltpu.make_async_copy(frames_ref, frames_out, io.at[3])
    store.start()
    lay_weight(x_all, core)
    lay_small(k_all, core)

    swap_all.wait_recv()
    lay_small(k_mate, other)
    swap_weight.wait_recv()
    lay_weight(x_mate, other)

    for copy in (swap_cot, swap_act, swap_k, swap_all, swap_weight):
        copy.wait_send()
    for step in range(far):
        for way, chunk in ways:
            if step < ring_steps(way, chunk):
                gather_hop(way, chunk, step, z).wait_send()
    for way in range(2):
        for chunk in range(2):
            for step in range(ring_steps(way, chunk)):
                ring_hop(way, chunk, step).wait_send()
    await_bytes(x_in, n.nx - 1, xr_send.at[0])
    await_bytes(x_all, n.nx - 1, xg_send.at[0])
    others_along_y(y_out, yr_send.at[0])

    @pl.when(cy < n.ltiles)
    def _():
        await_bytes(y_all, n.ny - 1, yg_send.at[0])

    await_bytes(whole.at[:, pl.ds(0, hrow)], n.nz - 1, gm_send.at[0])
    await_bytes(k_z, n.nz - 1, kz_send.at[0])
    await_bytes(k_in, n.chips - 1, ka_send.at[0])
    await_bytes(k_all, n.chips - 1, kc_send.at[0])
    await_bytes(label_out, n.nd - 1, l_send.at[0])
    await_bytes(outgoing, n.nd - 1, b_send.at[0])
    for group in range(n.groups):
        await_bytes(back.at[:, pl.ds(16 * group, 16)], n.nd - 1, h_send.at[group])
    store.wait()


def finish_kernel(
    n, frames_hbm, weight_ref, small_ref, frames_out, weight_out, taps_out, gain_out, shift_out, sem
):
    copy = pltpu.make_async_copy(frames_hbm, frames_out, sem)
    copy.start()
    weight_out[...] = weight_ref[...].astype(F32)
    taps_out[...] = small_ref[:TAPS]
    gain_out[...] = small_ref[TAPS : TAPS + 1].reshape(n.ch)
    shift_out[...] = small_ref[TAPS + 1 : TAPS + 2].reshape(n.ch)
    copy.wait()


def finish(n, frames, weight, small):
    vmem = pl.BlockSpec(memory_space=pltpu.VMEM)
    hbm = pl.BlockSpec(memory_space=pl.ANY)
    return pl.pallas_call(
        functools.partial(finish_kernel, n),
        out_shape=(
            jax.ShapeDtypeStruct((n.rows, n.ch), BF16),
            jax.ShapeDtypeStruct((n.shard, n.ch), F32),
            jax.ShapeDtypeStruct((TAPS, n.ch), F32),
            jax.ShapeDtypeStruct((n.ch,), F32),
            jax.ShapeDtypeStruct((n.ch,), F32),
        ),
        in_specs=[hbm, vmem, vmem],
        out_specs=(hbm, vmem, vmem, vmem, vmem),
        scratch_shapes=[pltpu.SemaphoreType.DMA],
    )(frames, weight, small)


def on_device(frames, destination, utt_lengths, cotangent, weight, kernel, norm_gain, norm_shift):
    n = Sizes(lax.axis_size("dp"), lax.axis_size("fsdp"), frames.shape[0], frames.shape[1], weight.shape[0])
    scale = 1.0 / math.sqrt(n.rows * n.nd * n.nz)
    far = n.nz // 2
    lanes = 16 * n.nb
    vmem = pl.BlockSpec(memory_space=pltpu.VMEM)
    smem = pl.BlockSpec(memory_space=pltpu.SMEM)
    hbm = pl.BlockSpec(memory_space=pl.ANY)

    def dma(count):
        return [pltpu.SemaphoreType.DMA((count,))] * 2

    def buf(*shape, dtype=F32):
        return pltpu.VMEM(shape, dtype)

    blocks = buf(n.nb, n.slab, 128, dtype=BF16)
    label = buf(n.nd, 1, 128)
    plane = buf(n.tiles, n.padded, 128)
    ring = buf(2, far, n.shard, n.quarter, dtype=BF16)
    band = buf(n.nx, n.prow, n.half, dtype=BF16)
    tile = buf(n.ny, n.prow, 128, dtype=BF16)
    small = buf(n.chips, n.krow, 128)
    grads = pl.pallas_call(
        functools.partial(module_kernel, n, scale),
        out_shape=(
            jax.ShapeDtypeStruct((n.rows, n.ch), BF16),
            jax.ShapeDtypeStruct((n.shard, n.ch), BF16),
            jax.ShapeDtypeStruct((KROWS, n.ch), F32),
        ),
        in_specs=[vmem, smem, hbm, hbm, hbm, vmem, vmem, vmem],
        out_specs=(hbm, vmem, vmem),
        scratch_shapes=[
            buf(n.rows, n.ch, dtype=BF16), buf(n.rows, n.ch, dtype=BF16),
            blocks, blocks, label, label, buf(16 * n.nb, 128), buf(n.nz, n.shard, n.ch, dtype=BF16),
            buf(4 * n.rows, lanes, dtype=BF16), buf(4 * n.padded, lanes, dtype=BF16), buf(4, lanes, n.padded, dtype=BF16),
            plane, plane, plane, plane, plane, buf(n.padded, 128), buf(n.padded, n.ch, dtype=BF16),
            buf(n.tiles, n.padded, 128, dtype=BF16), buf(TAPS, 8, 128), buf(2, n.kall, 128),
            buf(n.padded, n.ch, dtype=BF16), buf(n.ch, 2 * n.rows, dtype=BF16), buf(n.rows, n.ch, dtype=BF16),
            buf(2 * n.rows, n.half, dtype=BF16), buf(n.rows, n.half, dtype=BF16),
            buf(n.nz, n.shard, n.half), ring, ring, ring, ring, blocks, blocks,
            band, band, buf(n.ltiles, n.prow, 128), tile, tile, tile, band, band,
            buf(n.kall, 128), small, buf(n.nz, n.krow, 128), small, small,
            pltpu.SemaphoreType.DMA((4,)), *dma(1), *dma(1), *dma(n.groups),
            *dma(2 * far), *dma(2 * far), *dma(1), *dma(5),
            *dma(2 * far), *dma(2 * far),
            *dma(1), *dma(1), *dma(1), *dma(1),
            *dma(1), *dma(1), *dma(1),
        ],
        compiler_params=pltpu.CompilerParams(
            collective_id=0, has_side_effects=True, vmem_limit_bytes=VMEM_BYTES
        ),
    )(destination, utt_lengths, frames, cotangent, weight, kernel, norm_gain, norm_shift)
    return finish(n, *grads)


def solution(mesh):
    placed = (
        P(("dp", "fsdp"), None),
        P(("dp", "fsdp")),
        P(("dp", "fsdp"), None),
        P(("dp", "fsdp"), None),
        P("fsdp", None),
        P(),
        P(),
        P(),
    )
    return jax.shard_map(
        on_device,
        mesh=mesh,
        in_specs=placed,
        out_specs=(P(("dp", "fsdp"), None), P("fsdp", None), P(), P(), P()),
        check_vma=False,
    )
```

```python
import functools
import math

import jax
import jax.numpy as jnp
from jax import lax
from jax.experimental import pallas as pl
from jax.experimental.pallas import tpu as pltpu
from jax.sharding import PartitionSpec as P

EPSILON = 1e-05
MESH = pl.DeviceIdType.MESH
F32 = jnp.float32
BF16 = jnp.bfloat16
BLOCK = 4
TAPS = 31
HALO = 16
KROWS = 40
VMEM_BYTES = 56 * 1024 * 1024


class Sizes:
    def __init__(self, dp_size, fsdp_size, rows, channels, shard):
        self.nd = dp_size
        self.nz = fsdp_size
        self.rows = rows
        self.ch = channels
        self.shard = shard
        self.nb = rows // BLOCK
        self.tiles = channels // 128
        self.groups = self.tiles // 4
        self.slab = 4 * self.tiles
        self.chips = dp_size // 2
        self.half = channels // 2
        self.ltiles = self.half // 128
        self.quarter = self.half // 2
        self.nx = 4 if self.chips >= 32 else 2
        self.ny = self.chips // self.nx
        self.prow = shard // self.nx
        self.used = rows + 4 * HALO
        self.padded = self.used + 2 * HALO
        self.span = 80 if self.used % 80 == 0 else 48
        self.krow = 8 * (-(-(5 * self.ltiles) // self.chips))
        self.kall = self.krow * self.chips


def one_hot(mask):
    return jnp.where(mask, 1.0, 0.0).astype(BF16)


def dot(a, b):
    return jnp.dot(a, b, preferred_element_type=F32)


def remote(src, dst, send, recv, dp, z):
    return pltpu.make_async_remote_copy(
        src_ref=src, dst_ref=dst, send_sem=send, recv_sem=recv, device_id=(dp, z), device_id_type=MESH
    )


def await_bytes(ref, count, sem):
    part = ref.at[pl.ds(0, count)]
    pltpu.make_async_copy(part, part, sem).wait()


def padded_place(frame, ends):
    place = frame + HALO
    for end in ends:
        place = place + jnp.where(frame >= end, HALO, 0)
    return place


def module_kernel(
    n, scale,
    dest_ref, utt_ref, frames_hbm, cot_hbm, weight_hbm, taps_ref, gain_ref, shift_ref,
    frames_out, weight_out, small_out,
    frames_ref, cot_ref,
    outgoing, arrived, label_out, label_in, labels, whole, unsort, setting, taking,
    xs, filt, hidden, gf, slope, spread, actp, go, k8, kgrad, cot_pad, cot_turned, mate_cot, act_both, act_send,
    part, up_out, up_in, down_out, down_in, back, home,
    x_out, x_in, y_own, y_out, y_in, y_all, x_all, x_mate, mate_k, k_in, k_z, k_all, k_mate,
    io, b_send, b_recv, l_send, l_recv, h_send, h_recv,
    gu_send, gu_recv, gd_send, gd_recv, gm_send, gm_recv, m_send, m_recv,
    u_send, u_recv, d_send, d_recv,
    xr_send, xr_recv, yr_send, yr_recv, yg_send, yg_recv, xg_send, xg_recv,
    ka_send, ka_recv, kz_send, kz_recv, kc_send, kc_recv,
):
    dp = lax.axis_index("dp")
    z = lax.axis_index("fsdp")
    core = lax.rem(dp, 2)
    other = 1 - core
    mate = dp + 1 - 2 * core
    chip = dp // 2
    cx = chip // n.ny
    cy = lax.rem(chip, n.ny)
    far = n.nz // 2
    up = lax.rem(z + 1, n.nz)
    down = lax.rem(z + n.nz - 1, n.nz)
    hrow = n.shard // 2
    lanes = 16 * n.nb
    spans = range(n.used // n.span)
    mine = pl.ds(pl.multiple_of(core * n.half, 128), n.half)
    theirs = pl.ds(pl.multiple_of(other * n.half, 128), n.half)

    loads = [
        pltpu.make_async_copy(frames_hbm, frames_ref, io.at[0]),
        pltpu.make_async_copy(weight_hbm, whole.at[z], io.at[1]),
        pltpu.make_async_copy(cot_hbm, cot_ref, io.at[2]),
    ]
    for load in loads:
        load.start()

    barrier = pltpu.get_barrier_semaphore()

    def along_dp(step, carry):
        pl.semaphore_signal(
            barrier, inc=1, device_id=(lax.rem(dp + step, n.nd), z), device_id_type=MESH
        )
        return carry

    lax.fori_loop(1, n.nd, along_dp, 0)
    for step in range(1, n.nz):
        pl.semaphore_signal(
            barrier, inc=1, device_id=(dp, lax.rem(z + step, n.nz)), device_id_type=MESH
        )

    lane_rows = lax.broadcasted_iota(jnp.int32, (1, n.rows), 1)
    dest = dest_ref[...].reshape(1, n.nb)
    owners = dest // n.nb
    slots = dest - owners * n.nb
    owner_iota = lax.broadcasted_iota(jnp.int32, (n.nd, n.nb), 0)
    slot_of = jnp.sum(jnp.where(owner_iota == owners, slots, 0).astype(F32), axis=1, keepdims=True)
    slot_of = jnp.broadcast_to(slot_of, (n.nd, 128))
    for i in range(n.nd):
        label_out[i] = slot_of[i : i + 1]
    four = one_hot(
        lax.broadcasted_iota(jnp.int32, (n.nb, n.rows), 0)
        == lax.broadcasted_iota(jnp.int32, (n.nb, n.rows), 1) // BLOCK
    )
    wide = dot(jnp.broadcast_to(owners.astype(F32), (16, n.nb)).astype(BF16), four)[:1]
    code = wide.astype(jnp.int32) * 16 + lane_rows % BLOCK

    loads[0].wait()
    mats = [
        jnp.concatenate(
            [frames_ref[:, 128 * (4 * g + jj) : 128 * (4 * g + jj + 1)] for g in range(n.groups)], axis=1
        )
        for jj in range(4)
    ]
    chunk_rows = min(256, lanes)
    per_chunk = chunk_rows // 16

    def sort_chunk(chunk, carry):
        place = lax.broadcasted_iota(jnp.int32, (chunk_rows, n.rows), 0) + chunk * chunk_rows
        total = dot(one_hot(place == code), mats[0])
        for jj in range(1, 4):
            total = total + dot(one_hot(place == code + 4 * jj), mats[jj])
        for g in range(n.groups):
            piece = total[:, 128 * g : 128 * (g + 1)].astype(BF16).reshape(per_chunk, 16, 128)
            outgoing[pl.ds(chunk * per_chunk, per_chunk), 16 * g : 16 * (g + 1), :] = piece
        return carry

    lax.fori_loop(0, lanes // chunk_rows, sort_chunk, 0)

    loads[1].wait()
    pl.semaphore_wait(barrier, n.nd - 1 + n.nz - 1)

    hchunk = hrow // 2

    def gather_hop(way, chunk, step, block):
        send, recv, to = (gu_send, gu_recv, up) if way == 0 else (gd_send, gd_recv, down)
        rows = pl.ds(pl.multiple_of(core * hrow + chunk * hchunk, 16), hchunk)
        at = far * chunk + step
        return remote(whole.at[block, rows], whole.at[block, rows], send.at[at], recv.at[at], dp, to)

    def gather_mate(chunk, block):
        rows = pl.ds(pl.multiple_of(core * hrow + chunk * hchunk, 16), hchunk)
        return remote(whole.at[block, rows], whole.at[block, rows], gm_send.at[0], gm_recv.at[0], mate, z)

    def gather_block(way, step):
        return lax.rem(z + n.nz - step - 1, n.nz) if way == 0 else lax.rem(z + step + 1, n.nz)

    ways = ((0, 0), (1, 1), (0, 1), (1, 0))

    def ring_steps(way, chunk):
        return far if way == chunk else far - 1

    def gather_pass(step):
        for way, chunk in ways:
            if step < ring_steps(way, chunk):
                block = gather_block(way, step)
                gather_hop(way, chunk, step, block).wait_recv()
                if step + 1 < ring_steps(way, chunk):
                    gather_hop(way, chunk, step + 1, block).start()
                gather_mate(chunk, block).start()

    for way, chunk in ways:
        if ring_steps(way, chunk) > 0:
            gather_hop(way, chunk, 0, z).start()

    def block_to(peer):
        return remote(outgoing.at[peer], arrived.at[dp], b_send.at[0], b_recv.at[0], peer, z)

    def label_to(peer):
        return remote(label_out.at[peer], label_in.at[dp], l_send.at[0], l_recv.at[0], peer, z)

    def peers(body):
        def step_to(step, carry):
            body(lax.rem(dp + step, n.nd))
            return carry

        lax.fori_loop(1, n.nd, step_to, 0)

    def chips(body):
        def step_to(step, carry):
            body(lax.rem(chip + step, n.chips))
            return carry

        lax.fori_loop(1, n.chips, step_to, 0)

    def send_block(peer):
        label_to(peer).start()
        block_to(peer).start()

    peers(send_block)
    loads[2].wait()
    swap_cot = remote(cot_ref, mate_cot, m_send.at[0], m_recv.at[0], mate, z)
    swap_cot.start()
    arrived[dp] = outgoing[dp]
    label_in[dp] = label_out[dp]

    ends = [utt_ref[0, 0]]
    for i in range(1, 3):
        ends.append(ends[-1] + utt_ref[0, i])
    frame_row = padded_place(lane_rows, ends)
    pad_mat = one_hot(lax.broadcasted_iota(jnp.int32, (n.padded, n.rows), 0) == frame_row)
    cot_pad[...] = dot(pad_mat, cot_ref[...]).astype(BF16)
    cot_turned[:, : n.rows] = cot_ref[...].T
    kgrad[...] = jnp.zeros_like(kgrad)
    actp[...] = jnp.zeros_like(actp)
    go[...] = jnp.zeros_like(go)
    gf[:, :HALO, :] = jnp.zeros((n.tiles, HALO, 128), F32)
    gf[:, n.padded - HALO :, :] = jnp.zeros((n.tiles, HALO, 128), F32)
    sub_rows = lax.broadcasted_iota(jnp.int32, (n.rows, 1), 0)
    near = lax.broadcasted_iota(jnp.int32, (n.rows, n.nb), 1) == sub_rows // BLOCK
    code_col = jnp.sum(jnp.where(near, owners, 0).astype(F32), axis=1, keepdims=True)
    code_col = code_col.astype(jnp.int32) * 16 + sub_rows % BLOCK
    order = lax.broadcasted_iota(jnp.int32, (n.rows, lanes), 1)
    for jj in range(4):
        unsort[n.rows * jj : n.rows * (jj + 1)] = one_hot(order == code_col + 4 * jj)
    swap_cot.wait_recv()
    cot_turned[:, n.rows :] = mate_cot[...].T

    if far > 1:
        gather_pass(0)

    await_bytes(label_in, n.nd - 1, l_recv.at[0])
    lane128 = lax.broadcasted_iota(jnp.int32, (1, 128), 1)
    chunks = []
    for q in range(n.nb // 8):
        row = jnp.zeros((1, 128), F32)
        for s in range(8):
            row = row + jnp.where(lane128 // 16 == s, label_in[8 * q + s], 0.0)
        chunks.append(row)
    slot_row = jnp.concatenate(chunks, axis=1).astype(jnp.int32)
    lane_all = lax.broadcasted_iota(jnp.int32, (1, lanes), 1)
    place_row = padded_place(slot_row * BLOCK + lane_all % 4, ends)

    def lay_label(src, carry):
        labels[pl.ds(pl.multiple_of(16 * src, 16), 16), :] = jnp.broadcast_to(label_in[src], (16, 128))
        return carry

    lax.fori_loop(0, n.nb, lay_label, 0)

    row_iota = lax.broadcasted_iota(jnp.int32, (n.padded, lanes), 0)

    def setter(jj, carry):
        mask = row_iota == jnp.where((lane_all // 4) % 4 == jj, place_row, -1)
        setting[pl.ds(pl.multiple_of(jj * n.padded, 16), n.padded), :] = one_hot(mask)
        return carry

    lax.fori_loop(0, 4, setter, 0)

    def taker(chunk, carry):
        at = pl.ds(pl.multiple_of(chunk * chunk_rows, chunk_rows), chunk_rows)
        slot = labels[at, :][:, :1].astype(jnp.int32)
        sub = lax.broadcasted_iota(jnp.int32, (chunk_rows, 1), 0)
        place = padded_place(slot * BLOCK + sub % 4, ends)
        cols = lax.broadcasted_iota(jnp.int32, (chunk_rows, n.padded), 1)
        for jj in range(4):
            taking[jj, at, :] = one_hot(cols == jnp.where((sub // 4) % 4 == jj, place, -1))
        return carry

    lax.fori_loop(0, lanes // chunk_rows, taker, 0)

    if far > 2:
        gather_pass(1)

    await_bytes(arrived, n.nd - 1, b_recv.at[0])
    blocks = jnp.concatenate(
        [arrived[:, 16 * g : 16 * (g + 1), :].reshape(lanes, 128) for g in range(n.groups)], axis=1
    )

    def put(jj, carry):
        owned = dot(setting[pl.ds(pl.multiple_of(jj * n.padded, 16), n.padded), :], blocks)
        for g in range(n.groups):
            xs[4 * g + jj] = owned[:, 128 * g : 128 * (g + 1)]
        return carry

    lax.fori_loop(0, 4, put, 0)

    for step in range(2, far - 1):
        gather_pass(step)

    def filter_tile(j, carry):
        taps = taps_ref[:, pl.ds(pl.multiple_of(j * 128, 128), 128)]
        for b in spans:
            base = 1 + n.span * b
            total = jnp.zeros((n.span, 128), F32)
            for s in range(8):
                window = xs[j, base + s : base + s + n.span + 24, :]
                for m in range(4):
                    k = s + 8 * m
                    if k < TAPS:
                        total = total + taps[k : k + 1] * window[8 * m : 8 * m + n.span]
            filt[j, HALO + n.span * b : HALO + n.span * (b + 1), :] = total
        return carry

    lax.fori_loop(0, n.tiles, filter_tile, 0)
    gather_pass(far - 1)

    def norm_span(b, carry):
        rows = pl.ds(pl.multiple_of(HALO + n.span * b, 16), n.span)
        total = filt[0, rows, :]
        for j in range(1, n.tiles):
            total = total + filt[j, rows, :]
        mean = jnp.sum(total, axis=1, keepdims=True) * (1.0 / n.ch)
        square = jnp.zeros((n.span, 128), F32)
        for j in range(n.tiles):
            centred = filt[j, rows, :] - mean
            square = square + centred * centred
        variance = jnp.sum(square, axis=1, keepdims=True) * (1.0 / n.ch)
        inverse = 1.0 / jnp.sqrt(variance + EPSILON)
        spread[rows, :] = jnp.broadcast_to(inverse, (n.span, 128))
        for j in range(n.tiles):
            whitened = (filt[j, rows, :] - mean) * inverse
            normed = whitened * gain_ref[128 * j : 128 * (j + 1)].reshape(1, 128) + shift_ref[128 * j : 128 * (j + 1)].reshape(1, 128)
            logistic = 1.0 / (1.0 + jnp.exp(-normed))
            activated = normed * logistic
            actp[rows, 128 * j : 128 * (j + 1)] = activated.astype(BF16)
            filt[j, rows, :] = whitened
            slope[j, rows, :] = logistic * (1.0 + normed * (1.0 - logistic))
        return carry

    lax.fori_loop(0, n.used // n.span, norm_span, 0)

    frame_col = padded_place(lax.broadcasted_iota(jnp.int32, (n.rows, 1), 0), ends)
    take = one_hot(lax.broadcasted_iota(jnp.int32, (n.rows, n.padded), 1) == frame_col)
    act_send[...] = dot(take, actp[:, theirs]).astype(BF16)
    swap_act = remote(act_send, act_both.at[pl.ds(n.rows, n.rows)], m_send.at[1], m_recv.at[1], mate, z)
    swap_act.start()
    act_both[: n.rows] = dot(take, actp[:, mine]).astype(BF16)

    await_bytes(whole.at[:, pl.ds(0, hrow)], n.nz - 1, gm_recv.at[0])
    width = 512
    per = width // 128

    def project(i, carry):
        cols = pl.ds(pl.multiple_of(i * width, width), width)
        piece = dot(cot_pad[...], whole[:, :, cols].reshape(n.ch, width))
        for q in range(per):
            hidden[per * i + q] = piece[:, 128 * q : 128 * (q + 1)]
        return carry

    lax.fori_loop(0, n.ch // width, project, 0)

    swap_act.wait_recv()

    def product(target):
        part[target] = dot(cot_turned[pl.ds(pl.multiple_of(target * n.shard, 16), n.shard), :], act_both[...])

    chunk_of = [slice(0, n.quarter), slice(n.quarter, n.half)]

    def ring_hop(way, chunk, step):
        out, into, send, recv, to = (
            (up_out, up_in, u_send, u_recv, up) if way == 0 else (down_out, down_in, d_send, d_recv, down)
        )
        at = far * chunk + step
        return remote(out.at[chunk, step], into.at[chunk, step], send.at[at], recv.at[at], dp, to)

    def ring_target(way, chunk, step):
        ahead = (far if way == chunk else far - 1) - step
        return lax.rem(z + ahead, n.nz) if way == 0 else lax.rem(z + n.nz - ahead, n.nz)

    def ring_step(step):
        for way, chunk in ways:
            if step < ring_steps(way, chunk):
                out, into = (up_out, up_in) if way == 0 else (down_out, down_in)
                value = part[ring_target(way, chunk, step), :, chunk_of[chunk]]
                if step > 0:
                    ring_hop(way, chunk, step - 1).wait_recv()
                    value = value + into[chunk, step - 1].astype(F32)
                out[chunk, step] = value.astype(BF16)
                ring_hop(way, chunk, step).start()

    product(lax.rem(z + far, n.nz))
    if far > 1:
        product(lax.rem(z + far - 1, n.nz))
        product(lax.rem(z + n.nz - far + 1, n.nz))
    ring_step(0)

    def norm_back(b, carry):
        rows = pl.ds(pl.multiple_of(HALO + n.span * b, 16), n.span)
        first = jnp.zeros((n.span, 128), F32)
        second = jnp.zeros((n.span, 128), F32)
        for j in range(n.tiles):
            whitened = filt[j, rows, :]
            grad_normed = hidden[j, rows, :] * slope[j, rows, :]
            scaled = grad_normed * gain_ref[128 * j : 128 * (j + 1)].reshape(1, 128)
            hidden[j, rows, :] = scaled
            first = first + scaled
            second = second + scaled * whitened
            half, at = j // n.ltiles, (j % n.ltiles) * KROWS
            kgrad[half, at + TAPS : at + TAPS + 1, :] += jnp.sum(grad_normed * whitened, axis=0, keepdims=True)
            kgrad[half, at + TAPS + 1 : at + TAPS + 2, :] += jnp.sum(grad_normed, axis=0, keepdims=True)
        mean1 = jnp.sum(first, axis=1, keepdims=True) * (1.0 / n.ch)
        mean2 = jnp.sum(second, axis=1, keepdims=True) * (1.0 / n.ch)
        inverse = spread[rows, :]
        for j in range(n.tiles):
            gf[j, rows, :] = inverse * (hidden[j, rows, :] - mean1 - filt[j, rows, :] * mean2)
        return carry

    lax.fori_loop(0, n.used // n.span, norm_back, 0)

    def products(i, carry):
        product(lax.rem(z + n.nz - far + 2 + i, n.nz))
        return carry

    if far > 1:
        lax.fori_loop(0, n.nz - 3, products, 0)
    else:
        product(z)

    def back_tile(j, carry):
        taps = taps_ref[:, pl.ds(pl.multiple_of(j * 128, 128), 128)]
        for b in spans:
            base = 1 + n.span * b
            here = slice(HALO + n.span * b, HALO + n.span * (b + 1))
            signal = xs[j, here, :]
            total = jnp.zeros((n.span, 128), F32)
            for s in range(8):
                window = gf[j, base + s : base + s + n.span + 24, :]
                for m in range(4):
                    k = TAPS - 1 - s - 8 * m
                    if k >= 0:
                        shifted = window[8 * m : 8 * m + n.span]
                        total = total + taps[k : k + 1] * shifted
                        product = jnp.sum((shifted * signal).reshape(n.span // 8, 8, 128), axis=0)
                        if b == 0:
                            k8[k] = product
                        else:
                            k8[k] += product
            go[j, here, :] = total.astype(BF16)
        at = pl.multiple_of(lax.rem(j, n.ltiles) * KROWS, 8)
        kgrad[j // n.ltiles, pl.ds(at, TAPS), :] = jnp.sum(k8[...], axis=1)
        return carry

    def home_to(peer, group):
        rows = pl.ds(16 * group, 16)
        return remote(
            back.at[peer, rows], home.at[dp, rows], h_send.at[group], h_recv.at[group], peer, z
        )

    def k_rows(at):
        return pl.ds(pl.multiple_of(at * n.krow, 8), n.krow)

    def k_scatter(at, slot):
        return remote(mate_k.at[k_rows(at)], k_in.at[slot], ka_send.at[0], ka_recv.at[0], 2 * at + core, z)

    def k_over_z(slot, to):
        return remote(k_z.at[z], k_z.at[slot], kz_send.at[0], kz_recv.at[0], dp, to)

    def k_gather(slot, to):
        return remote(k_all.at[slot], k_all.at[slot], kc_send.at[0], kc_recv.at[0], 2 * to + core, z)

    swap_k = remote(kgrad.at[other], mate_k, m_send.at[2], m_recv.at[2], mate, z)
    for group in range(n.groups):
        lax.fori_loop(4 * group, 4 * group + 4, back_tile, 0)
        if group == n.groups - 1:
            swap_k.start()
        if group + 1 < far:
            ring_step(group + 1)

        def gather_chunk(chunk, carry):
            at = pl.ds(pl.multiple_of(chunk * chunk_rows, chunk_rows), chunk_rows)
            total = dot(taking[0, at, :], go[4 * group])
            for jj in range(1, 4):
                total = total + dot(taking[jj, at, :], go[4 * group + jj])
            piece = total.astype(BF16).reshape(per_chunk, 16, 128)
            back[pl.ds(chunk * per_chunk, per_chunk), 16 * group : 16 * (group + 1), :] = piece
            return carry

        lax.fori_loop(0, lanes // chunk_rows, gather_chunk, 0)
        if group == n.groups - 1:
            swap_k.wait_recv()
            mate_k[...] += kgrad[core]
            chips(lambda at: k_scatter(at, chip).start())
        peers(lambda peer: home_to(peer, group).start())
    home[dp] = back[dp]


    for step in range(n.groups + 1, far):
        ring_step(step)

    for way, chunk in ((1, 0), (0, 1), (0, 0), (1, 1)):
        steps = ring_steps(way, chunk)
        if steps > 0:
            into = up_in if way == 0 else down_in
            ring_hop(way, chunk, steps - 1).wait_recv()
            part[z, :, chunk_of[chunk]] += into[chunk, steps - 1].astype(F32)

    def along_x(step):
        there = lax.rem(cx + step, n.nx)
        return there, (there * n.ny + cy) * 2 + core

    def along_y(step):
        there = lax.rem(cy + step, n.ny)
        return there, (cx * n.ny + there) * 2 + core

    def x_scatter(step):
        there, peer = along_x(step)
        return remote(x_out.at[there], x_in.at[cx], xr_send.at[0], xr_recv.at[0], peer, z)

    def y_scatter(step):
        there, peer = along_y(step)
        return there, remote(y_out.at[there], y_in.at[cy], yr_send.at[0], yr_recv.at[0], peer, z)

    def y_gather(step):
        there, peer = along_y(step)
        return remote(y_all.at[cy], y_all.at[cy], yg_send.at[0], yg_recv.at[0], peer, z)

    def x_gather(step):
        there, peer = along_x(step)
        return remote(x_all.at[cx], x_all.at[cx], xg_send.at[0], xg_recv.at[0], peer, z)

    for i in range(n.nx):
        x_out[i] = part[z, n.prow * i : n.prow * (i + 1), :].astype(BF16)
    for step in range(1, n.nx):
        x_scatter(step).start()

    await_bytes(k_in, n.chips - 1, ka_recv.at[0])
    k_in[chip] = mate_k[k_rows(chip), :]

    def k_sum(step, carry):
        return carry + k_in[lax.rem(chip + step, n.chips)]

    k_z[z] = lax.fori_loop(1, n.chips, k_sum, k_in[chip])
    for hop in range(1, n.nz):
        k_over_z(z, lax.rem(z + hop, n.nz)).start()

    band = part[z, pl.ds(pl.multiple_of(cx * n.prow, 16), n.prow), :]
    await_bytes(x_in, n.nx - 1, xr_recv.at[0])
    for step in range(1, n.nx):
        band = band + x_in[lax.rem(cx + step, n.nx)].astype(F32)
    for l in range(n.ltiles):
        y_own[l] = band[:, 128 * l : 128 * (l + 1)]
        y_out[l] = band[:, 128 * l : 128 * (l + 1)].astype(BF16)
    for step in range(1, n.ny):
        there, copy = y_scatter(step)

        @pl.when(there < n.ltiles)
        def _():
            copy.start()

    await_bytes(k_z, n.nz - 1, kz_recv.at[0])
    small = k_z[0]
    for i in range(1, n.nz):
        small = small + k_z[i]
    k_all[chip] = small * scale
    chips(lambda at: k_gather(chip, at).start())

    @pl.when(cy < n.ltiles)
    def _():
        await_bytes(y_in, n.ny - 1, yr_recv.at[0])
        total = y_own[cy]
        for step in range(1, n.ny):
            total = total + y_in[lax.rem(cy + step, n.ny)].astype(F32)
        y_all[cy] = (total * scale).astype(BF16)
        for step in range(1, n.ny):
            y_gather(step).start()

    def others_along_y(ref, sem):
        @pl.when(cy < n.ltiles)
        def _():
            await_bytes(ref, n.ltiles - 1, sem)

        @pl.when(cy >= n.ltiles)
        def _():
            await_bytes(ref, n.ltiles, sem)

    others_along_y(y_all, yg_recv.at[0])

    for l in range(n.ltiles):
        x_all[cx, :, 128 * l : 128 * (l + 1)] = y_all[l]
    for step in range(1, n.nx):
        x_gather(step).start()

    def unsort_group(group):
        rows = slice(16 * group, 16 * (group + 1))
        await_bytes(home.at[:, pl.ds(16 * group, 16)], n.nd - 1, h_recv.at[group])
        block = home[:, rows, :].reshape(lanes, 128)
        for jj in range(4):
            tile = 4 * group + jj
            found = dot(unsort[n.rows * jj : n.rows * (jj + 1)], block).astype(BF16)
            frames_ref[:, 128 * tile : 128 * (tile + 1)] = found

    for group in range(n.groups - 1):
        unsort_group(group)
    await_bytes(x_all, n.nx - 1, xg_recv.at[0])
    swap_weight = remote(x_all, x_mate, m_send.at[4], m_recv.at[4], mate, z)
    swap_weight.start()

    await_bytes(k_all, n.chips - 1, kc_recv.at[0])
    swap_all = remote(k_all, k_mate, m_send.at[3], m_recv.at[3], mate, z)
    swap_all.start()

    def lay_weight(source, half):
        cols = pl.ds(pl.multiple_of(half * n.half, 128), n.half)
        for i in range(n.nx):
            weight_out[n.prow * i : n.prow * (i + 1), cols] = source[i]

    def lay_small(source, half):
        rows = source[...].reshape(n.kall, 128)
        for l in range(n.ltiles):
            cols = pl.ds(pl.multiple_of(half * n.half + 128 * l, 128), 128)
            small_out[:, cols] = rows[KROWS * l : KROWS * (l + 1)]

    unsort_group(n.groups - 1)
    store = pltpu.make_async_copy(frames_ref, frames_out, io.at[3])
    store.start()
    lay_weight(x_all, core)
    lay_small(k_all, core)

    swap_all.wait_recv()
    lay_small(k_mate, other)
    swap_weight.wait_recv()
    lay_weight(x_mate, other)

    for copy in (swap_cot, swap_act, swap_k, swap_all, swap_weight):
        copy.wait_send()
    for step in range(far):
        for way, chunk in ways:
            if step < ring_steps(way, chunk):
                gather_hop(way, chunk, step, z).wait_send()
    for way in range(2):
        for chunk in range(2):
            for step in range(ring_steps(way, chunk)):
                ring_hop(way, chunk, step).wait_send()
    await_bytes(x_in, n.nx - 1, xr_send.at[0])
    await_bytes(x_all, n.nx - 1, xg_send.at[0])
    others_along_y(y_out, yr_send.at[0])

    @pl.when(cy < n.ltiles)
    def _():
        await_bytes(y_all, n.ny - 1, yg_send.at[0])

    await_bytes(whole.at[:, pl.ds(0, hrow)], n.nz - 1, gm_send.at[0])
    await_bytes(k_z, n.nz - 1, kz_send.at[0])
    await_bytes(k_in, n.chips - 1, ka_send.at[0])
    await_bytes(k_all, n.chips - 1, kc_send.at[0])
    await_bytes(label_out, n.nd - 1, l_send.at[0])
    await_bytes(outgoing, n.nd - 1, b_send.at[0])
    for group in range(n.groups):
        await_bytes(back.at[:, pl.ds(16 * group, 16)], n.nd - 1, h_send.at[group])
    store.wait()


def finish_kernel(n, frames_ref, weight_ref, small_ref, frames_out, weight_out, taps_out, gain_out, shift_out):
    frames_out[...] = frames_ref[...]
    weight_out[...] = weight_ref[...].astype(F32)
    taps_out[...] = small_ref[:TAPS]
    gain_out[...] = small_ref[TAPS : TAPS + 1].reshape(n.ch)
    shift_out[...] = small_ref[TAPS + 1 : TAPS + 2].reshape(n.ch)


def finish(n, frames, weight, small):
    vmem = pl.BlockSpec(memory_space=pltpu.VMEM)
    return pl.pallas_call(
        functools.partial(finish_kernel, n),
        out_shape=(
            jax.ShapeDtypeStruct((n.rows, n.ch), BF16),
            jax.ShapeDtypeStruct((n.shard, n.ch), F32),
            jax.ShapeDtypeStruct((TAPS, n.ch), F32),
            jax.ShapeDtypeStruct((n.ch,), F32),
            jax.ShapeDtypeStruct((n.ch,), F32),
        ),
        in_specs=[vmem] * 3,
        out_specs=(vmem,) * 5,
        compiler_params=pltpu.CompilerParams(vmem_limit_bytes=16 * 1024 * 1024),
    )(frames, weight, small)


def on_device(frames, destination, utt_lengths, cotangent, weight, kernel, norm_gain, norm_shift):
    n = Sizes(lax.axis_size("dp"), lax.axis_size("fsdp"), frames.shape[0], frames.shape[1], weight.shape[0])
    scale = 1.0 / math.sqrt(n.rows * n.nd * n.nz)
    far = n.nz // 2
    lanes = 16 * n.nb
    vmem = pl.BlockSpec(memory_space=pltpu.VMEM)
    smem = pl.BlockSpec(memory_space=pltpu.SMEM)
    hbm = pl.BlockSpec(memory_space=pl.ANY)

    def dma(count):
        return [pltpu.SemaphoreType.DMA((count,))] * 2

    def buf(*shape, dtype=F32):
        return pltpu.VMEM(shape, dtype)

    blocks = buf(n.nb, n.slab, 128, dtype=BF16)
    label = buf(n.nd, 1, 128)
    plane = buf(n.tiles, n.padded, 128)
    ring = buf(2, far, n.shard, n.quarter, dtype=BF16)
    band = buf(n.nx, n.prow, n.half, dtype=BF16)
    tile = buf(n.ny, n.prow, 128, dtype=BF16)
    small = buf(n.chips, n.krow, 128)
    grads = pl.pallas_call(
        functools.partial(module_kernel, n, scale),
        out_shape=(
            jax.ShapeDtypeStruct((n.rows, n.ch), BF16),
            jax.ShapeDtypeStruct((n.shard, n.ch), BF16),
            jax.ShapeDtypeStruct((KROWS, n.ch), F32),
        ),
        in_specs=[vmem, smem, hbm, hbm, hbm, vmem, vmem, vmem],
        out_specs=(hbm, vmem, vmem),
        scratch_shapes=[
            buf(n.rows, n.ch, dtype=BF16), buf(n.rows, n.ch, dtype=BF16),
            blocks, blocks, label, label, buf(16 * n.nb, 128), buf(n.nz, n.shard, n.ch, dtype=BF16),
            buf(4 * n.rows, lanes, dtype=BF16), buf(4 * n.padded, lanes, dtype=BF16), buf(4, lanes, n.padded, dtype=BF16),
            plane, plane, plane, plane, plane, buf(n.padded, 128), buf(n.padded, n.ch, dtype=BF16),
            buf(n.tiles, n.padded, 128, dtype=BF16), buf(TAPS, 8, 128), buf(2, n.kall, 128),
            buf(n.padded, n.ch, dtype=BF16), buf(n.ch, 2 * n.rows, dtype=BF16), buf(n.rows, n.ch, dtype=BF16),
            buf(2 * n.rows, n.half, dtype=BF16), buf(n.rows, n.half, dtype=BF16),
            buf(n.nz, n.shard, n.half), ring, ring, ring, ring, blocks, blocks,
            band, band, buf(n.ltiles, n.prow, 128), tile, tile, tile, band, band,
            buf(n.kall, 128), small, buf(n.nz, n.krow, 128), small, small,
            pltpu.SemaphoreType.DMA((4,)), *dma(1), *dma(1), *dma(n.groups),
            *dma(2 * far), *dma(2 * far), *dma(1), *dma(5),
            *dma(2 * far), *dma(2 * far),
            *dma(1), *dma(1), *dma(1), *dma(1),
            *dma(1), *dma(1), *dma(1),
        ],
        compiler_params=pltpu.CompilerParams(
            collective_id=0, has_side_effects=True, vmem_limit_bytes=VMEM_BYTES
        ),
    )(destination, utt_lengths, frames, cotangent, weight, kernel, norm_gain, norm_shift)
    return finish(n, *grads)


def solution(mesh):
    placed = (
        P(("dp", "fsdp"), None),
        P(("dp", "fsdp")),
        P(("dp", "fsdp"), None),
        P(("dp", "fsdp"), None),
        P("fsdp", None),
        P(),
        P(),
        P(),
    )
    return jax.shard_map(
        on_device,
        mesh=mesh,
        in_specs=placed,
        out_specs=(P(("dp", "fsdp"), None), P("fsdp", None), P(), P(), P()),
        check_vma=False,
    )
```
